32 devices in a mesh: groups: 2 (over x), tensor: 16 (over z, y, core).
Axes of the slice: x: 2, y: 2, z: 4, core: 2. Of those that a mesh axis runs over, the one named last changes fastest.
Arguments:
- hidden_in: bfloat16 [256, 16384], P('groups'), parts along dimension 0, may hold values from -4 to 4
- attn_gain: bfloat16 [16384], replicated, may hold values from 0.099609375 to 1.8984375
- w_query: bfloat16 [16384, 8192], P(None, 'tensor'), may hold values from -0.046875 to 0.046875
- w_keyval: bfloat16 [16384, 1024], P(None, 'tensor'), may hold values from -0.046875 to 0.046875
- cache_keys: bfloat16 [256, 1024, 512], P(('groups', 'tensor')), parts along dimension 0, may hold values from -140 to 140, as said below
- cache_values: bfloat16 [256, 1024, 512], P(('groups', 'tensor')), parts along dimension 0, may hold values from -8 to 8
- w_out: bfloat16 [8192, 16384], P('tensor'), may hold values from -0.09375 to 0.09375
- ffn_gain: bfloat16 [16384], replicated, may hold values from 0.099609375 to 1.8984375
- lengths: int32 [256], P(('groups', 'tensor')), parts along dimension 0, may hold values from 1 to 1024, as said below
- positions: int32 [256], P('groups'), parts along dimension 0, may hold values from 0 to 8191
Outputs:
- stream: bfloat16 [256, 16384], P('groups', 'tensor'), parts along dimension 0
- normed: bfloat16 [256, 16384], P('groups'), parts along dimension 0
The draws below stay inside these ranges and needn't reach their ends.
There are 2 independent parts, one for each index of `groups`. The reference program is written for one: setup_inputs(seed, part) draws one part's arguments, and reference() takes and returns one part's arrays. A program takes and returns all parts, laid end to end along the dimension named above; an argument that names none is the same for every part. Nothing has to cross between parts.
Inputs may be any that keep to these rules, and one draw needn't show every extreme that they name: `lengths`: every draw has a row whose length is exactly 1024. `cache_keys`: cached keys are already rotated to their own positions.
All inputs are finite; a program needn't handle non-finite values.
Results may differ from the reference program's by a relative error of at most 0.018.
The reference program's roundings to bfloat16 on the way count: a program that leaves them out, or rounds other values in their place, can miss the bound.
Values may be sent and summed in bfloat16 or wider, within the bound.
No kernel may reach another device: no remote copies, remote signals or barrier semaphores. Data moves between devices by JAX's collectives and lax.ppermute only.
A program may use at most 192 MiB of HBM per device.

```python
import math
import jax
import jax.numpy as jnp
from jax import lax

D = 16384
HQ = 64
KVH = 4
HD = 128
CACHE_LEN = 1024
ROWS = 128
N_TENSOR = 16


def draw_lengths(key, part):
    key = jax.random.fold_in(key, 11)
    drawn = jax.random.randint(jax.random.fold_in(key, 1), (ROWS,), 1, CACHE_LEN + 1)
    chosen = jax.random.randint(jax.random.fold_in(key, 2), (), 0, ROWS)
    return jnp.where(jnp.arange(ROWS) == chosen, CACHE_LEN, drawn).astype(jnp.int32)


def draw_cache_keys(key, part):
    key = jax.random.fold_in(key, 23)
    full_shape = (ROWS, CACHE_LEN, KVH * HD)
    entries = jnp.clip(jax.random.normal(jax.random.fold_in(key, 2), full_shape, dtype=jnp.float32), -4.0, 4.0)
    return (2.0 * entries).astype(jnp.bfloat16)


def set_ends(values, stream_key, low, high):
    place = [jax.random.randint(jax.random.fold_in(stream_key, axis), (), 0, length) for axis, length in enumerate(values.shape)]
    main_axis = values.shape.index(max(values.shape))
    neighbour = place[:main_axis] + [(place[main_axis] + 1) % values.shape[main_axis]] + place[main_axis + 1:]
    return values.at[tuple(place)].set(low).at[tuple(neighbour)].set(high)


def raised(values, rng, source, target, parts, factor):
    owner, partner = [(jnp.arange(values.shape[dim]) // (values.shape[dim] // parts)).reshape([-1 if axis == dim else 1 for axis in range(values.ndim)]) for dim in (source, target)]
    chosen = jax.random.permutation(rng, parts)[partner]
    strong = (owner == chosen) | (owner == (partner + parts // 2) % parts)
    return jnp.where(strong, factor * values, values)


def steps_of(rng, shape, shards, low, high):
    level = 1.0
    for dim, blocks in shards:
        heights = jax.random.uniform(jax.random.fold_in(jax.random.fold_in(rng, 6), dim), (blocks,), jnp.float32, low / len(shards), high / len(shards))
        level = level * jnp.repeat(jnp.exp(heights), shape[dim] // blocks).reshape((-1,) + (1,) * (len(shape) - 1 - dim))
    return level


def centred(stream_key, shape, scale, limit, pieces=(), kind=jnp.bfloat16):
    loudness = steps_of(stream_key, shape, pieces, -0.22, 0.18) if pieces else 1.0
    values = jax.random.normal(stream_key, shape, jnp.float32) * scale * loudness
    return jnp.minimum(jnp.maximum(values, -limit), limit).astype(kind)


def gaussian_with(key, dims, spread, bound, shards, heavy, held_as=jnp.bfloat16):
    values = spread * jax.random.normal(key, dims, jnp.float32)
    if shards:
        values = values * steps_of(key, dims, shards, -0.22, 0.18)
    return jnp.clip(raised(values, jax.random.fold_in(key, 3), *heavy), -bound, bound).astype(held_as)


def setup_inputs(seed: int = 0, part: int = 0) -> dict:
    keys = jax.random.split(jax.random.key(seed), 11)
    part_keys = jax.random.split(jax.random.fold_in(keys[10], part), 11)
    hidden_in = centred(part_keys[0], (ROWS, D), 0.5, 4.0)
    attn_gain = jnp.clip(1.0 + 0.18 * jax.random.normal(keys[1], (D,), jnp.float32), 0.099609375, 1.8984375).astype(jnp.bfloat16)
    w_query = centred(keys[2], (D, HQ * HD), D ** -0.5, 0.046875, ((1, 16),))
    w_keyval = centred(keys[3], (D, 2 * KVH * HD), D ** -0.5, 0.046875, ((1, 16),))
    cache_keys = draw_cache_keys(jax.random.fold_in(jax.random.fold_in(keys[10], part), 71), part)
    cache_values = centred(part_keys[5], (ROWS, CACHE_LEN, KVH * HD), 2.0, 8.0, ((0, 16),))
    w_out = gaussian_with(keys[6], (HQ * HD, D), (HQ * HD) ** -0.5, 0.09375, ((0, 16),), (0, 1, 16, 2.0))
    ffn_gain = jnp.clip(1.0 + 0.18 * jax.random.normal(keys[7], (D,), jnp.float32), 0.099609375, 1.8984375).astype(jnp.bfloat16)
    lengths = draw_lengths(jax.random.fold_in(jax.random.fold_in(keys[10], part), 71), part)
    positions = set_ends(jax.random.randint(part_keys[9], (ROWS,), 0, 8192), jax.random.fold_in(part_keys[9], 1), 0, 8191).astype(jnp.int32)
    return dict(hidden_in=hidden_in, attn_gain=attn_gain, w_query=w_query, w_keyval=w_keyval, cache_keys=cache_keys, cache_values=cache_values, w_out=w_out, ffn_gain=ffn_gain, lengths=lengths, positions=positions)


epsilon = 1e-05
rope_theta = 500000.0

def normalize(values, gain):
    floats = values.astype(jnp.float32)
    mean_square = lax.optimization_barrier(jnp.mean(floats * floats, axis=-1, keepdims=True))
    return (floats * lax.rsqrt(mean_square + epsilon) * gain.astype(jnp.float32)).astype(jnp.bfloat16)

def rotate(values, positions):
    half_width = values.shape[-1] // 2
    frequency = jnp.exp(jnp.arange(half_width, dtype=jnp.float32) * (-math.log(rope_theta) / half_width))
    angles = positions.astype(jnp.float32)[:, None] * frequency[None, :]
    cosine = jnp.cos(angles)[:, None, :]
    sine_part = jnp.sin(angles)[:, None, :]
    first_half = values[..., :half_width]
    second_half = values[..., half_width:]
    return jnp.concatenate([first_half * cosine - second_half * sine_part, second_half * cosine + first_half * sine_part], axis=-1)

def attend(queries, keyval, cache_keys, cache_values, lengths, positions):
    row_count = queries.shape[0]
    key_width = keyval.shape[1] // 2
    kv_groups = key_width // HD
    span = cache_keys.shape[1]
    grouped = queries.reshape(row_count, kv_groups, -1, HD).astype(jnp.float32)
    new_keys = rotate(keyval[:, :key_width].astype(jnp.float32).reshape(row_count, kv_groups, HD), positions).astype(jnp.bfloat16)
    new_values = keyval[:, key_width:].reshape(row_count, kv_groups, HD).astype(jnp.float32)
    old_keys = cache_keys.reshape(row_count, span, kv_groups, HD).astype(jnp.float32)
    old_values = cache_values.reshape(row_count, span, kv_groups, HD).astype(jnp.float32)
    score_scale = HD ** (-0.5)
    scores = jnp.einsum('rgqd,rlgd->rgql', grouped, old_keys) * score_scale
    valid_mask = jnp.arange(span)[None, :] < lengths[:, None]
    scores = jnp.where(valid_mask[:, None, None, :], scores, -1e+30)
    own_score = jnp.einsum('rgqd,rgd->rgq', grouped, new_keys.astype(jnp.float32)) * score_scale
    largest = jnp.maximum(lax.optimization_barrier(jnp.max(scores, axis=-1)), own_score)
    expsum = jnp.exp(scores - largest[..., None])
    own_exp = jnp.exp(own_score - largest)
    totals = lax.optimization_barrier(jnp.sum(expsum, axis=-1)) + own_exp
    weights = (expsum / totals[..., None]).astype(jnp.bfloat16)
    own_weight = (own_exp / totals).astype(jnp.bfloat16)
    mixed = jnp.einsum('rgql,rlgd->rgqd', weights.astype(jnp.float32), old_values)
    mixed = mixed + own_weight.astype(jnp.float32)[..., None] * new_values[:, :, None, :]
    return mixed.astype(jnp.bfloat16).reshape(row_count, -1)

def reference(hidden_in, attn_gain, w_query, w_keyval, cache_keys, cache_values, w_out, ffn_gain, lengths, positions):
    normed_in = normalize(hidden_in, attn_gain)
    queries = jnp.dot(normed_in, w_query, preferred_element_type=jnp.float32).reshape(ROWS, HQ, HD)
    queries = rotate(queries, positions).astype(jnp.bfloat16).reshape(ROWS, HQ * HD)
    keyval = jnp.dot(normed_in, w_keyval, preferred_element_type=jnp.float32).astype(jnp.bfloat16)
    attended = attend(queries, keyval, cache_keys, cache_values, lengths, positions)
    block_width = HQ * HD // N_TENSOR
    head_blocks = attended.reshape(ROWS, N_TENSOR, block_width).astype(jnp.float32)
    out_blocks = w_out.reshape(N_TENSOR, block_width, D).astype(jnp.float32)
    partials = jnp.einsum('rnk,nkd->nrd', head_blocks, out_blocks).astype(jnp.bfloat16)
    summed = lax.optimization_barrier(jnp.sum(partials.astype(jnp.float32), axis=0))
    stream = (hidden_in.astype(jnp.float32) + summed).astype(jnp.bfloat16)
    normed = normalize(stream, ffn_gain)
    return (stream, normed)
```

```python
import functools
import math

import jax
import jax.numpy as jnp
from jax import lax
from jax.experimental import pallas as pl
from jax.experimental.pallas import tpu as pltpu
from jax.sharding import PartitionSpec as P

HD = 128


epsilon = 1e-05
rope_theta = 500000.0


def normalize(values, gain):
    floats = values.astype(jnp.float32)
    mean_square = jnp.mean(floats * floats, axis=-1, keepdims=True)
    return (floats * lax.rsqrt(mean_square + epsilon) * gain.astype(jnp.float32)).astype(
        jnp.bfloat16
    )


def rotate(values, positions):
    half_width = values.shape[-1] // 2
    frequency = jnp.exp(
        jnp.arange(half_width, dtype=jnp.float32) * (-math.log(rope_theta) / half_width)
    )
    angles = positions.astype(jnp.float32)[:, None] * frequency[None, :]
    cosine = jnp.cos(angles)[:, None, :]
    sine_part = jnp.sin(angles)[:, None, :]
    first_half = values[..., :half_width]
    second_half = values[..., half_width:]
    return jnp.concatenate(
        [
            first_half * cosine - second_half * sine_part,
            second_half * cosine + first_half * sine_part,
        ],
        axis=-1,
    )


def attend(queries, keyval, cache_keys, cache_values, lengths, positions):
    row_count = queries.shape[0]
    key_width = keyval.shape[1] // 2
    kv_groups = key_width // HD
    span = cache_keys.shape[1]
    grouped = queries.reshape(row_count, kv_groups, -1, HD)
    new_keys = rotate(
        keyval[:, :key_width].astype(jnp.float32).reshape(row_count, kv_groups, HD), positions
    ).astype(jnp.bfloat16)
    new_values = keyval[:, key_width:].reshape(row_count, kv_groups, HD)
    old_keys = cache_keys.reshape(row_count, span, kv_groups, HD)
    old_values = cache_values.reshape(row_count, span, kv_groups, HD)
    score_scale = HD ** (-0.5)
    scores = (
        jnp.einsum("rgqd,rlgd->rgql", grouped, old_keys, preferred_element_type=jnp.float32)
        * score_scale
    )
    valid_mask = jnp.arange(span)[None, :] < lengths[:, None]
    scores = jnp.where(valid_mask[:, None, None, :], scores, -1e30)
    own_score = (
        jnp.einsum("rgqd,rgd->rgq", grouped, new_keys, preferred_element_type=jnp.float32)
        * score_scale
    )
    largest = jnp.maximum(jnp.max(scores, axis=-1), own_score)
    expsum = jnp.exp(scores - largest[..., None])
    own_exp = jnp.exp(own_score - largest)
    totals = jnp.sum(expsum, axis=-1) + own_exp
    weights = (expsum / totals[..., None]).astype(jnp.bfloat16)
    own_weight = (own_exp / totals).astype(jnp.bfloat16)
    mixed = jnp.einsum("rgql,rlgd->rgqd", weights, old_values, preferred_element_type=jnp.float32)
    mixed = (
        mixed
        + own_weight.astype(jnp.float32)[..., None] * new_values.astype(jnp.float32)[:, :, None, :]
    )
    return mixed.astype(jnp.bfloat16).reshape(row_count, -1)


def bit_orders(count):
    bits = list(range(count.bit_length() - 1))
    return (bits, bits[:1] + bits[2:] + bits[1:2])


def place(offset, order):
    spot = 0
    for bit in order:
        spot = spot * 2 + ((offset >> bit) & 1)
    return spot


def project_kernel(count, offsets, heads_ref, w_ref, first_ref, second_ref, w_buffer, arrived):
    me = lax.axis_index("tensor")
    width = w_buffer.shape[2]
    orders = bit_orders(count)
    half = len(offsets)
    copies = []
    for slot, offset in enumerate(offsets):
        column = pl.multiple_of(jnp.bitwise_xor(me, offset) * width, width)
        copies.append(
            pltpu.make_async_copy(
                w_ref.at[:, pl.ds(column, width)], w_buffer.at[slot], arrived.at[slot]
            )
        )
        copies[-1].start()
    heads = heads_ref[...]
    for slot, offset in enumerate(offsets):
        copies[slot].wait()
        product = jnp.dot(heads, w_buffer[slot], preferred_element_type=jnp.float32).astype(
            jnp.bfloat16
        )
        first_ref[place(offset, orders[0]) % half] = product[:, : width // 2]
        second_ref[place(offset, orders[1]) % half] = product[:, width // 2 :]


def project(heads, w_out, count, offsets):
    rows, depth = heads.shape
    width = w_out.shape[1] // count
    share = jax.ShapeDtypeStruct((len(offsets), rows, width // 2), jnp.bfloat16)
    return pl.pallas_call(
        functools.partial(project_kernel, count, offsets),
        out_shape=(share, share),
        in_specs=[pl.BlockSpec(memory_space=pltpu.VMEM), pl.BlockSpec(memory_space=pl.ANY)],
        out_specs=(pl.BlockSpec(memory_space=pltpu.VMEM),) * 2,
        scratch_shapes=[
            pltpu.VMEM((len(offsets), depth, width), jnp.bfloat16),
            pltpu.SemaphoreType.DMA((len(offsets),)),
        ],
        compiler_params=pltpu.CompilerParams(vmem_limit_bytes=30 * 1024 * 1024),
        cost_estimate=pl.CostEstimate(
            flops=2 * rows * depth * width * len(offsets),
            bytes_accessed=2 * (depth + rows) * width * len(offsets),
            transcendentals=0,
        ),
    )(heads, w_out)


def swap(values, bit, count):
    return lax.ppermute(values, "tensor", [(i, i ^ (1 << bit)) for i in range(count)])


def add(one, other):
    return (one.astype(jnp.float32) + other.astype(jnp.float32)).astype(jnp.bfloat16)


def on_device(
    hidden_in,
    attn_gain,
    w_query,
    w_keyval,
    cache_keys,
    cache_values,
    w_out,
    ffn_gain,
    lengths,
    positions,
):
    row_count = hidden_in.shape[0]
    count = lax.axis_size("tensor")
    my_index = lax.axis_index("tensor")
    normed_in = normalize(hidden_in, attn_gain)
    queries = jnp.dot(normed_in, w_query, preferred_element_type=jnp.float32)
    queries = queries.reshape(row_count, queries.shape[1] // HD, HD)
    queries = rotate(queries, positions).astype(jnp.bfloat16).reshape(row_count, -1)
    keyval = jnp.dot(normed_in, w_keyval, preferred_element_type=jnp.float32).astype(jnp.bfloat16)
    query_width = queries.shape[1]
    rows_here = row_count // count
    both = lax.all_to_all(
        jnp.concatenate([queries, keyval], axis=1).reshape(count, rows_here, -1),
        "tensor",
        split_axis=0,
        concat_axis=0,
        tiled=True,
    )
    both = jnp.swapaxes(both, 0, 1)
    row_queries = both[..., :query_width].reshape(rows_here, -1)
    row_keyval = both[..., query_width:].reshape(rows_here, -1)
    own_positions = lax.dynamic_slice_in_dim(positions, my_index * rows_here, rows_here)
    attended = attend(row_queries, row_keyval, cache_keys, cache_values, lengths, own_positions)
    head_rows = lax.all_to_all(attended, "tensor", split_axis=1, concat_axis=0, tiled=True)

    orders = bit_orders(count)
    sent = project(head_rows, w_out, count, list(range(1, count, 2)))
    received = [swap(block, orders[k][0], count) for k, block in enumerate(sent)]
    kept = project(head_rows, w_out, count, list(range(0, count, 2)))
    sums = []
    for k, order in enumerate(orders):
        keep, arrival = kept[k], received[k]
        for bit in order[1:]:
            half = keep.shape[0] // 2
            leave = add(keep[half:], arrival[half:])
            stay = add(keep[:half], arrival[:half])
            keep, arrival = stay, swap(leave, bit, count)
        sums.append(keep[0].astype(jnp.float32) + arrival[0].astype(jnp.float32))
    summed = jnp.concatenate(sums, axis=1)
    share_width = w_out.shape[1] // count
    mine = lax.dynamic_slice_in_dim(hidden_in, my_index * share_width, share_width, 1)
    stream = (mine.astype(jnp.float32) + summed).astype(jnp.bfloat16)
    full_stream = lax.all_gather(stream, "tensor", axis=1, tiled=True)
    normed = normalize(full_stream, ffn_gain)
    return (stream, normed)


def solution(mesh):
    placed = (
        P("groups", None),
        P(),
        P(None, "tensor"),
        P(None, "tensor"),
        P(("groups", "tensor"), None, None),
        P(("groups", "tensor"), None, None),
        P("tensor", None),
        P(),
        P(("groups", "tensor")),
        P("groups"),
    )
    return jax.shard_map(
        on_device,
        mesh=mesh,
        in_specs=placed,
        out_specs=(P("groups", "tensor"), P("groups", None)),
        check_vma=False,
    )
```

```python
import functools
import math

import jax
import jax.numpy as jnp
from jax import lax
from jax.experimental import pallas as pl
from jax.experimental.pallas import tpu as pltpu
from jax.sharding import PartitionSpec as P

HD = 128


epsilon = 1e-05
rope_theta = 500000.0


def normalize(values, gain):
    floats = values.astype(jnp.float32)
    mean_square = jnp.mean(floats * floats, axis=-1, keepdims=True)
    return (floats * lax.rsqrt(mean_square + epsilon) * gain.astype(jnp.float32)).astype(
        jnp.bfloat16
    )


def rotate(values, positions):
    half_width = values.shape[-1] // 2
    frequency = jnp.exp(
        jnp.arange(half_width, dtype=jnp.float32) * (-math.log(rope_theta) / half_width)
    )
    angles = positions.astype(jnp.float32)[:, None] * frequency[None, :]
    cosine = jnp.cos(angles)[:, None, :]
    sine_part = jnp.sin(angles)[:, None, :]
    first_half = values[..., :half_width]
    second_half = values[..., half_width:]
    return jnp.concatenate(
        [
            first_half * cosine - second_half * sine_part,
            second_half * cosine + first_half * sine_part,
        ],
        axis=-1,
    )


def attend(queries, keyval, cache_keys, cache_values, lengths, positions):
    row_count = queries.shape[0]
    key_width = keyval.shape[1] // 2
    kv_groups = key_width // HD
    span = cache_keys.shape[1]
    grouped = queries.reshape(row_count, kv_groups, -1, HD)
    new_keys = rotate(
        keyval[:, :key_width].astype(jnp.float32).reshape(row_count, kv_groups, HD), positions
    ).astype(jnp.bfloat16)
    new_values = keyval[:, key_width:].reshape(row_count, kv_groups, HD)
    old_keys = cache_keys.reshape(row_count, span, kv_groups, HD)
    old_values = cache_values.reshape(row_count, span, kv_groups, HD)
    score_scale = HD ** (-0.5)
    scores = (
        jnp.einsum("rgqd,rlgd->rgql", grouped, old_keys, preferred_element_type=jnp.float32)
        * score_scale
    )
    valid_mask = jnp.arange(span)[None, :] < lengths[:, None]
    scores = jnp.where(valid_mask[:, None, None, :], scores, -1e30)
    own_score = (
        jnp.einsum("rgqd,rgd->rgq", grouped, new_keys, preferred_element_type=jnp.float32)
        * score_scale
    )
    largest = jnp.maximum(jnp.max(scores, axis=-1), own_score)
    expsum = jnp.exp(scores - largest[..., None])
    own_exp = jnp.exp(own_score - largest)
    totals = jnp.sum(expsum, axis=-1) + own_exp
    weights = (expsum / totals[..., None]).astype(jnp.bfloat16)
    own_weight = (own_exp / totals).astype(jnp.bfloat16)
    mixed = jnp.einsum("rgql,rlgd->rgqd", weights, old_values, preferred_element_type=jnp.float32)
    mixed = (
        mixed
        + own_weight.astype(jnp.float32)[..., None] * new_values.astype(jnp.float32)[:, :, None, :]
    )
    return mixed.astype(jnp.bfloat16).reshape(row_count, -1)


def plans(count):
    bits = list(range(1, count.bit_length() - 1))
    turned = bits[::-1]
    crossed = turned[:-2] + turned[:-3:-1]
    return [
        (bits, turned),
        (bits, crossed),
        (bits, crossed),
        (bits[1:] + bits[:1], turned),
    ]


def timetable(count):
    if count == 16:
        return [int(c) for c in "03013120032130121302120321013232"]
    return [s for _ in range(2 * (count.bit_length() - 2) + 2) for s in (0, 3, 1, 2)]


def place(offset, order):
    spot = 0
    for bit in order:
        spot = spot * 2 + ((offset >> bit) & 1)
    return spot


def project_kernel(count, offsets, heads_ref, w_ref, *refs):
    *set_refs, w_buffer, arrived = refs
    me = lax.axis_index("tensor")
    width = w_buffer.shape[2]
    copies = []
    for slot, offset in enumerate(offsets):
        column = pl.multiple_of(jnp.bitwise_xor(me, offset) * width, width)
        copies.append(
            pltpu.make_async_copy(
                w_ref.at[:, pl.ds(column, width)], w_buffer.at[slot], arrived.at[slot]
            )
        )
        copies[-1].start()
    heads = heads_ref[...]
    for slot, offset in enumerate(offsets):
        copies[slot].wait()
        product = jnp.dot(heads, w_buffer[slot], preferred_element_type=jnp.float32).astype(
            jnp.bfloat16
        )
        start = 0
        for ref, (order, _) in zip(set_refs, plans(count)):
            ref[place(offset, order)] = product[start : start + ref.shape[1]]
            start += ref.shape[1]


def project(heads, w_out, count, offsets):
    rows, depth = heads.shape
    width = w_out.shape[1] // count
    sets = len(plans(count))
    share = jax.ShapeDtypeStruct((len(offsets), rows // sets, width), jnp.bfloat16)
    return pl.pallas_call(
        functools.partial(project_kernel, count, offsets),
        out_shape=(share,) * sets,
        in_specs=[pl.BlockSpec(memory_space=pltpu.VMEM), pl.BlockSpec(memory_space=pl.ANY)],
        out_specs=(pl.BlockSpec(memory_space=pltpu.VMEM),) * sets,
        scratch_shapes=[
            pltpu.VMEM((len(offsets), depth, width), jnp.bfloat16),
            pltpu.SemaphoreType.DMA((len(offsets),)),
        ],
        compiler_params=pltpu.CompilerParams(vmem_limit_bytes=50 * 1024 * 1024),
        cost_estimate=pl.CostEstimate(
            flops=2 * rows * depth * width * len(offsets),
            bytes_accessed=2 * (depth + rows) * width * len(offsets),
            transcendentals=0,
        ),
    )(heads, w_out)


def finish_kernel(offsets, own_ref, other_ref, gain_ref, *refs):
    out_ref = refs[-1]
    me = lax.axis_index("tensor")
    half, rows, width = own_ref.shape
    total = jnp.zeros((rows, width), jnp.float32)
    for ref in (own_ref, other_ref):
        for k in range(half):
            block = ref[k].astype(jnp.float32)
            total = total + block * block
    mean_square = jnp.sum(total, axis=1, keepdims=True) / (2 * half * width)
    scale = lax.rsqrt(mean_square + epsilon)
    for k, offset in enumerate(offsets):
        block = (own_ref if k < half else other_ref)[k % half].astype(jnp.float32)
        index = jnp.bitwise_xor(me, offset)
        column = pl.multiple_of(index * width, width)
        gain = gain_ref[pl.ds(index, 1), :]
        out_ref[:, pl.ds(column, width)] = (block * scale * gain).astype(jnp.bfloat16)


def finish(own, other, gain, offsets, which, sets, earlier):
    half, rows, width = own.shape
    columns = 2 * half * width
    operands = [own, other, gain] + ([] if earlier is None else [earlier])
    whole = pl.BlockSpec(memory_space=pltpu.VMEM)
    return pl.pallas_call(
        functools.partial(finish_kernel, offsets),
        grid=(1,),
        out_shape=jax.ShapeDtypeStruct((rows * sets, columns), jnp.bfloat16),
        in_specs=[whole] * 3 + [pl.BlockSpec(memory_space=pl.ANY)] * (len(operands) - 3),
        out_specs=pl.BlockSpec((rows, columns), lambda i: (which, 0)),
        input_output_aliases={} if earlier is None else {3: 0},
        compiler_params=pltpu.CompilerParams(vmem_limit_bytes=24 * 1024 * 1024),
        cost_estimate=pl.CostEstimate(
            flops=6 * rows * columns, bytes_accessed=4 * rows * columns, transcendentals=0
        ),
    )(*operands)


def swap(values, bit, count):
    return lax.ppermute(values, "tensor", [(i, i ^ (1 << bit)) for i in range(count)])


def add(one, other):
    return (one.astype(jnp.float32) + other.astype(jnp.float32)).astype(jnp.bfloat16)


def on_device(
    hidden_in,
    attn_gain,
    w_query,
    w_keyval,
    cache_keys,
    cache_values,
    w_out,
    ffn_gain,
    lengths,
    positions,
):
    row_count = hidden_in.shape[0]
    count = lax.axis_size("tensor")
    my_index = lax.axis_index("tensor")
    normed_in = normalize(hidden_in, attn_gain)
    queries = jnp.dot(normed_in, w_query, preferred_element_type=jnp.float32)
    queries = queries.reshape(row_count, queries.shape[1] // HD, HD)
    queries = rotate(queries, positions).astype(jnp.bfloat16).reshape(row_count, -1)
    keyval = jnp.dot(normed_in, w_keyval, preferred_element_type=jnp.float32).astype(jnp.bfloat16)
    query_width = queries.shape[1]
    rows_here = row_count // count
    both = lax.all_to_all(
        jnp.concatenate([queries, keyval], axis=1).reshape(count, rows_here, -1),
        "tensor",
        split_axis=0,
        concat_axis=0,
        tiled=True,
    )
    both = jnp.swapaxes(both, 0, 1)
    row_queries = both[..., :query_width].reshape(rows_here, -1)
    row_keyval = both[..., query_width:].reshape(rows_here, -1)
    own_positions = lax.dynamic_slice_in_dim(positions, my_index * rows_here, rows_here)
    attended = attend(row_queries, row_keyval, cache_keys, cache_values, lengths, own_positions)
    head_rows = lax.all_to_all(attended, "tensor", split_axis=1, concat_axis=0, tiled=True)

    share_width = w_out.shape[1] // count
    mine = lax.dynamic_slice_in_dim(hidden_in, my_index * share_width, share_width, 1)
    gain = ffn_gain.astype(jnp.float32).reshape(count, share_width)
    orders = plans(count)
    sets = len(orders)
    set_rows = row_count // sets
    sent = project(head_rows, w_out, count, list(range(1, count, 2)))
    arrivals = [swap(block, 0, count) for block in sent]
    held = list(project(head_rows, w_out, count, list(range(0, count, 2))))

    streams = [None] * sets
    offsets = [[0] for _ in range(sets)]
    steps = [0] * sets
    last = None
    normed = None
    for k in timetable(count):
        scatter, gather = orders[k]
        step = steps[k]
        steps[k] += 1
        if last is not None:
            held[k], arrivals[k], _ = lax.optimization_barrier((held[k], arrivals[k], last))
        if step < len(scatter):
            half = held[k].shape[0] // 2
            last = add(held[k][half:], arrivals[k][half:])
            held[k] = add(held[k][:half], arrivals[k][:half])
            arrivals[k] = swap(last, scatter[step], count)
            continue
        if step == len(scatter):
            own_rows = mine[k * set_rows : (k + 1) * set_rows].astype(jnp.float32)
            total = held[k][0].astype(jnp.float32) + arrivals[k][0].astype(jnp.float32)
            streams[k] = (own_rows + total).astype(jnp.bfloat16)
            last = held[k] = streams[k][None]
        elif step <= len(scatter) + len(gather):
            last = held[k] = jnp.concatenate([held[k], arrivals[k]], axis=0)
        else:
            last = normed = finish(held[k], arrivals[k], gain, offsets[k], k, sets, normed)
            continue
        bit = (gather + [0])[step - len(scatter)]
        arrivals[k] = swap(held[k], bit, count)
        offsets[k] = offsets[k] + [offset ^ (1 << bit) for offset in offsets[k]]
    return (jnp.concatenate(streams, axis=0), normed)


def solution(mesh):
    placed = (
        P("groups", None),
        P(),
        P(None, "tensor"),
        P(None, "tensor"),
        P(("groups", "tensor"), None, None),
        P(("groups", "tensor"), None, None),
        P("tensor", None),
        P(),
        P(("groups", "tensor")),
        P("groups"),
    )
    return jax.shard_map(
        on_device,
        mesh=mesh,
        in_specs=placed,
        out_specs=(P("groups", "tensor"), P("groups", None)),
        check_vma=False,
    )
```

```python
import functools
import math

import jax
import jax.numpy as jnp
from jax import lax
from jax.experimental import pallas as pl
from jax.experimental.pallas import tpu as pltpu
from jax.sharding import PartitionSpec as P

HD = 128


epsilon = 1e-05
rope_theta = 500000.0


def turns(positions):
    half = HD // 2
    entry = jnp.arange(HD, dtype=jnp.int32)
    frequency = jnp.exp((entry % half).astype(jnp.float32) * (-math.log(rope_theta) / half))
    angles = positions.astype(jnp.float32)[:, None] * frequency[None, :]
    sign = jnp.where(entry < half, -1.0, 1.0)
    return jnp.cos(angles), jnp.sin(angles) * sign


def rotate(head, cosine, sine):
    return head * cosine + pltpu.roll(head, HD // 2, 1) * sine


def input_kernel(count, hidden_ref, gain_ref, w_ref, kv_ref, cosine_ref, sine_ref, *refs):
    *out_refs, hidden, w_buffer, kv_buffer, products, kv_products, result, h_sem, w_sem, kv_sem = refs
    me = lax.axis_index("tensor")
    rows, columns = hidden.shape
    chunks = h_sem.shape[0]
    depth = columns // chunks
    width = products.shape[1]
    kv_width = kv_products.shape[1]
    here = rows // count

    def spans(k):
        return pl.ds(pl.multiple_of(k * depth, depth), depth)

    def hidden_copy(k):
        return pltpu.make_async_copy(
            hidden_ref.at[:, spans(k)], hidden.at[:, spans(k)], h_sem.at[k]
        )

    def w_copy(k):
        return pltpu.make_async_copy(
            w_ref.at[spans(k), :], w_buffer.at[spans(k), :], w_sem.at[k]
        )

    for k in range(chunks):
        hidden_copy(k).start()
    early = chunks // 4
    for k in range(early):
        w_copy(k).start()
    kv_copy = pltpu.make_async_copy(kv_ref, kv_buffer, kv_sem)
    kv_copy.start()

    def square(k, total):
        hidden_copy(k).wait()
        for lane in range(0, depth, 128):
            part = hidden[:, pl.ds(pl.multiple_of(k * depth + lane, 128), 128)].astype(jnp.float32)
            total = total + part * part
        return total

    total = lax.fori_loop(0, chunks, square, jnp.zeros((rows, 128), jnp.float32))
    for k in range(early, chunks):
        w_copy(k).start()
    scale = lax.rsqrt(jnp.sum(total, axis=1, keepdims=True) / columns + epsilon)
    products[...] = jnp.zeros_like(products)
    kv_products[...] = jnp.zeros_like(kv_products)
    kv_copy.wait()

    def multiply(k, carry):
        floats = hidden[:, spans(k)].astype(jnp.float32)
        gain = gain_ref[:, spans(k)].astype(jnp.float32)
        normed = (floats * scale * gain).astype(jnp.bfloat16)
        w_copy(k).wait()
        products[...] += jnp.dot(
            normed, w_buffer[spans(k), :], preferred_element_type=jnp.float32
        )
        kv_products[...] += lax.dot_general(
            normed,
            kv_buffer[:, spans(k)],
            (((1,), (1,)), ((), ())),
            preferred_element_type=jnp.float32,
        )
        return carry

    lax.fori_loop(0, chunks, multiply, 0)
    for start in range(0, width, HD):
        result[:, start : start + HD] = rotate(
            products[:, start : start + HD], cosine_ref[...], sine_ref[...]
        )
    result[:, width:] = jnp.zeros((rows, HD), jnp.float32)
    result[:, width : width + kv_width] = kv_products[...]
    shift = lax.rem(me, HD // kv_width) * kv_width
    result[:, width:] = pltpu.roll(result[:, width:], shift, 1)
    for k, ref in enumerate(out_refs):
        block = pl.ds(pl.multiple_of(jnp.bitwise_xor(me, k) * here, here), here)
        ref[...] = result[block, :].astype(jnp.bfloat16)


def project_in(hidden_in, gain, w_query, w_keyval, cosine, sine, count):
    rows, columns = hidden_in.shape
    width, kv_width = w_query.shape[1], w_keyval.shape[1]
    chunks = 16
    vmem = pl.BlockSpec(memory_space=pltpu.VMEM)
    whole = pl.BlockSpec(memory_space=pl.ANY)
    share = jax.ShapeDtypeStruct((rows // count, width + HD), jnp.bfloat16)
    return pl.pallas_call(
        functools.partial(input_kernel, count),
        out_shape=(share,) * count,
        in_specs=[whole, vmem, whole, whole, vmem, vmem],
        out_specs=(vmem,) * count,
        scratch_shapes=[
            pltpu.VMEM((rows, columns), jnp.bfloat16),
            pltpu.VMEM((columns, width), jnp.bfloat16),
            pltpu.VMEM((kv_width, columns), jnp.bfloat16),
            pltpu.VMEM((rows, width), jnp.float32),
            pltpu.VMEM((rows, kv_width), jnp.float32),
            pltpu.VMEM((rows, width + HD), jnp.float32),
            pltpu.SemaphoreType.DMA((chunks,)),
            pltpu.SemaphoreType.DMA((chunks,)),
            pltpu.SemaphoreType.DMA,
        ],
        compiler_params=pltpu.CompilerParams(vmem_limit_bytes=50 * 1024 * 1024),
        cost_estimate=pl.CostEstimate(
            flops=2 * rows * columns * (width + kv_width),
            bytes_accessed=2 * columns * (rows + width + kv_width),
            transcendentals=0,
        ),
    )(hidden_in, gain, w_query, w_keyval.T, cosine, sine)


def attend_kernel(count, lengths_ref, cosine_ref, sine_ref, keys_ref, values_ref, *refs):
    in_refs, out_refs = refs[:count], refs[count : 2 * count]
    queries, attended, keys, values, k_sem, v_sem = refs[2 * count :]
    me = lax.axis_index("tensor")
    here, span, key_width = keys.shape
    kv_groups = key_width // HD
    parts = attended.shape[0]
    copies = []
    for row in range(here):
        copies.append(
            (
                pltpu.make_async_copy(keys_ref.at[row], keys.at[row], k_sem.at[row]),
                pltpu.make_async_copy(values_ref.at[row], values.at[row], v_sem.at[row]),
            )
        )
        for copy in copies[-1]:
            copy.start()

    for k, ref in enumerate(in_refs):
        block = pl.ds(pl.multiple_of(jnp.bitwise_xor(me, k) * here, here), here)
        for part in range(parts + 1):
            queries[part, block, :] = ref[:, part * HD : (part + 1) * HD].astype(jnp.float32)
    mine = pl.ds(pl.multiple_of(me * here, here), here)
    cosine, sine = cosine_ref[mine, :], sine_ref[mine, :]
    shares = count // (2 * kv_groups)
    tiles = []
    for tile in range(2 * kv_groups):
        joined = jnp.zeros((here, HD), jnp.float32)
        for device in range(tile * shares, (tile + 1) * shares):
            joined = joined + queries[parts, device * here : (device + 1) * here, :]
        tiles.append(joined)
    new_keys = [rotate(tile, cosine, sine) for tile in tiles[:kv_groups]]
    new_keys = jnp.concatenate(new_keys, axis=1).astype(jnp.bfloat16).astype(jnp.float32)
    new_values = jnp.concatenate(tiles[kv_groups:], axis=1)

    shape = (parts * count, key_width)
    group_devices = count // kv_groups
    device = lax.rem(lax.broadcasted_iota(jnp.int32, shape, 0), count)
    column = lax.broadcasted_iota(jnp.int32, shape, 1)
    own_group = lax.div(device, group_devices) == lax.div(column, HD)
    token = lax.broadcasted_iota(jnp.int32, (parts * count, span), 1)
    score_scale = HD ** (-0.5)
    for row in range(here):
        heads = jnp.concatenate(
            [
                queries[part, pl.ds(row, count, stride=here), :]
                for part in range(parts)
            ],
            axis=0,
        )
        heads = jnp.where(own_group, jnp.concatenate([heads] * kv_groups, axis=1), 0.0)
        own_score = (
            jnp.sum(heads * new_keys[row : row + 1], axis=1, keepdims=True) * score_scale
        )
        copies[row][0].wait()
        scores = (
            lax.dot_general(
                heads.astype(jnp.bfloat16),
                keys[row],
                (((1,), (1,)), ((), ())),
                preferred_element_type=jnp.float32,
            )
            * score_scale
        )
        scores = jnp.where(token < lengths_ref[row], scores, -1e30)
        largest = jnp.maximum(jnp.max(scores, axis=1, keepdims=True), own_score)
        raised = jnp.exp(scores - largest)
        own_raised = jnp.exp(own_score - largest)
        share = 1.0 / (jnp.sum(raised, axis=1, keepdims=True) + own_raised)
        weights = (raised * share).astype(jnp.bfloat16)
        own_weight = (own_raised * share).astype(jnp.bfloat16).astype(jnp.float32)
        copies[row][1].wait()
        mixed = jnp.dot(weights, values[row], preferred_element_type=jnp.float32)
        mixed = mixed + own_weight * new_values[row : row + 1]
        mixed = jnp.where(own_group, mixed, 0.0)
        chosen = mixed[:, :HD]
        for group in range(1, kv_groups):
            chosen = chosen + mixed[:, group * HD : (group + 1) * HD]
        for part in range(parts):
            attended[part, pl.ds(row, count, stride=here), :] = chosen[
                part * count : (part + 1) * count
            ]
    for k, ref in enumerate(out_refs):
        block = pl.ds(pl.multiple_of(jnp.bitwise_xor(me, k) * here, here), here)
        for part in range(parts):
            ref[:, part * HD : (part + 1) * HD] = attended[part, block, :].astype(jnp.bfloat16)


def attend(blocks, lengths, cosine, sine, cache_keys, cache_values):
    count = len(blocks)
    here, span, key_width = cache_keys.shape
    width = blocks[0].shape[1] - HD
    vmem = pl.BlockSpec(memory_space=pltpu.VMEM)
    whole = pl.BlockSpec(memory_space=pl.ANY)
    share = jax.ShapeDtypeStruct((here, width), jnp.bfloat16)
    return pl.pallas_call(
        functools.partial(attend_kernel, count),
        out_shape=(share,) * count,
        in_specs=[pl.BlockSpec(memory_space=pltpu.SMEM), vmem, vmem, whole, whole]
        + [vmem] * count,
        out_specs=(vmem,) * count,
        scratch_shapes=[
            pltpu.VMEM((width // HD + 1, here * count, HD), jnp.float32),
            pltpu.VMEM((width // HD, here * count, HD), jnp.float32),
            pltpu.VMEM((here, span, key_width), jnp.bfloat16),
            pltpu.VMEM((here, span, key_width), jnp.bfloat16),
            pltpu.SemaphoreType.DMA((here,)),
            pltpu.SemaphoreType.DMA((here,)),
        ],
        compiler_params=pltpu.CompilerParams(vmem_limit_bytes=50 * 1024 * 1024),
        cost_estimate=pl.CostEstimate(
            flops=4 * here * count * width * span,
            bytes_accessed=4 * here * span * key_width,
            transcendentals=here * count * width // HD * span,
        ),
    )(lengths, cosine, sine, cache_keys, cache_values, *blocks)


def exchange(blocks):
    count = len(blocks)
    return [blocks[0]] + [
        lax.ppermute(blocks[k], "tensor", [(i, i ^ k) for i in range(count)])
        for k in range(1, count)
    ]


def plans(count):
    bits = list(range(1, count.bit_length() - 1))
    turned = bits[::-1]
    crossed = turned[:-2] + turned[:-3:-1]
    return [
        (bits, turned),
        (bits, crossed),
        (bits, crossed),
        (bits[1:] + bits[:1], turned),
    ]


def timetable(count):
    if count == 16:
        return [int(c) for c in "03013120032130121302120321013232"]
    return [s for _ in range(2 * (count.bit_length() - 2) + 2) for s in (0, 3, 1, 2)]


def place(offset, order):
    spot = 0
    for bit in order:
        spot = spot * 2 + ((offset >> bit) & 1)
    return spot


def project_kernel(count, offsets, w_ref, *refs):
    in_refs = refs[:count]
    *set_refs, heads_buffer, w_buffer, arrived = refs[count:]
    me = lax.axis_index("tensor")
    width = w_buffer.shape[2]
    copies = []
    for slot, offset in enumerate(offsets):
        column = pl.multiple_of(jnp.bitwise_xor(me, offset) * width, width)
        copies.append(
            pltpu.make_async_copy(
                w_ref.at[:, pl.ds(column, width)], w_buffer.at[slot], arrived.at[slot]
            )
        )
        copies[-1].start()
    here = in_refs[0].shape[0]
    for k, ref in enumerate(in_refs):
        block = pl.ds(pl.multiple_of(jnp.bitwise_xor(me, k) * here, here), here)
        heads_buffer[block, :] = ref[...].astype(jnp.float32)
    heads = heads_buffer[...].astype(jnp.bfloat16)
    for slot, offset in enumerate(offsets):
        copies[slot].wait()
        product = jnp.dot(heads, w_buffer[slot], preferred_element_type=jnp.float32).astype(
            jnp.bfloat16
        )
        start = 0
        for ref, (order, _) in zip(set_refs, plans(count)):
            ref[place(offset, order)] = product[start : start + ref.shape[1]]
            start += ref.shape[1]


def project(blocks, w_out, offsets):
    count = len(blocks)
    rows, depth = blocks[0].shape[0] * count, blocks[0].shape[1]
    width = w_out.shape[1] // count
    sets = len(plans(count))
    share = jax.ShapeDtypeStruct((len(offsets), rows // sets, width), jnp.bfloat16)
    return pl.pallas_call(
        functools.partial(project_kernel, count, offsets),
        out_shape=(share,) * sets,
        in_specs=[pl.BlockSpec(memory_space=pl.ANY)]
        + [pl.BlockSpec(memory_space=pltpu.VMEM)] * count,
        out_specs=(pl.BlockSpec(memory_space=pltpu.VMEM),) * sets,
        scratch_shapes=[
            pltpu.VMEM((rows, depth), jnp.float32),
            pltpu.VMEM((len(offsets), depth, width), jnp.bfloat16),
            pltpu.SemaphoreType.DMA((len(offsets),)),
        ],
        compiler_params=pltpu.CompilerParams(vmem_limit_bytes=50 * 1024 * 1024),
        cost_estimate=pl.CostEstimate(
            flops=2 * rows * depth * width * len(offsets),
            bytes_accessed=2 * (depth + rows) * width * len(offsets),
            transcendentals=0,
        ),
    )(w_out, *blocks)


def finish_kernel(offsets, own_ref, other_ref, gain_ref, *refs):
    out_ref = refs[-1]
    me = lax.axis_index("tensor")
    half, rows, width = own_ref.shape
    total = jnp.zeros((rows, width), jnp.float32)
    for ref in (own_ref, other_ref):
        for k in range(half):
            block = ref[k].astype(jnp.float32)
            total = total + block * block
    mean_square = jnp.sum(total, axis=1, keepdims=True) / (2 * half * width)
    scale = lax.rsqrt(mean_square + epsilon)
    for k, offset in enumerate(offsets):
        block = (own_ref if k < half else other_ref)[k % half].astype(jnp.float32)
        index = jnp.bitwise_xor(me, offset)
        column = pl.multiple_of(index * width, width)
        gain = gain_ref[pl.ds(index, 1), :]
        out_ref[:, pl.ds(column, width)] = (block * scale * gain).astype(jnp.bfloat16)


def finish(own, other, gain, offsets, which, sets, earlier):
    half, rows, width = own.shape
    columns = 2 * half * width
    operands = [own, other, gain] + ([] if earlier is None else [earlier])
    whole = pl.BlockSpec(memory_space=pltpu.VMEM)
    return pl.pallas_call(
        functools.partial(finish_kernel, offsets),
        grid=(1,),
        out_shape=jax.ShapeDtypeStruct((rows * sets, columns), jnp.bfloat16),
        in_specs=[whole] * 3 + [pl.BlockSpec(memory_space=pl.ANY)] * (len(operands) - 3),
        out_specs=pl.BlockSpec((rows, columns), lambda i: (which, 0)),
        input_output_aliases={} if earlier is None else {3: 0},
        compiler_params=pltpu.CompilerParams(vmem_limit_bytes=24 * 1024 * 1024),
        cost_estimate=pl.CostEstimate(
            flops=6 * rows * columns, bytes_accessed=4 * rows * columns, transcendentals=0
        ),
    )(*operands)


def swap(values, bit, count):
    return lax.ppermute(values, "tensor", [(i, i ^ (1 << bit)) for i in range(count)])


def add(one, other):
    return (one.astype(jnp.float32) + other.astype(jnp.float32)).astype(jnp.bfloat16)


def on_device(
    hidden_in,
    attn_gain,
    w_query,
    w_keyval,
    cache_keys,
    cache_values,
    w_out,
    ffn_gain,
    lengths,
    positions,
):
    row_count = hidden_in.shape[0]
    count = lax.axis_size("tensor")
    my_index = lax.axis_index("tensor")
    cosine, sine = turns(positions)
    blocks = project_in(
        hidden_in, attn_gain.reshape(1, -1), w_query, w_keyval, cosine, sine, count
    )
    head_blocks = exchange(
        attend(exchange(blocks), lengths, cosine, sine, cache_keys, cache_values)
    )
    share_width = w_out.shape[1] // count
    mine = lax.dynamic_slice_in_dim(hidden_in, my_index * share_width, share_width, 1)
    gain = ffn_gain.astype(jnp.float32).reshape(count, share_width)
    orders = plans(count)
    sets = len(orders)
    set_rows = row_count // sets
    sent = project(head_blocks, w_out, list(range(1, count, 2)))
    arrivals = [swap(block, 0, count) for block in sent]
    held = list(project(head_blocks, w_out, list(range(0, count, 2))))

    streams = [None] * sets
    offsets = [[0] for _ in range(sets)]
    steps = [0] * sets
    last = None
    normed = None
    for k in timetable(count):
        scatter, gather = orders[k]
        step = steps[k]
        steps[k] += 1
        if last is not None:
            held[k], arrivals[k], _ = lax.optimization_barrier((held[k], arrivals[k], last))
        if step < len(scatter):
            half = held[k].shape[0] // 2
            last = add(held[k][half:], arrivals[k][half:])
            held[k] = add(held[k][:half], arrivals[k][:half])
            arrivals[k] = swap(last, scatter[step], count)
            continue
        if step == len(scatter):
            own_rows = mine[k * set_rows : (k + 1) * set_rows].astype(jnp.float32)
            total = held[k][0].astype(jnp.float32) + arrivals[k][0].astype(jnp.float32)
            streams[k] = (own_rows + total).astype(jnp.bfloat16)
            last = held[k] = streams[k][None]
        elif step <= len(scatter) + len(gather):
            last = held[k] = jnp.concatenate([held[k], arrivals[k]], axis=0)
        else:
            last = normed = finish(held[k], arrivals[k], gain, offsets[k], k, sets, normed)
            continue
        bit = (gather + [0])[step - len(scatter)]
        arrivals[k] = swap(held[k], bit, count)
        offsets[k] = offsets[k] + [offset ^ (1 << bit) for offset in offsets[k]]
    return (jnp.concatenate(streams, axis=0), normed)


def solution(mesh):
    placed = (
        P("groups", None),
        P(),
        P(None, "tensor"),
        P(None, "tensor"),
        P(("groups", "tensor"), None, None),
        P(("groups", "tensor"), None, None),
        P("tensor", None),
        P(),
        P(("groups", "tensor")),
        P("groups"),
    )
    return jax.shard_map(
        on_device,
        mesh=mesh,
        in_specs=placed,
        out_specs=(P("groups", "tensor"), P("groups", None)),
        check_vma=False,
    )
```

```python
import functools
import math

import jax
import jax.numpy as jnp
from jax import lax
from jax.experimental import pallas as pl
from jax.experimental.pallas import tpu as pltpu
from jax.sharding import PartitionSpec as P

HD = 128


TABLE = "20210320213032013021313012023131"

epsilon = 1e-05
rope_theta = 500000.0


def turns(positions):
    half = HD // 2
    entry = jnp.arange(HD, dtype=jnp.int32)
    frequency = jnp.exp((entry % half).astype(jnp.float32) * (-math.log(rope_theta) / half))
    angles = positions.astype(jnp.float32)[:, None] * frequency[None, :]
    sign = jnp.where(entry < half, -1.0, 1.0)
    return jnp.cos(angles), jnp.sin(angles) * sign


def rotate(head, cosine, sine):
    return head * cosine + pltpu.roll(head, HD // 2, 1) * sine


def input_kernel(count, hidden_ref, gain_ref, w_ref, kv_ref, cosine_ref, sine_ref, *refs):
    out_ref, hidden, w_buffer, kv_buffer, normed, products, kv_products, *sems = refs
    h_sem, w_sem, kv_sem = sems
    me = lax.axis_index("tensor")
    rows, columns = hidden.shape
    depth = normed.shape[2]
    chunks = columns // depth
    width = products.shape[1]
    kv_width = kv_products.shape[1]
    here = rows // count

    def span(k):
        return pl.ds(k * depth, depth)

    def hidden_copy(k):
        return pltpu.make_async_copy(
            hidden_ref.at[:, span(k)], hidden.at[:, span(k)], h_sem.at[k]
        )

    def w_copy(k):
        return pltpu.make_async_copy(w_ref.at[span(k), :], w_buffer.at[span(k), :], w_sem.at[k])

    for k in range(chunks):
        hidden_copy(k).start()
    early = chunks // 4
    for k in range(early):
        w_copy(k).start()
    kv_copy = pltpu.make_async_copy(kv_ref, kv_buffer, kv_sem)
    kv_copy.start()
    products[...] = jnp.zeros_like(products)
    kv_products[...] = jnp.zeros_like(kv_products)
    total = jnp.zeros((rows, 128), jnp.float32)
    for k in range(chunks):
        hidden_copy(k).wait()
        for lane in range(k * depth, (k + 1) * depth, 128):
            part = hidden[:, lane : lane + 128].astype(jnp.float32)
            total = total + part * part
    for k in range(early, chunks):
        w_copy(k).start()
    scale = lax.rsqrt(jnp.sum(total, axis=1, keepdims=True) / columns + epsilon)

    def norm(k):
        floats = hidden[:, span(k)].astype(jnp.float32)
        gain = gain_ref[:, span(k)].astype(jnp.float32)
        normed[k % 2] = (floats * scale * gain).astype(jnp.bfloat16)

    norm(0)
    kv_copy.wait()
    for k in range(chunks):
        w_copy(k).wait()
        products[...] += jnp.dot(
            normed[k % 2], w_buffer[span(k), :], preferred_element_type=jnp.float32
        )
        kv_products[...] += lax.dot_general(
            normed[k % 2],
            kv_buffer[:, span(k)],
            (((1,), (1,)), ((), ())),
            preferred_element_type=jnp.float32,
        )
        if k + 1 < chunks:
            norm(k + 1)

    shift = lax.rem(me, HD // kv_width) * kv_width
    blank = jnp.zeros((rows, HD - kv_width), jnp.float32)
    moved = pltpu.roll(jnp.concatenate([kv_products[...], blank], axis=1), shift, 1)
    results = [
        rotate(products[:, start : start + HD], cosine_ref[...], sine_ref[...])
        for start in range(0, width, HD)
    ] + [moved]
    for part, result in enumerate(results):
        for k in range(count):
            out_ref[k, :, part * HD : (part + 1) * HD] = result[
                k * here : (k + 1) * here
            ].astype(jnp.bfloat16)


def project_in(hidden_in, gain, w_query, w_keyval, cosine, sine, count):
    rows, columns = hidden_in.shape
    width, kv_width = w_query.shape[1], w_keyval.shape[1]
    depth = columns // 8
    chunks = columns // depth
    vmem = pl.BlockSpec(memory_space=pltpu.VMEM)
    whole = pl.BlockSpec(memory_space=pltpu.HBM)
    return pl.pallas_call(
        functools.partial(input_kernel, count),
        out_shape=jax.ShapeDtypeStruct((count, rows // count, width + HD), jnp.bfloat16),
        in_specs=[whole, vmem, whole, whole, vmem, vmem],
        out_specs=vmem,
        scratch_shapes=[
            pltpu.VMEM((rows, columns), jnp.bfloat16),
            pltpu.VMEM((columns, width), jnp.bfloat16),
            pltpu.VMEM((kv_width, columns), jnp.bfloat16),
            pltpu.VMEM((2, rows, depth), jnp.bfloat16),
            pltpu.VMEM((rows, width), jnp.float32),
            pltpu.VMEM((rows, kv_width), jnp.float32),
            pltpu.SemaphoreType.DMA((chunks,)),
            pltpu.SemaphoreType.DMA((chunks,)),
            pltpu.SemaphoreType.DMA,
        ],
        compiler_params=pltpu.CompilerParams(vmem_limit_bytes=40 * 1024 * 1024),
        cost_estimate=pl.CostEstimate(
            flops=2 * rows * columns * (width + kv_width),
            bytes_accessed=2 * columns * (rows + width + kv_width),
            transcendentals=0,
        ),
    )(hidden_in, gain, w_query, w_keyval.T, cosine, sine)


def attend_kernel(count, lengths_ref, cosine_ref, sine_ref, keys_ref, values_ref, *refs):
    in_ref, out_ref, queries, attended, scores, weights, keys, values, k_sem, v_sem = refs
    me = lax.axis_index("tensor")
    here, span, key_width = keys.shape
    kv_groups = key_width // HD
    parts = attended.shape[0]

    def key_copy(row):
        return pltpu.make_async_copy(keys_ref.at[row], keys.at[row], k_sem.at[row])

    def value_copy(row):
        return pltpu.make_async_copy(values_ref.at[row], values.at[row], v_sem.at[row])

    for row in range(here + 2):
        if row < here:
            key_copy(row).start()
        if row >= 2:
            value_copy(row - 2).start()

    for device in range(count):
        for part in range(parts + 1):
            queries[part, device * here : (device + 1) * here, :] = in_ref[
                device, :, part * HD : (part + 1) * HD
            ].astype(jnp.float32)
    mine = pl.ds(pl.multiple_of(me * here, here), here)
    cosine, sine = cosine_ref[mine, :], sine_ref[mine, :]
    shares = count // (2 * kv_groups)
    tiles = []
    for tile in range(2 * kv_groups):
        joined = jnp.zeros((here, HD), jnp.float32)
        for device in range(tile * shares, (tile + 1) * shares):
            joined = joined + queries[parts, device * here : (device + 1) * here, :]
        tiles.append(joined)
    new_keys = [rotate(tile, cosine, sine) for tile in tiles[:kv_groups]]
    new_keys = jnp.concatenate(new_keys, axis=1).astype(jnp.bfloat16).astype(jnp.float32)
    new_values = jnp.concatenate(tiles[kv_groups:], axis=1)

    shape = (parts * count, key_width)
    group_devices = count // kv_groups
    device = lax.rem(lax.broadcasted_iota(jnp.int32, shape, 0), count)
    column = lax.broadcasted_iota(jnp.int32, shape, 1)
    own_group = lax.div(device, group_devices) == lax.div(column, HD)
    token = lax.broadcasted_iota(jnp.int32, (1, span), 1)
    score_scale = HD ** (-0.5)
    own_scores, own_weights = {}, {}

    def score(row):
        heads = jnp.concatenate(
            [queries[part, pl.ds(row, count, stride=here), :] for part in range(parts)], axis=0
        )
        heads = jnp.where(own_group, jnp.concatenate([heads] * kv_groups, axis=1), 0.0)
        own_scores[row] = (
            jnp.sum(heads * new_keys[row : row + 1], axis=1, keepdims=True) * score_scale
        )
        scores[row % 2] = lax.dot_general(
            heads.astype(jnp.bfloat16),
            keys[row],
            (((1,), (1,)), ((), ())),
            preferred_element_type=jnp.float32,
        )

    def weigh(row):
        valid = token < lengths_ref[row]
        scaled = jnp.where(valid, scores[row % 2] * score_scale, -1e30)
        largest = jnp.maximum(jnp.max(scaled, axis=1, keepdims=True), own_scores[row])
        raised = jnp.exp(scaled - largest)
        own_raised = jnp.exp(own_scores[row] - largest)
        share = 1.0 / (jnp.sum(raised, axis=1, keepdims=True) + own_raised)
        weights[row % 2] = (raised * share).astype(jnp.bfloat16)
        own_weights[row] = (own_raised * share).astype(jnp.bfloat16).astype(jnp.float32)

    def mix(row):
        mixed = jnp.dot(weights[row % 2], values[row], preferred_element_type=jnp.float32)
        mixed = mixed + own_weights[row] * new_values[row : row + 1]
        mixed = jnp.where(own_group, mixed, 0.0)
        chosen = mixed[:, :HD]
        for group in range(1, kv_groups):
            chosen = chosen + mixed[:, group * HD : (group + 1) * HD]
        for part in range(parts):
            attended[part, pl.ds(row, count, stride=here), :] = chosen[
                part * count : (part + 1) * count
            ]

    for step in range(here + 2):
        if step < here:
            key_copy(step).wait()
        if step >= 2:
            value_copy(step - 2).wait()
        if step >= 2:
            mix(step - 2)
        if 1 <= step <= here:
            weigh(step - 1)
        if step < here:
            score(step)
    for k in range(count):
        for part in range(parts):
            out_ref[k, :, part * HD : (part + 1) * HD] = attended[
                part, k * here : (k + 1) * here, :
            ].astype(jnp.bfloat16)


def attend(blocks, lengths, cosine, sine, cache_keys, cache_values):
    count = blocks.shape[0]
    here, span, key_width = cache_keys.shape
    width = blocks.shape[2] - HD
    heads = count * width // HD
    vmem = pl.BlockSpec(memory_space=pltpu.VMEM)
    whole = pl.BlockSpec(memory_space=pltpu.HBM)
    return pl.pallas_call(
        functools.partial(attend_kernel, count),
        out_shape=jax.ShapeDtypeStruct((count, here, width), jnp.bfloat16),
        in_specs=[pl.BlockSpec(memory_space=pltpu.SMEM), vmem, vmem, whole, whole, vmem],
        out_specs=vmem,
        scratch_shapes=[
            pltpu.VMEM((width // HD + 1, here * count, HD), jnp.float32),
            pltpu.VMEM((width // HD, here * count, HD), jnp.float32),
            pltpu.VMEM((2, heads, span), jnp.float32),
            pltpu.VMEM((2, heads, span), jnp.bfloat16),
            pltpu.VMEM((here, span, key_width), jnp.bfloat16),
            pltpu.VMEM((here, span, key_width), jnp.bfloat16),
            pltpu.SemaphoreType.DMA((here,)),
            pltpu.SemaphoreType.DMA((here,)),
        ],
        compiler_params=pltpu.CompilerParams(vmem_limit_bytes=40 * 1024 * 1024),
        cost_estimate=pl.CostEstimate(
            flops=4 * here * count * width * span,
            bytes_accessed=4 * here * span * key_width,
            transcendentals=here * heads * span,
        ),
    )(lengths, cosine, sine, cache_keys, cache_values, blocks)


def exchange(blocks):
    return lax.all_to_all(blocks, "tensor", split_axis=0, concat_axis=0, tiled=True)


def plans(count):
    bits = list(range(1, count.bit_length() - 1))
    turned = bits[::-1]
    late = bits[1:2] + bits[:1] + bits[2:]
    return [(late, late[::-1]), (bits, turned), (bits, turned), (late, late[::-1])]


def timetable(count):
    if count == 16:
        return [int(c) for c in TABLE]
    return [s for _ in range(2 * (count.bit_length() - 2) + 2) for s in (0, 3, 1, 2)]


def place(offset, order):
    spot = 0
    for bit in order:
        spot = spot * 2 + ((offset >> bit) & 1)
    return spot


def project_kernel(count, offsets, w_ref, *refs):
    in_ref, *set_refs, heads_buffer, w_buffer, arrived = refs
    me = lax.axis_index("tensor")
    width = w_buffer.shape[2]
    copies = []
    for slot, offset in enumerate(offsets):
        column = pl.multiple_of(jnp.bitwise_xor(me, offset) * width, width)
        copies.append(
            pltpu.make_async_copy(
                w_ref.at[:, pl.ds(column, width)], w_buffer.at[slot], arrived.at[slot]
            )
        )
        copies[-1].start()
    here = in_ref.shape[1]
    for k in range(count):
        heads_buffer[k * here : (k + 1) * here, :] = in_ref[k].astype(jnp.float32)
    heads = heads_buffer[...].astype(jnp.bfloat16)
    for slot, offset in enumerate(offsets):
        copies[slot].wait()
        product = jnp.dot(heads, w_buffer[slot], preferred_element_type=jnp.float32).astype(
            jnp.bfloat16
        )
        start = 0
        for ref, (order, _) in zip(set_refs, plans(count)):
            ref[place(offset, order)] = product[start : start + ref.shape[1]]
            start += ref.shape[1]


def project(blocks, w_out, offsets):
    count, here, depth = blocks.shape
    rows = count * here
    width = w_out.shape[1] // count
    sets = len(plans(count))
    share = jax.ShapeDtypeStruct((len(offsets), rows // sets, width), jnp.bfloat16)
    return pl.pallas_call(
        functools.partial(project_kernel, count, offsets),
        out_shape=(share,) * sets,
        in_specs=[pl.BlockSpec(memory_space=pltpu.HBM), pl.BlockSpec(memory_space=pltpu.VMEM)],
        out_specs=(pl.BlockSpec(memory_space=pltpu.VMEM),) * sets,
        scratch_shapes=[
            pltpu.VMEM((rows, depth), jnp.float32),
            pltpu.VMEM((len(offsets), depth, width), jnp.bfloat16),
            pltpu.SemaphoreType.DMA((len(offsets),)),
        ],
        compiler_params=pltpu.CompilerParams(vmem_limit_bytes=30 * 1024 * 1024),
        cost_estimate=pl.CostEstimate(
            flops=2 * rows * depth * width * len(offsets),
            bytes_accessed=2 * (depth + rows) * width * len(offsets),
            transcendentals=0,
        ),
    )(w_out, blocks)


def finish_kernel(offsets, own_ref, other_ref, gain_ref, *refs):
    out_ref = refs[-1]
    me = lax.axis_index("tensor")
    half, rows, width = own_ref.shape
    total = jnp.zeros((rows, width), jnp.float32)
    for ref in (own_ref, other_ref):
        for k in range(half):
            block = ref[k].astype(jnp.float32)
            total = total + block * block
    mean_square = jnp.sum(total, axis=1, keepdims=True) / (2 * half * width)
    scale = lax.rsqrt(mean_square + epsilon)
    for k, offset in enumerate(offsets):
        block = (own_ref if k < half else other_ref)[k % half].astype(jnp.float32)
        index = jnp.bitwise_xor(me, offset)
        column = pl.multiple_of(index * width, width)
        gain = gain_ref[pl.ds(index, 1), :]
        out_ref[:, pl.ds(column, width)] = (block * scale * gain).astype(jnp.bfloat16)


def finish(own, other, gain, offsets, which, sets, earlier):
    half, rows, width = own.shape
    columns = 2 * half * width
    operands = [own, other, gain] + ([] if earlier is None else [earlier])
    whole = pl.BlockSpec(memory_space=pltpu.VMEM)
    return pl.pallas_call(
        functools.partial(finish_kernel, offsets),
        grid=(1,),
        out_shape=jax.ShapeDtypeStruct((rows * sets, columns), jnp.bfloat16),
        in_specs=[whole] * 3 + [pl.BlockSpec(memory_space=pl.ANY)] * (len(operands) - 3),
        out_specs=pl.BlockSpec((rows, columns), lambda i: (which, 0)),
        input_output_aliases={} if earlier is None else {3: 0},
        compiler_params=pltpu.CompilerParams(vmem_limit_bytes=24 * 1024 * 1024),
        cost_estimate=pl.CostEstimate(
            flops=6 * rows * columns, bytes_accessed=4 * rows * columns, transcendentals=0
        ),
    )(*operands)


def swap(values, bit, count):
    return lax.ppermute(values, "tensor", [(i, i ^ (1 << bit)) for i in range(count)])


def add(one, other):
    return (one.astype(jnp.float32) + other.astype(jnp.float32)).astype(jnp.bfloat16)


def on_device(
    hidden_in,
    attn_gain,
    w_query,
    w_keyval,
    cache_keys,
    cache_values,
    w_out,
    ffn_gain,
    lengths,
    positions,
):
    row_count = hidden_in.shape[0]
    count = lax.axis_size("tensor")
    my_index = lax.axis_index("tensor")
    cosine, sine = turns(positions)
    blocks = project_in(
        hidden_in, attn_gain.reshape(1, -1), w_query, w_keyval, cosine, sine, count
    )
    head_blocks = exchange(
        attend(exchange(blocks), lengths, cosine, sine, cache_keys, cache_values)
    )
    share_width = w_out.shape[1] // count
    mine = lax.dynamic_slice_in_dim(hidden_in, my_index * share_width, share_width, 1)
    gain = ffn_gain.astype(jnp.float32).reshape(count, share_width)
    orders = plans(count)
    sets = len(orders)
    set_rows = row_count // sets
    sent = project(head_blocks, w_out, list(range(1, count, 2)))
    arrivals = [swap(block, 0, count) for block in sent]
    kept = project(head_blocks, w_out, list(range(0, count, 2)))

    def halves(keep, arrival):
        half = keep.shape[0] // 2
        return add(keep[:half], arrival[:half]), add(keep[half:], arrival[half:])

    held, leaving = zip(*[halves(kept[k], arrivals[k]) for k in range(sets)])
    held = list(held)
    streams = [None] * sets
    offsets = [[0] for _ in range(sets)]
    steps = [0] * sets
    last = normed = None
    for k in timetable(count):
        scatter, gather = orders[k]
        step = steps[k]
        steps[k] += 1
        if step == 0:
            if last is None:
                last = leaving[k]
            else:
                last, _ = lax.optimization_barrier((leaving[k], last))
            arrivals[k] = swap(last, scatter[0], count)
            continue
        held[k], arrivals[k], _ = lax.optimization_barrier((held[k], arrivals[k], last))
        if step < len(scatter):
            held[k], last = halves(held[k], arrivals[k])
            arrivals[k] = swap(last, scatter[step], count)
            continue
        if step == len(scatter):
            own_rows = mine[k * set_rows : (k + 1) * set_rows].astype(jnp.float32)
            total = held[k][0].astype(jnp.float32) + arrivals[k][0].astype(jnp.float32)
            streams[k] = (own_rows + total).astype(jnp.bfloat16)
            last = held[k] = streams[k][None]
        elif step <= len(scatter) + len(gather):
            last = held[k] = jnp.concatenate([held[k], arrivals[k]], axis=0)
        else:
            last = normed = finish(held[k], arrivals[k], gain, offsets[k], k, sets, normed)
            continue
        bit = (gather + [0])[step - len(scatter)]
        arrivals[k] = swap(held[k], bit, count)
        offsets[k] = offsets[k] + [offset ^ (1 << bit) for offset in offsets[k]]
    return (jnp.concatenate(streams, axis=0), normed)


def solution(mesh):
    placed = (
        P("groups", None),
        P(),
        P(None, "tensor"),
        P(None, "tensor"),
        P(("groups", "tensor"), None, None),
        P(("groups", "tensor"), None, None),
        P("tensor", None),
        P(),
        P(("groups", "tensor")),
        P("groups"),
    )
    return jax.shard_map(
        on_device,
        mesh=mesh,
        in_specs=placed,
        out_specs=(P("groups", "tensor"), P("groups", None)),
        check_vma=False,
    )
```

```python
import functools
import math

import jax
import jax.numpy as jnp
from jax import lax
from jax.experimental import pallas as pl
from jax.experimental.pallas import tpu as pltpu
from jax.sharding import PartitionSpec as P

HD = 128


TABLE = "20210320213032013021313012023131"

epsilon = 1e-05
rope_theta = 500000.0


def turns(positions):
    half = HD // 2
    entry = jnp.arange(HD, dtype=jnp.int32)
    frequency = jnp.exp((entry % half).astype(jnp.float32) * (-math.log(rope_theta) / half))
    angles = positions.astype(jnp.float32)[:, None] * frequency[None, :]
    sign = jnp.where(entry < half, -1.0, 1.0)
    return jnp.cos(angles), jnp.sin(angles) * sign


def rotate(head, cosine, sine):
    return head * cosine + pltpu.roll(head, HD // 2, 1) * sine


def input_kernel(count, hidden_ref, gain_ref, w_ref, kv_ref, cosine_ref, sine_ref, *refs):
    out_ref, hidden, w_buffer, kv_buffer, normed, products, kv_products, *sems = refs
    h_sem, w_sem, kv_sem = sems
    me = lax.axis_index("tensor")
    rows, columns = hidden.shape
    depth = normed.shape[2]
    chunks = columns // depth
    width = products.shape[1]
    kv_width = kv_products.shape[1]
    here = rows // count

    def span(k):
        return pl.ds(k * depth, depth)

    def hidden_copy(k):
        return pltpu.make_async_copy(
            hidden_ref.at[:, span(k)], hidden.at[:, span(k)], h_sem.at[k]
        )

    def w_copy(k):
        return pltpu.make_async_copy(w_ref.at[span(k), :], w_buffer.at[span(k), :], w_sem.at[k])

    for k in range(chunks):
        hidden_copy(k).start()
    early = chunks // 4
    for k in range(early):
        w_copy(k).start()
    kv_copy = pltpu.make_async_copy(kv_ref, kv_buffer, kv_sem)
    kv_copy.start()
    products[...] = jnp.zeros_like(products)
    kv_products[...] = jnp.zeros_like(kv_products)
    total = jnp.zeros((rows, 128), jnp.float32)
    for k in range(chunks):
        hidden_copy(k).wait()
        for lane in range(k * depth, (k + 1) * depth, 128):
            part = hidden[:, lane : lane + 128].astype(jnp.float32)
            total = total + part * part
    for k in range(early, chunks):
        w_copy(k).start()
    scale = lax.rsqrt(jnp.sum(total, axis=1, keepdims=True) / columns + epsilon)

    def norm(k):
        floats = hidden[:, span(k)].astype(jnp.float32)
        gain = gain_ref[:, span(k)].astype(jnp.float32)
        normed[k % 2] = (floats * scale * gain).astype(jnp.bfloat16)

    norm(0)
    kv_copy.wait()
    for k in range(chunks):
        w_copy(k).wait()
        products[...] += jnp.dot(
            normed[k % 2], w_buffer[span(k), :], preferred_element_type=jnp.float32
        )
        kv_products[...] += lax.dot_general(
            normed[k % 2],
            kv_buffer[:, span(k)],
            (((1,), (1,)), ((), ())),
            preferred_element_type=jnp.float32,
        )
        if k + 1 < chunks:
            norm(k + 1)

    shift = lax.rem(me, HD // kv_width) * kv_width
    blank = jnp.zeros((rows, HD - kv_width), jnp.float32)
    moved = pltpu.roll(jnp.concatenate([kv_products[...], blank], axis=1), shift, 1)
    results = [
        rotate(products[:, start : start + HD], cosine_ref[...], sine_ref[...])
        for start in range(0, width, HD)
    ] + [moved]
    for part, result in enumerate(results):
        for k in range(count):
            out_ref[k, :, part * HD : (part + 1) * HD] = result[
                k * here : (k + 1) * here
            ].astype(jnp.bfloat16)


def project_in(hidden_in, gain, w_query, w_keyval, cosine, sine, count):
    rows, columns = hidden_in.shape
    width, kv_width = w_query.shape[1], w_keyval.shape[1]
    depth = columns // 8
    chunks = columns // depth
    vmem = pl.BlockSpec(memory_space=pltpu.VMEM)
    whole = pl.BlockSpec(memory_space=pl.ANY)
    return pl.pallas_call(
        functools.partial(input_kernel, count),
        out_shape=jax.ShapeDtypeStruct((count, rows // count, width + HD), jnp.bfloat16),
        in_specs=[whole, vmem, whole, whole, vmem, vmem],
        out_specs=vmem,
        scratch_shapes=[
            pltpu.VMEM((rows, columns), jnp.bfloat16),
            pltpu.VMEM((columns, width), jnp.bfloat16),
            pltpu.VMEM((kv_width, columns), jnp.bfloat16),
            pltpu.VMEM((2, rows, depth), jnp.bfloat16),
            pltpu.VMEM((rows, width), jnp.float32),
            pltpu.VMEM((rows, kv_width), jnp.float32),
            pltpu.SemaphoreType.DMA((chunks,)),
            pltpu.SemaphoreType.DMA((chunks,)),
            pltpu.SemaphoreType.DMA,
        ],
        compiler_params=pltpu.CompilerParams(vmem_limit_bytes=60 * 1024 * 1024),
        cost_estimate=pl.CostEstimate(
            flops=2 * rows * columns * (width + kv_width),
            bytes_accessed=2 * columns * (rows + width + kv_width),
            transcendentals=0,
        ),
    )(hidden_in, gain, w_query, w_keyval.T, cosine, sine)


def attend_kernel(count, lengths_ref, cosine_ref, sine_ref, keys_ref, values_ref, *refs):
    in_ref, out_ref, queries, attended, scores, weights, keys, values, k_sem, v_sem = refs
    me = lax.axis_index("tensor")
    here, span, key_width = keys.shape
    kv_groups = key_width // HD
    parts = attended.shape[0]

    def key_copy(row):
        return pltpu.make_async_copy(keys_ref.at[row], keys.at[row], k_sem.at[row])

    def value_copy(row):
        return pltpu.make_async_copy(values_ref.at[row], values.at[row], v_sem.at[row])

    for row in range(here + 2):
        if row < here:
            key_copy(row).start()
        if row >= 2:
            value_copy(row - 2).start()

    for device in range(count):
        for part in range(parts + 1):
            queries[part, device * here : (device + 1) * here, :] = in_ref[
                device, :, part * HD : (part + 1) * HD
            ].astype(jnp.float32)
    mine = pl.ds(pl.multiple_of(me * here, here), here)
    cosine, sine = cosine_ref[mine, :], sine_ref[mine, :]
    shares = count // (2 * kv_groups)
    tiles = []
    for tile in range(2 * kv_groups):
        joined = jnp.zeros((here, HD), jnp.float32)
        for device in range(tile * shares, (tile + 1) * shares):
            joined = joined + queries[parts, device * here : (device + 1) * here, :]
        tiles.append(joined)
    new_keys = [rotate(tile, cosine, sine) for tile in tiles[:kv_groups]]
    new_keys = jnp.concatenate(new_keys, axis=1).astype(jnp.bfloat16).astype(jnp.float32)
    new_values = jnp.concatenate(tiles[kv_groups:], axis=1)

    shape = (parts * count, key_width)
    group_devices = count // kv_groups
    device = lax.rem(lax.broadcasted_iota(jnp.int32, shape, 0), count)
    column = lax.broadcasted_iota(jnp.int32, shape, 1)
    own_group = lax.div(device, group_devices) == lax.div(column, HD)
    token = lax.broadcasted_iota(jnp.int32, (1, span), 1)
    score_scale = HD ** (-0.5)
    own_scores, own_weights = {}, {}

    def score(row):
        heads = jnp.concatenate(
            [queries[part, pl.ds(row, count, stride=here), :] for part in range(parts)], axis=0
        )
        heads = jnp.where(own_group, jnp.concatenate([heads] * kv_groups, axis=1), 0.0)
        own_scores[row] = (
            jnp.sum(heads * new_keys[row : row + 1], axis=1, keepdims=True) * score_scale
        )
        scores[row % 2] = lax.dot_general(
            heads.astype(jnp.bfloat16),
            keys[row],
            (((1,), (1,)), ((), ())),
            preferred_element_type=jnp.float32,
        )

    def weigh(row):
        valid = token < lengths_ref[row]
        scaled = jnp.where(valid, scores[row % 2] * score_scale, -1e30)
        largest = jnp.maximum(jnp.max(scaled, axis=1, keepdims=True), own_scores[row])
        raised = jnp.exp(scaled - largest)
        own_raised = jnp.exp(own_scores[row] - largest)
        share = 1.0 / (jnp.sum(raised, axis=1, keepdims=True) + own_raised)
        weights[row % 2] = (raised * share).astype(jnp.bfloat16)
        own_weights[row] = (own_raised * share).astype(jnp.bfloat16).astype(jnp.float32)

    def mix(row):
        mixed = jnp.dot(weights[row % 2], values[row], preferred_element_type=jnp.float32)
        mixed = mixed + own_weights[row] * new_values[row : row + 1]
        mixed = jnp.where(own_group, mixed, 0.0)
        chosen = mixed[:, :HD]
        for group in range(1, kv_groups):
            chosen = chosen + mixed[:, group * HD : (group + 1) * HD]
        for part in range(parts):
            attended[part, pl.ds(row, count, stride=here), :] = chosen[
                part * count : (part + 1) * count
            ]

    for step in range(here + 2):
        if step < here:
            key_copy(step).wait()
        if step >= 2:
            value_copy(step - 2).wait()
        if step >= 2:
            mix(step - 2)
        if 1 <= step <= here:
            weigh(step - 1)
        if step < here:
            score(step)
    for k in range(count):
        for part in range(parts):
            out_ref[k, :, part * HD : (part + 1) * HD] = attended[
                part, k * here : (k + 1) * here, :
            ].astype(jnp.bfloat16)


def attend(blocks, lengths, cosine, sine, cache_keys, cache_values):
    count = blocks.shape[0]
    here, span, key_width = cache_keys.shape
    width = blocks.shape[2] - HD
    heads = count * width // HD
    vmem = pl.BlockSpec(memory_space=pltpu.VMEM)
    whole = pl.BlockSpec(memory_space=pl.ANY)
    return pl.pallas_call(
        functools.partial(attend_kernel, count),
        out_shape=jax.ShapeDtypeStruct((count, here, width), jnp.bfloat16),
        in_specs=[pl.BlockSpec(memory_space=pltpu.SMEM), vmem, vmem, whole, whole, vmem],
        out_specs=vmem,
        scratch_shapes=[
            pltpu.VMEM((width // HD + 1, here * count, HD), jnp.float32),
            pltpu.VMEM((width // HD, here * count, HD), jnp.float32),
            pltpu.VMEM((2, heads, span), jnp.float32),
            pltpu.VMEM((2, heads, span), jnp.bfloat16),
            pltpu.VMEM((here, span, key_width), jnp.bfloat16),
            pltpu.VMEM((here, span, key_width), jnp.bfloat16),
            pltpu.SemaphoreType.DMA((here,)),
            pltpu.SemaphoreType.DMA((here,)),
        ],
        compiler_params=pltpu.CompilerParams(vmem_limit_bytes=56 * 1024 * 1024),
        cost_estimate=pl.CostEstimate(
            flops=4 * here * count * width * span,
            bytes_accessed=4 * here * span * key_width,
            transcendentals=here * heads * span,
        ),
    )(lengths, cosine, sine, cache_keys, cache_values, blocks)


def exchange(blocks):
    count, inner = blocks.shape[0], 4
    outer = count // inner
    near = [[o * inner + i for i in range(inner)] for o in range(outer)]
    far = [[o * inner + i for o in range(outer)] for i in range(inner)]
    square = blocks.reshape(outer, inner, *blocks.shape[1:])
    square = lax.all_to_all(square, "tensor", 1, 1, axis_index_groups=near, tiled=True)
    square = lax.all_to_all(square, "tensor", 0, 0, axis_index_groups=far, tiled=True)
    return square.reshape(blocks.shape)


def plans(count):
    bits = list(range(1, count.bit_length() - 1))
    turned = bits[::-1]
    late = bits[1:2] + bits[:1] + bits[2:]
    return [(late, late[::-1]), (bits, turned), (bits, turned), (late, late[::-1])]


def timetable(count):
    if count == 16:
        return [int(c) for c in TABLE]
    return [s for _ in range(2 * (count.bit_length() - 2) + 2) for s in (0, 3, 1, 2)]


def place(offset, order):
    spot = 0
    for bit in order:
        spot = spot * 2 + ((offset >> bit) & 1)
    return spot


def project_kernel(count, offsets, w_ref, *refs):
    in_ref, *set_refs, heads_buffer, w_buffer, arrived = refs
    me = lax.axis_index("tensor")
    width = w_buffer.shape[2]
    copies = []
    for slot, offset in enumerate(offsets):
        column = pl.multiple_of(jnp.bitwise_xor(me, offset) * width, width)
        copies.append(
            pltpu.make_async_copy(
                w_ref.at[:, pl.ds(column, width)], w_buffer.at[slot], arrived.at[slot]
            )
        )
        copies[-1].start()
    here = in_ref.shape[1]
    for k in range(count):
        heads_buffer[k * here : (k + 1) * here, :] = in_ref[k].astype(jnp.float32)
    heads = heads_buffer[...].astype(jnp.bfloat16)
    for slot, offset in enumerate(offsets):
        copies[slot].wait()
        product = jnp.dot(heads, w_buffer[slot], preferred_element_type=jnp.float32).astype(
            jnp.bfloat16
        )
        start = 0
        for ref, (order, _) in zip(set_refs, plans(count)):
            ref[place(offset, order)] = product[start : start + ref.shape[1]]
            start += ref.shape[1]


def project(blocks, w_out, offsets):
    count, here, depth = blocks.shape
    rows = count * here
    width = w_out.shape[1] // count
    sets = len(plans(count))
    share = jax.ShapeDtypeStruct((len(offsets), rows // sets, width), jnp.bfloat16)
    return pl.pallas_call(
        functools.partial(project_kernel, count, offsets),
        out_shape=(share,) * sets,
        in_specs=[pl.BlockSpec(memory_space=pl.ANY), pl.BlockSpec(memory_space=pltpu.VMEM)],
        out_specs=(pl.BlockSpec(memory_space=pltpu.VMEM),) * sets,
        scratch_shapes=[
            pltpu.VMEM((rows, depth), jnp.float32),
            pltpu.VMEM((len(offsets), depth, width), jnp.bfloat16),
            pltpu.SemaphoreType.DMA((len(offsets),)),
        ],
        compiler_params=pltpu.CompilerParams(vmem_limit_bytes=49 * 1024 * 1024),
        cost_estimate=pl.CostEstimate(
            flops=2 * rows * depth * width * len(offsets),
            bytes_accessed=2 * (depth + rows) * width * len(offsets),
            transcendentals=0,
        ),
    )(w_out, blocks)


def finish_kernel(offsets, own_ref, other_ref, gain_ref, *refs):
    out_ref = refs[-1]
    me = lax.axis_index("tensor")
    half, rows, width = own_ref.shape
    total = jnp.zeros((rows, width), jnp.float32)
    for ref in (own_ref, other_ref):
        for k in range(half):
            block = ref[k].astype(jnp.float32)
            total = total + block * block
    mean_square = jnp.sum(total, axis=1, keepdims=True) / (2 * half * width)
    scale = lax.rsqrt(mean_square + epsilon)
    for k, offset in enumerate(offsets):
        block = (own_ref if k < half else other_ref)[k % half].astype(jnp.float32)
        index = jnp.bitwise_xor(me, offset)
        column = pl.multiple_of(index * width, width)
        gain = gain_ref[pl.ds(index, 1), :]
        out_ref[:, pl.ds(column, width)] = (block * scale * gain).astype(jnp.bfloat16)


def finish(own, other, gain, offsets, which, sets, earlier):
    half, rows, width = own.shape
    columns = 2 * half * width
    operands = [own, other, gain] + ([] if earlier is None else [earlier])
    whole = pl.BlockSpec(memory_space=pltpu.VMEM)
    return pl.pallas_call(
        functools.partial(finish_kernel, offsets),
        grid=(1,),
        out_shape=jax.ShapeDtypeStruct((rows * sets, columns), jnp.bfloat16),
        in_specs=[whole] * 3 + [pl.BlockSpec(memory_space=pl.ANY)] * (len(operands) - 3),
        out_specs=pl.BlockSpec((rows, columns), lambda i: (which, 0)),
        input_output_aliases={} if earlier is None else {3: 0},
        compiler_params=pltpu.CompilerParams(vmem_limit_bytes=24 * 1024 * 1024),
        cost_estimate=pl.CostEstimate(
            flops=6 * rows * columns, bytes_accessed=4 * rows * columns, transcendentals=0
        ),
    )(*operands)


def swap(values, bit, count):
    return lax.ppermute(values, "tensor", [(i, i ^ (1 << bit)) for i in range(count)])


def add(one, other):
    return (one.astype(jnp.float32) + other.astype(jnp.float32)).astype(jnp.bfloat16)


def on_device(
    hidden_in,
    attn_gain,
    w_query,
    w_keyval,
    cache_keys,
    cache_values,
    w_out,
    ffn_gain,
    lengths,
    positions,
):
    row_count = hidden_in.shape[0]
    count = lax.axis_size("tensor")
    my_index = lax.axis_index("tensor")
    cosine, sine = turns(positions)
    blocks = project_in(
        hidden_in, attn_gain.reshape(1, -1), w_query, w_keyval, cosine, sine, count
    )
    head_blocks = exchange(
        attend(exchange(blocks), lengths, cosine, sine, cache_keys, cache_values)
    )
    share_width = w_out.shape[1] // count
    mine = lax.dynamic_slice_in_dim(hidden_in, my_index * share_width, share_width, 1)
    gain = ffn_gain.astype(jnp.float32).reshape(count, share_width)
    orders = plans(count)
    sets = len(orders)
    set_rows = row_count // sets
    sent = project(head_blocks, w_out, list(range(1, count, 2)))
    arrivals = [swap(block, 0, count) for block in sent]
    kept = project(head_blocks, w_out, list(range(0, count, 2)))

    def halves(keep, arrival):
        half = keep.shape[0] // 2
        return add(keep[:half], arrival[:half]), add(keep[half:], arrival[half:])

    held, leaving = zip(*[halves(kept[k], arrivals[k]) for k in range(sets)])
    held = list(held)
    streams = [None] * sets
    offsets = [[0] for _ in range(sets)]
    steps = [0] * sets
    last = normed = None
    for k in timetable(count):
        scatter, gather = orders[k]
        step = steps[k]
        steps[k] += 1
        if step == 0:
            if last is None:
                last = leaving[k]
            else:
                last, _ = lax.optimization_barrier((leaving[k], last))
            arrivals[k] = swap(last, scatter[0], count)
            continue
        held[k], arrivals[k], _ = lax.optimization_barrier((held[k], arrivals[k], last))
        if step < len(scatter):
            held[k], last = halves(held[k], arrivals[k])
            arrivals[k] = swap(last, scatter[step], count)
            continue
        if step == len(scatter):
            own_rows = mine[k * set_rows : (k + 1) * set_rows].astype(jnp.float32)
            total = held[k][0].astype(jnp.float32) + arrivals[k][0].astype(jnp.float32)
            streams[k] = (own_rows + total).astype(jnp.bfloat16)
            last = held[k] = streams[k][None]
        elif step <= len(scatter) + len(gather):
            last = held[k] = jnp.concatenate([held[k], arrivals[k]], axis=0)
        else:
            last = normed = finish(held[k], arrivals[k], gain, offsets[k], k, sets, normed)
            continue
        bit = (gather + [0])[step - len(scatter)]
        arrivals[k] = swap(held[k], bit, count)
        offsets[k] = offsets[k] + [offset ^ (1 << bit) for offset in offsets[k]]
    return (jnp.concatenate(streams, axis=0), normed)


def solution(mesh):
    placed = (
        P("groups", None),
        P(),
        P(None, "tensor"),
        P(None, "tensor"),
        P(("groups", "tensor"), None, None),
        P(("groups", "tensor"), None, None),
        P("tensor", None),
        P(),
        P(("groups", "tensor")),
        P("groups"),
    )
    return jax.shard_map(
        on_device,
        mesh=mesh,
        in_specs=placed,
        out_specs=(P("groups", "tensor"), P("groups", None)),
        check_vma=False,
    )
```

```python
import functools
import math

import jax
import jax.numpy as jnp
from jax import lax
from jax.experimental import pallas as pl
from jax.experimental.pallas import tpu as pltpu
from jax.sharding import PartitionSpec as P

HD = 128


TABLE = "20210320213032013021313012023131"

epsilon = 1e-05
rope_theta = 500000.0


def turns(positions):
    half = HD // 2
    entry = jnp.arange(HD, dtype=jnp.int32)
    frequency = jnp.exp((entry % half).astype(jnp.float32) * (-math.log(rope_theta) / half))
    angles = positions.astype(jnp.float32)[:, None] * frequency[None, :]
    sign = jnp.where(entry < half, -1.0, 1.0)
    return jnp.cos(angles), jnp.sin(angles) * sign


def rotate(head, cosine, sine):
    return head * cosine + pltpu.roll(head, HD // 2, 1) * sine


def input_kernel(count, hidden_ref, gain_ref, w_ref, kv_ref, cosine_ref, sine_ref, *refs):
    out_ref, mine_ref, hidden, w_buffer, kv_buffer, normed, products, kv_products, *sems = refs
    h_sem, w_sem, kv_sem, mine_sem = sems
    me = lax.axis_index("tensor")
    rows, columns = hidden.shape
    depth = normed.shape[2]
    chunks = columns // depth
    width = products.shape[1]
    kv_width = kv_products.shape[1]
    here = rows // count

    def span(k):
        return pl.ds(k * depth, depth)

    def hidden_copy(k):
        return pltpu.make_async_copy(
            hidden_ref.at[:, span(k)], hidden.at[:, span(k)], h_sem.at[k]
        )

    def w_copy(k):
        return pltpu.make_async_copy(w_ref.at[span(k), :], w_buffer.at[span(k), :], w_sem.at[k])

    for k in range(chunks):
        hidden_copy(k).start()
    kv_copy = pltpu.make_async_copy(kv_ref, kv_buffer, kv_sem)
    own = pl.ds(pl.multiple_of(me * (columns // count), columns // count), columns // count)
    mine_copy = pltpu.make_async_copy(hidden_ref.at[:, own], mine_ref, mine_sem)
    products[...] = jnp.zeros_like(products)
    kv_products[...] = jnp.zeros_like(kv_products)
    total = jnp.zeros((rows, 128), jnp.float32)
    for k in range(chunks):
        hidden_copy(k).wait()
        w_copy(k).start()
        if k == 0:
            kv_copy.start()
        for lane in range(k * depth, (k + 1) * depth, 128):
            part = hidden[:, lane : lane + 128].astype(jnp.float32)
            total = total + part * part
    mine_copy.start()
    scale = lax.rsqrt(jnp.sum(total, axis=1, keepdims=True) / columns + epsilon)

    def norm(k):
        floats = hidden[:, span(k)].astype(jnp.float32)
        gain = gain_ref[span(k)].astype(jnp.float32).reshape(1, depth)
        normed[k % 2] = (floats * scale * gain).astype(jnp.bfloat16)

    norm(0)
    kv_copy.wait()
    for k in range(chunks):
        w_copy(k).wait()
        products[...] += jnp.dot(
            normed[k % 2], w_buffer[span(k), :], preferred_element_type=jnp.float32
        )
        kv_products[...] += lax.dot_general(
            normed[k % 2],
            kv_buffer[:, span(k)],
            (((1,), (1,)), ((), ())),
            preferred_element_type=jnp.float32,
        )
        if k + 1 < chunks:
            norm(k + 1)

    shift = lax.rem(me, HD // kv_width) * kv_width
    blank = jnp.zeros((rows, HD - kv_width), jnp.float32)
    moved = pltpu.roll(jnp.concatenate([kv_products[...], blank], axis=1), shift, 1)
    results = [
        rotate(products[:, start : start + HD], cosine_ref[...], sine_ref[...])
        for start in range(0, width, HD)
    ] + [moved]
    for part, result in enumerate(results):
        for k in range(count):
            out_ref[k, :, part * HD : (part + 1) * HD] = result[
                k * here : (k + 1) * here
            ].astype(jnp.bfloat16)
    mine_copy.wait()


def project_in(hidden_in, gain, w_query, w_keyval, cosine, sine, count):
    rows, columns = hidden_in.shape
    width, kv_width = w_query.shape[1], w_keyval.shape[1]
    depth = columns // 8
    chunks = columns // depth
    vmem = pl.BlockSpec(memory_space=pltpu.VMEM)
    whole = pl.BlockSpec(memory_space=pl.ANY)
    return pl.pallas_call(
        functools.partial(input_kernel, count),
        out_shape=(
            jax.ShapeDtypeStruct((count, rows // count, width + HD), jnp.bfloat16),
            jax.ShapeDtypeStruct((rows, columns // count), jnp.bfloat16),
        ),
        in_specs=[whole, vmem, whole, whole, vmem, vmem],
        out_specs=(vmem, vmem),
        scratch_shapes=[
            pltpu.VMEM((rows, columns), jnp.bfloat16),
            pltpu.VMEM((columns, width), jnp.bfloat16),
            pltpu.VMEM((kv_width, columns), jnp.bfloat16),
            pltpu.VMEM((2, rows, depth), jnp.bfloat16),
            pltpu.VMEM((rows, width), jnp.float32),
            pltpu.VMEM((rows, kv_width), jnp.float32),
            pltpu.SemaphoreType.DMA((chunks,)),
            pltpu.SemaphoreType.DMA((chunks,)),
            pltpu.SemaphoreType.DMA,
            pltpu.SemaphoreType.DMA,
        ],
        compiler_params=pltpu.CompilerParams(vmem_limit_bytes=52 * 1024 * 1024),
        cost_estimate=pl.CostEstimate(
            flops=2 * rows * columns * (width + kv_width),
            bytes_accessed=2 * columns * (rows + width + kv_width),
            transcendentals=0,
        ),
    )(hidden_in, gain, w_query, w_keyval.T, cosine, sine)


def attend_kernel(count, lengths_ref, cosine_ref, sine_ref, keys_ref, values_ref, *refs):
    in_ref, out_ref, queries, attended, scores, weights, keys, values, k_sem, v_sem = refs
    me = lax.axis_index("tensor")
    here, span, key_width = keys.shape
    kv_groups = key_width // HD
    parts = attended.shape[0]

    def key_copy(row):
        return pltpu.make_async_copy(keys_ref.at[row], keys.at[row], k_sem.at[row])

    def value_copy(row):
        return pltpu.make_async_copy(values_ref.at[row], values.at[row], v_sem.at[row])

    for row in range(here + 2):
        if row < here:
            key_copy(row).start()
        if row >= 2:
            value_copy(row - 2).start()

    for device in range(count):
        for part in range(parts + 1):
            queries[part, device * here : (device + 1) * here, :] = in_ref[
                device, :, part * HD : (part + 1) * HD
            ].astype(jnp.float32)
    mine = pl.ds(pl.multiple_of(me * here, here), here)
    cosine, sine = cosine_ref[mine, :], sine_ref[mine, :]
    shares = count // (2 * kv_groups)
    tiles = []
    for tile in range(2 * kv_groups):
        joined = jnp.zeros((here, HD), jnp.float32)
        for device in range(tile * shares, (tile + 1) * shares):
            joined = joined + queries[parts, device * here : (device + 1) * here, :]
        tiles.append(joined)
    new_keys = [rotate(tile, cosine, sine) for tile in tiles[:kv_groups]]
    new_keys = jnp.concatenate(new_keys, axis=1).astype(jnp.bfloat16).astype(jnp.float32)
    new_values = jnp.concatenate(tiles[kv_groups:], axis=1)

    shape = (parts * count, key_width)
    group_devices = count // kv_groups
    device = lax.rem(lax.broadcasted_iota(jnp.int32, shape, 0), count)
    column = lax.broadcasted_iota(jnp.int32, shape, 1)
    own_group = lax.div(device, group_devices) == lax.div(column, HD)
    token = lax.broadcasted_iota(jnp.int32, (1, span), 1)
    score_scale = HD ** (-0.5)
    own_scores, own_weights = {}, {}

    def score(row):
        heads = jnp.concatenate(
            [queries[part, pl.ds(row, count, stride=here), :] for part in range(parts)], axis=0
        )
        heads = jnp.where(own_group, jnp.concatenate([heads] * kv_groups, axis=1), 0.0)
        own_scores[row] = (
            jnp.sum(heads * new_keys[row : row + 1], axis=1, keepdims=True) * score_scale
        )
        scores[row % 2] = lax.dot_general(
            heads.astype(jnp.bfloat16),
            keys[row],
            (((1,), (1,)), ((), ())),
            preferred_element_type=jnp.float32,
        )

    def weigh(row):
        valid = token < lengths_ref[row]
        scaled = jnp.where(valid, scores[row % 2] * score_scale, -1e30)
        largest = jnp.maximum(jnp.max(scaled, axis=1, keepdims=True), own_scores[row])
        raised = jnp.exp(scaled - largest)
        own_raised = jnp.exp(own_scores[row] - largest)
        share = 1.0 / (jnp.sum(raised, axis=1, keepdims=True) + own_raised)
        weights[row % 2] = (raised * share).astype(jnp.bfloat16)
        own_weights[row] = (own_raised * share).astype(jnp.bfloat16).astype(jnp.float32)

    def mix(row):
        mixed = jnp.dot(weights[row % 2], values[row], preferred_element_type=jnp.float32)
        mixed = mixed + own_weights[row] * new_values[row : row + 1]
        mixed = jnp.where(own_group, mixed, 0.0)
        chosen = mixed[:, :HD]
        for group in range(1, kv_groups):
            chosen = chosen + mixed[:, group * HD : (group + 1) * HD]
        for part in range(parts):
            attended[part, pl.ds(row, count, stride=here), :] = chosen[
                part * count : (part + 1) * count
            ]

    for step in range(here + 2):
        if step < here:
            key_copy(step).wait()
        if step >= 2:
            value_copy(step - 2).wait()
        if step >= 2:
            mix(step - 2)
        if 1 <= step <= here:
            weigh(step - 1)
        if step < here:
            score(step)
    for k in range(count):
        for part in range(parts):
            out_ref[k, :, part * HD : (part + 1) * HD] = attended[
                part, k * here : (k + 1) * here, :
            ].astype(jnp.bfloat16)


def attend(blocks, lengths, cosine, sine, cache_keys, cache_values):
    count = blocks.shape[0]
    here, span, key_width = cache_keys.shape
    width = blocks.shape[2] - HD
    heads = count * width // HD
    vmem = pl.BlockSpec(memory_space=pltpu.VMEM)
    whole = pl.BlockSpec(memory_space=pl.ANY)
    return pl.pallas_call(
        functools.partial(attend_kernel, count),
        out_shape=jax.ShapeDtypeStruct((count, here, width), jnp.bfloat16),
        in_specs=[pl.BlockSpec(memory_space=pltpu.SMEM), vmem, vmem, whole, whole, vmem],
        out_specs=vmem,
        scratch_shapes=[
            pltpu.VMEM((width // HD + 1, here * count, HD), jnp.float32),
            pltpu.VMEM((width // HD, here * count, HD), jnp.float32),
            pltpu.VMEM((2, heads, span), jnp.float32),
            pltpu.VMEM((2, heads, span), jnp.bfloat16),
            pltpu.VMEM((here, span, key_width), jnp.bfloat16),
            pltpu.VMEM((here, span, key_width), jnp.bfloat16),
            pltpu.SemaphoreType.DMA((here,)),
            pltpu.SemaphoreType.DMA((here,)),
        ],
        compiler_params=pltpu.CompilerParams(vmem_limit_bytes=40 * 1024 * 1024),
        cost_estimate=pl.CostEstimate(
            flops=4 * here * count * width * span,
            bytes_accessed=4 * here * span * key_width,
            transcendentals=here * heads * span,
        ),
    )(lengths, cosine, sine, cache_keys, cache_values, blocks)


def exchange(blocks):
    return lax.all_to_all(blocks, "tensor", split_axis=0, concat_axis=0, tiled=True)


def plans(count):
    bits = list(range(1, count.bit_length() - 1))
    turned = bits[::-1]
    late = bits[1:2] + bits[:1] + bits[2:]
    return [(late, late[::-1]), (bits, turned), (bits, turned), (late, late[::-1])]


def timetable(count):
    if count == 16:
        return [int(c) for c in TABLE]
    return [s for _ in range(2 * (count.bit_length() - 2) + 2) for s in (0, 3, 1, 2)]


def place(offset, order):
    spot = 0
    for bit in order:
        spot = spot * 2 + ((offset >> bit) & 1)
    return spot


def project_kernel(count, offsets, w_ref, *refs):
    in_ref, *set_refs, heads_buffer, w_buffer, arrived = refs
    me = lax.axis_index("tensor")
    width = w_buffer.shape[2]
    copies = []
    for slot, offset in enumerate(offsets):
        column = pl.multiple_of(jnp.bitwise_xor(me, offset) * width, width)
        copies.append(
            pltpu.make_async_copy(
                w_ref.at[:, pl.ds(column, width)], w_buffer.at[slot], arrived.at[slot]
            )
        )
        copies[-1].start()
    here = in_ref.shape[1]
    for k in range(count):
        heads_buffer[k * here : (k + 1) * here, :] = in_ref[k].astype(jnp.float32)
    heads = heads_buffer[...].astype(jnp.bfloat16)
    for slot, offset in enumerate(offsets):
        copies[slot].wait()
        product = jnp.dot(heads, w_buffer[slot], preferred_element_type=jnp.float32).astype(
            jnp.bfloat16
        )
        start = 0
        for ref, (order, _) in zip(set_refs, plans(count)):
            ref[place(offset, order)] = product[start : start + ref.shape[1]]
            start += ref.shape[1]


def project(blocks, w_out, offsets):
    count, here, depth = blocks.shape
    rows = count * here
    width = w_out.shape[1] // count
    sets = len(plans(count))
    share = jax.ShapeDtypeStruct((len(offsets), rows // sets, width), jnp.bfloat16)
    return pl.pallas_call(
        functools.partial(project_kernel, count, offsets),
        out_shape=(share,) * sets,
        in_specs=[pl.BlockSpec(memory_space=pl.ANY), pl.BlockSpec(memory_space=pltpu.VMEM)],
        out_specs=(pl.BlockSpec(memory_space=pltpu.VMEM),) * sets,
        scratch_shapes=[
            pltpu.VMEM((rows, depth), jnp.float32),
            pltpu.VMEM((len(offsets), depth, width), jnp.bfloat16),
            pltpu.SemaphoreType.DMA((len(offsets),)),
        ],
        compiler_params=pltpu.CompilerParams(vmem_limit_bytes=48 * 1024 * 1024),
        cost_estimate=pl.CostEstimate(
            flops=2 * rows * depth * width * len(offsets),
            bytes_accessed=2 * (depth + rows) * width * len(offsets),
            transcendentals=0,
        ),
    )(w_out, blocks)


def finish_kernel(offsets, own_ref, other_ref, gain_ref, *refs):
    out_ref = refs[-1]
    me = lax.axis_index("tensor")
    half, rows, width = own_ref.shape
    total = jnp.zeros((rows, width), jnp.float32)
    for ref in (own_ref, other_ref):
        for k in range(half):
            block = ref[k].astype(jnp.float32)
            total = total + block * block
    mean_square = jnp.sum(total, axis=1, keepdims=True) / (2 * half * width)
    scale = lax.rsqrt(mean_square + epsilon)
    for k, offset in enumerate(offsets):
        block = (own_ref if k < half else other_ref)[k % half].astype(jnp.float32)
        index = jnp.bitwise_xor(me, offset)
        column = pl.multiple_of(index * width, width)
        gain = gain_ref[pl.ds(index, 1), :]
        out_ref[:, pl.ds(column, width)] = (block * scale * gain).astype(jnp.bfloat16)


def finish(own, other, gain, offsets, which, sets, earlier):
    half, rows, width = own.shape
    columns = 2 * half * width
    operands = [own, other, gain] + ([] if earlier is None else [earlier])
    whole = pl.BlockSpec(memory_space=pltpu.VMEM)
    return pl.pallas_call(
        functools.partial(finish_kernel, offsets),
        grid=(1,),
        out_shape=jax.ShapeDtypeStruct((rows * sets, columns), jnp.bfloat16),
        in_specs=[whole] * 3 + [pl.BlockSpec(memory_space=pl.ANY)] * (len(operands) - 3),
        out_specs=pl.BlockSpec((rows, columns), lambda i: (which, 0)),
        input_output_aliases={} if earlier is None else {3: 0},
        compiler_params=pltpu.CompilerParams(vmem_limit_bytes=24 * 1024 * 1024),
        cost_estimate=pl.CostEstimate(
            flops=6 * rows * columns, bytes_accessed=4 * rows * columns, transcendentals=0
        ),
    )(*operands)


def swap(values, bit, count):
    return lax.ppermute(values, "tensor", [(i, i ^ (1 << bit)) for i in range(count)])


def add(one, other):
    return (one.astype(jnp.float32) + other.astype(jnp.float32)).astype(jnp.bfloat16)


def on_device(
    hidden_in,
    attn_gain,
    w_query,
    w_keyval,
    cache_keys,
    cache_values,
    w_out,
    ffn_gain,
    lengths,
    positions,
):
    row_count = hidden_in.shape[0]
    count = lax.axis_size("tensor")
    cosine, sine = turns(positions)
    blocks, mine = project_in(
        hidden_in, attn_gain, w_query, w_keyval, cosine, sine, count
    )
    head_blocks = exchange(
        attend(exchange(blocks), lengths, cosine, sine, cache_keys, cache_values)
    )
    share_width = w_out.shape[1] // count
    gain = ffn_gain.astype(jnp.float32).reshape(count, share_width)
    orders = plans(count)
    sets = len(orders)
    set_rows = row_count // sets
    sent = project(head_blocks, w_out, list(range(1, count, 2)))
    arrivals = [swap(block, 0, count) for block in sent]
    kept = project(head_blocks, w_out, list(range(0, count, 2)))

    def halves(keep, arrival):
        half = keep.shape[0] // 2
        return add(keep[:half], arrival[:half]), add(keep[half:], arrival[half:])

    held, leaving = zip(*[halves(kept[k], arrivals[k]) for k in range(sets)])
    held = list(held)
    streams = [None] * sets
    offsets = [[0] for _ in range(sets)]
    steps = [0] * sets
    last = normed = None
    for k in timetable(count):
        scatter, gather = orders[k]
        step = steps[k]
        steps[k] += 1
        if step == 0:
            if last is None:
                last = leaving[k]
            else:
                last, _ = lax.optimization_barrier((leaving[k], last))
            arrivals[k] = swap(last, scatter[0], count)
            continue
        held[k], arrivals[k], _ = lax.optimization_barrier((held[k], arrivals[k], last))
        if step < len(scatter):
            held[k], last = halves(held[k], arrivals[k])
            arrivals[k] = swap(last, scatter[step], count)
            continue
        if step == len(scatter):
            own_rows = mine[k * set_rows : (k + 1) * set_rows].astype(jnp.float32)
            total = held[k][0].astype(jnp.float32) + arrivals[k][0].astype(jnp.float32)
            streams[k] = (own_rows + total).astype(jnp.bfloat16)
            last = held[k] = streams[k][None]
        elif step <= len(scatter) + len(gather):
            last = held[k] = jnp.concatenate([held[k], arrivals[k]], axis=0)
        else:
            last = normed = finish(held[k], arrivals[k], gain, offsets[k], k, sets, normed)
            continue
        bit = (gather + [0])[step - len(scatter)]
        arrivals[k] = swap(held[k], bit, count)
        offsets[k] = offsets[k] + [offset ^ (1 << bit) for offset in offsets[k]]
    return (jnp.concatenate(streams, axis=0), normed)


def solution(mesh):
    placed = (
        P("groups", None),
        P(),
        P(None, "tensor"),
        P(None, "tensor"),
        P(("groups", "tensor"), None, None),
        P(("groups", "tensor"), None, None),
        P("tensor", None),
        P(),
        P(("groups", "tensor")),
        P("groups"),
    )
    return jax.shard_map(
        on_device,
        mesh=mesh,
        in_specs=placed,
        out_specs=(P("groups", "tensor"), P("groups", None)),
        check_vma=False,
    )
```

```python
import functools
import math

import jax
import jax.numpy as jnp
from jax import lax
from jax.experimental import pallas as pl
from jax.experimental.pallas import tpu as pltpu
from jax.sharding import PartitionSpec as P

HD = 128


TABLE = "101203101230310230123230211323"

epsilon = 1e-05
rope_theta = 500000.0


def turns(positions):
    half = HD // 2
    entry = jnp.arange(HD, dtype=jnp.int32)
    frequency = jnp.exp((entry % half).astype(jnp.float32) * (-math.log(rope_theta) / half))
    angles = positions.astype(jnp.float32)[:, None] * frequency[None, :]
    sign = jnp.where(entry < half, -1.0, 1.0)
    return jnp.cos(angles), jnp.sin(angles) * sign


def rotate(head, cosine, sine):
    return head * cosine + pltpu.roll(head, HD // 2, 1) * sine


def input_kernel(count, hidden_ref, gain_ref, w_ref, kv_ref, cosine_ref, sine_ref, *refs):
    out_ref, mine_ref, hidden, gain_buffer, w_buffer, kv_buffer, normed, products, kv_products, *sems = refs
    h_sem, w_sem, kv_sem, mine_sem, gain_sem = sems
    me = lax.axis_index("tensor")
    rows, columns = hidden.shape
    depth = normed.shape[2]
    chunks = columns // depth
    width = products.shape[1]
    kv_width = kv_products.shape[1]
    here = rows // count

    def span(k):
        return pl.ds(k * depth, depth)

    def hidden_copy(k):
        return pltpu.make_async_copy(
            hidden_ref.at[:, span(k)], hidden.at[:, span(k)], h_sem.at[k]
        )

    def w_copy(k):
        return pltpu.make_async_copy(w_ref.at[span(k), :], w_buffer.at[span(k), :], w_sem.at[k])

    for k in range(chunks):
        hidden_copy(k).start()
    gain_copy = pltpu.make_async_copy(gain_ref, gain_buffer, gain_sem)
    gain_copy.start()
    kv_copy = pltpu.make_async_copy(kv_ref, kv_buffer, kv_sem)
    own = pl.ds(pl.multiple_of(me * (columns // count), columns // count), columns // count)
    mine_copy = pltpu.make_async_copy(hidden_ref.at[:, own], mine_ref, mine_sem)
    products[...] = jnp.zeros_like(products)
    kv_products[...] = jnp.zeros_like(kv_products)
    total = jnp.zeros((rows, 128), jnp.float32)
    for k in range(chunks):
        hidden_copy(k).wait()
        w_copy(k).start()
        if k == 0:
            kv_copy.start()
        for lane in range(k * depth, (k + 1) * depth, 128):
            part = hidden[:, lane : lane + 128].astype(jnp.float32)
            total = total + part * part
    mine_copy.start()
    scale = lax.rsqrt(jnp.sum(total, axis=1, keepdims=True) / columns + epsilon)

    def norm(k):
        floats = hidden[:, span(k)].astype(jnp.float32)
        gain = gain_buffer[span(k)].astype(jnp.float32).reshape(1, depth)
        normed[k % 2] = (floats * scale * gain).astype(jnp.bfloat16)

    gain_copy.wait()
    norm(0)
    kv_copy.wait()
    for k in range(chunks):
        w_copy(k).wait()
        products[...] += jnp.dot(
            normed[k % 2], w_buffer[span(k), :], preferred_element_type=jnp.float32
        )
        kv_products[...] += lax.dot_general(
            normed[k % 2],
            kv_buffer[:, span(k)],
            (((1,), (1,)), ((), ())),
            preferred_element_type=jnp.float32,
        )
        if k + 1 < chunks:
            norm(k + 1)

    shift = lax.rem(me, HD // kv_width) * kv_width
    blank = jnp.zeros((rows, HD - kv_width), jnp.float32)
    moved = pltpu.roll(jnp.concatenate([kv_products[...], blank], axis=1), shift, 1)
    results = [
        rotate(products[:, start : start + HD], cosine_ref[...], sine_ref[...])
        for start in range(0, width, HD)
    ] + [moved]
    for part, result in enumerate(results):
        for k in range(count):
            out_ref[k, :, part * HD : (part + 1) * HD] = result[
                k * here : (k + 1) * here
            ].astype(jnp.bfloat16)
    mine_copy.wait()


def project_in(hidden_in, gain, w_query, w_keyval, cosine, sine, count):
    rows, columns = hidden_in.shape
    width, kv_width = w_query.shape[1], w_keyval.shape[1]
    depth = columns // 8
    chunks = columns // depth
    vmem = pl.BlockSpec(memory_space=pltpu.VMEM)
    whole = pl.BlockSpec(memory_space=pl.ANY)
    return pl.pallas_call(
        functools.partial(input_kernel, count),
        out_shape=(
            jax.ShapeDtypeStruct((count, rows // count, width + HD), jnp.bfloat16),
            jax.ShapeDtypeStruct((rows, columns // count), jnp.bfloat16),
        ),
        in_specs=[whole, whole, whole, whole, vmem, vmem],
        out_specs=(vmem, vmem),
        scratch_shapes=[
            pltpu.VMEM((rows, columns), jnp.bfloat16),
            pltpu.VMEM((columns,), jnp.bfloat16),
            pltpu.VMEM((columns, width), jnp.bfloat16),
            pltpu.VMEM((kv_width, columns), jnp.bfloat16),
            pltpu.VMEM((2, rows, depth), jnp.bfloat16),
            pltpu.VMEM((rows, width), jnp.float32),
            pltpu.VMEM((rows, kv_width), jnp.float32),
            pltpu.SemaphoreType.DMA((chunks,)),
            pltpu.SemaphoreType.DMA((chunks,)),
            pltpu.SemaphoreType.DMA,
            pltpu.SemaphoreType.DMA,
            pltpu.SemaphoreType.DMA,
        ],
        compiler_params=pltpu.CompilerParams(vmem_limit_bytes=52 * 1024 * 1024),
        cost_estimate=pl.CostEstimate(
            flops=2 * rows * columns * (width + kv_width),
            bytes_accessed=2 * columns * (rows + width + kv_width),
            transcendentals=0,
        ),
    )(hidden_in, gain, w_query, w_keyval.T, cosine, sine)


def attend_kernel(count, lengths_ref, cosine_ref, sine_ref, keys_ref, values_ref, *refs):
    in_ref, out_ref, queries, attended, scores, weights, keys, values, k_sem, v_sem = refs
    me = lax.axis_index("tensor")
    here, span, key_width = keys.shape
    kv_groups = key_width // HD
    parts = attended.shape[0]

    def key_copy(row):
        return pltpu.make_async_copy(keys_ref.at[row], keys.at[row], k_sem.at[row])

    def value_copy(row):
        return pltpu.make_async_copy(values_ref.at[row], values.at[row], v_sem.at[row])

    for row in range(here + 2):
        if row < here:
            key_copy(row).start()
        if row >= 2:
            value_copy(row - 2).start()

    for device in range(count):
        for part in range(parts + 1):
            queries[part, device * here : (device + 1) * here, :] = in_ref[
                device, :, part * HD : (part + 1) * HD
            ].astype(jnp.float32)
    mine = pl.ds(pl.multiple_of(me * here, here), here)
    cosine, sine = cosine_ref[mine, :], sine_ref[mine, :]
    shares = count // (2 * kv_groups)
    tiles = []
    for tile in range(2 * kv_groups):
        joined = jnp.zeros((here, HD), jnp.float32)
        for device in range(tile * shares, (tile + 1) * shares):
            joined = joined + queries[parts, device * here : (device + 1) * here, :]
        tiles.append(joined)
    new_keys = [rotate(tile, cosine, sine) for tile in tiles[:kv_groups]]
    new_keys = jnp.concatenate(new_keys, axis=1).astype(jnp.bfloat16).astype(jnp.float32)
    new_values = jnp.concatenate(tiles[kv_groups:], axis=1)

    shape = (parts * count, key_width)
    group_devices = count // kv_groups
    device = lax.rem(lax.broadcasted_iota(jnp.int32, shape, 0), count)
    column = lax.broadcasted_iota(jnp.int32, shape, 1)
    own_group = lax.div(device, group_devices) == lax.div(column, HD)
    token = lax.broadcasted_iota(jnp.int32, (1, span), 1)
    score_scale = HD ** (-0.5)
    own_scores, own_weights = {}, {}

    def score(row):
        heads = jnp.concatenate(
            [queries[part, pl.ds(row, count, stride=here), :] for part in range(parts)], axis=0
        )
        heads = jnp.where(own_group, jnp.concatenate([heads] * kv_groups, axis=1), 0.0)
        own_scores[row] = (
            jnp.sum(heads * new_keys[row : row + 1], axis=1, keepdims=True) * score_scale
        )
        scores[row % 2] = lax.dot_general(
            heads.astype(jnp.bfloat16),
            keys[row],
            (((1,), (1,)), ((), ())),
            preferred_element_type=jnp.float32,
        )

    def weigh(row):
        valid = token < lengths_ref[row]
        scaled = jnp.where(valid, scores[row % 2] * score_scale, -1e30)
        largest = jnp.maximum(jnp.max(scaled, axis=1, keepdims=True), own_scores[row])
        raised = jnp.exp(scaled - largest)
        own_raised = jnp.exp(own_scores[row] - largest)
        share = 1.0 / (jnp.sum(raised, axis=1, keepdims=True) + own_raised)
        weights[row % 2] = (raised * share).astype(jnp.bfloat16)
        own_weights[row] = (own_raised * share).astype(jnp.bfloat16).astype(jnp.float32)

    def mix(row):
        mixed = jnp.dot(weights[row % 2], values[row], preferred_element_type=jnp.float32)
        mixed = mixed + own_weights[row] * new_values[row : row + 1]
        mixed = jnp.where(own_group, mixed, 0.0)
        chosen = mixed[:, :HD]
        for group in range(1, kv_groups):
            chosen = chosen + mixed[:, group * HD : (group + 1) * HD]
        for part in range(parts):
            attended[part, pl.ds(row, count, stride=here), :] = chosen[
                part * count : (part + 1) * count
            ]

    for step in range(here + 2):
        if step < here:
            key_copy(step).wait()
        if step >= 2:
            value_copy(step - 2).wait()
        if step >= 2:
            mix(step - 2)
        if 1 <= step <= here:
            weigh(step - 1)
        if step < here:
            score(step)
    for k in range(count):
        for part in range(parts):
            out_ref[k, :, part * HD : (part + 1) * HD] = attended[
                part, k * here : (k + 1) * here, :
            ].astype(jnp.bfloat16)


def attend(blocks, lengths, cosine, sine, cache_keys, cache_values):
    count = blocks.shape[0]
    here, span, key_width = cache_keys.shape
    width = blocks.shape[2] - HD
    heads = count * width // HD
    vmem = pl.BlockSpec(memory_space=pltpu.VMEM)
    whole = pl.BlockSpec(memory_space=pl.ANY)
    return pl.pallas_call(
        functools.partial(attend_kernel, count),
        out_shape=jax.ShapeDtypeStruct((count, here, width), jnp.bfloat16),
        in_specs=[pl.BlockSpec(memory_space=pltpu.SMEM), vmem, vmem, whole, whole, vmem],
        out_specs=vmem,
        scratch_shapes=[
            pltpu.VMEM((width // HD + 1, here * count, HD), jnp.float32),
            pltpu.VMEM((width // HD, here * count, HD), jnp.float32),
            pltpu.VMEM((2, heads, span), jnp.float32),
            pltpu.VMEM((2, heads, span), jnp.bfloat16),
            pltpu.VMEM((here, span, key_width), jnp.bfloat16),
            pltpu.VMEM((here, span, key_width), jnp.bfloat16),
            pltpu.SemaphoreType.DMA((here,)),
            pltpu.SemaphoreType.DMA((here,)),
        ],
        compiler_params=pltpu.CompilerParams(vmem_limit_bytes=40 * 1024 * 1024),
        cost_estimate=pl.CostEstimate(
            flops=4 * here * count * width * span,
            bytes_accessed=4 * here * span * key_width,
            transcendentals=here * heads * span,
        ),
    )(lengths, cosine, sine, cache_keys, cache_values, blocks)


def exchange(blocks):
    return lax.all_to_all(blocks, "tensor", split_axis=0, concat_axis=0, tiled=True)


def plans(count):
    bits = list(range(1, count.bit_length() - 1))
    turned = bits[::-1]
    late = bits[1:2] + bits[:1] + bits[2:]
    return [(late, late[::-1]), (bits, turned), (bits, turned), (late, late[::-1])]


def timetable(count):
    if count == 16:
        return [int(c) for c in TABLE]
    steps = 2 * (count.bit_length() - 2) + 1
    return [s for _ in range(steps) for s in (1, 0, 2, 3)] + [1, 3]


def place(offset, order):
    spot = 0
    for bit in order:
        spot = spot * 2 + ((offset >> bit) & 1)
    return spot


def project_kernel(count, side, in_ref, w_ref, *refs):
    *set_refs, heads_buffer, w_buffer, arrived = refs
    me = lax.axis_index("tensor")
    width = w_buffer.shape[2]
    offsets = [k for k in range(count) if (k >> 1) % 2 == side]
    offsets = [k for k in offsets if k % 2] + [k for k in offsets if k % 2 == 0]
    copies = []
    for slot, offset in enumerate(offsets):
        column = pl.multiple_of(jnp.bitwise_xor(me, offset) * width, width)
        copies.append(
            pltpu.make_async_copy(
                w_ref.at[:, pl.ds(column, width)], w_buffer.at[slot], arrived.at[slot]
            )
        )
        copies[-1].start()
    here = in_ref.shape[1]
    for k in range(count):
        heads_buffer[k * here : (k + 1) * here, :] = in_ref[k].astype(jnp.float32)
    heads = heads_buffer[...].astype(jnp.bfloat16)
    for slot, offset in enumerate(offsets):
        copies[slot].wait()
        product = jnp.dot(heads, w_buffer[slot], preferred_element_type=jnp.float32).astype(
            jnp.bfloat16
        )
        start = 0
        for which, (order, _) in enumerate(plans(count)):
            ref = set_refs[2 * which + (1 - offset % 2)]
            spot = place(offset, [bit for bit in order if bit != 1])
            ref[spot] = product[start : start + ref.shape[1]]
            start += ref.shape[1]


def project(blocks, w_out, side):
    count, here, depth = blocks.shape
    rows = count * here
    width = w_out.shape[1] // count
    sets = len(plans(count))
    share = jax.ShapeDtypeStruct((count // 4, rows // sets, width), jnp.bfloat16)
    outs = pl.pallas_call(
        functools.partial(project_kernel, count, side),
        out_shape=(share,) * (2 * sets),
        in_specs=[pl.BlockSpec(memory_space=pltpu.VMEM), pl.BlockSpec(memory_space=pl.ANY)],
        out_specs=(pl.BlockSpec(memory_space=pltpu.VMEM),) * (2 * sets),
        scratch_shapes=[
            pltpu.VMEM((rows, depth), jnp.float32),
            pltpu.VMEM((count // 2, depth, width), jnp.bfloat16),
            pltpu.SemaphoreType.DMA((count // 2,)),
        ],
        compiler_params=pltpu.CompilerParams(vmem_limit_bytes=48 * 1024 * 1024),
        cost_estimate=pl.CostEstimate(
            flops=rows * depth * width * count,
            bytes_accessed=(depth + rows) * width * count,
            transcendentals=0,
        ),
    )(blocks, w_out)
    return outs[0::2], outs[1::2]


def finish_kernel(offsets, gain_ref, *refs):
    out_ref = refs[-1]
    me = lax.axis_index("tensor")
    half, rows, width = refs[0].shape
    for k, order in enumerate(offsets):
        parts = refs[2 * k : 2 * k + 2]
        total = jnp.zeros((rows, width), jnp.float32)
        for ref in parts:
            for spot in range(half):
                block = ref[spot].astype(jnp.float32)
                total = total + block * block
        mean_square = jnp.sum(total, axis=1, keepdims=True) / (2 * half * width)
        scale = lax.rsqrt(mean_square + epsilon)
        for spot, offset in enumerate(order):
            block = parts[spot // half][spot % half].astype(jnp.float32)
            index = jnp.bitwise_xor(me, offset)
            column = pl.multiple_of(index * width, width)
            gain = gain_ref[pl.ds(index, 1), :]
            out_ref[k * rows : (k + 1) * rows, pl.ds(column, width)] = (
                block * scale * gain
            ).astype(jnp.bfloat16)


def finish(parts, gain, offsets, which, groups, earlier):
    half, rows, width = parts[0].shape
    columns, rows = 2 * half * width, rows * len(offsets)
    operands = [gain, *parts] + ([] if earlier is None else [earlier])
    specs = [pl.BlockSpec(memory_space=pltpu.VMEM)] * (1 + len(parts))
    if earlier is not None:
        specs.append(pl.BlockSpec(memory_space=pl.ANY))
    return pl.pallas_call(
        functools.partial(finish_kernel, offsets),
        grid=(1,),
        out_shape=jax.ShapeDtypeStruct((rows * groups, columns), jnp.bfloat16),
        in_specs=specs,
        out_specs=pl.BlockSpec((rows, columns), lambda i: (which, 0)),
        input_output_aliases={} if earlier is None else {len(operands) - 1: 0},
        compiler_params=pltpu.CompilerParams(vmem_limit_bytes=24 * 1024 * 1024),
        cost_estimate=pl.CostEstimate(
            flops=6 * rows * columns, bytes_accessed=4 * rows * columns, transcendentals=0
        ),
    )(*operands)


def swap(values, bit, count):
    return lax.ppermute(values, "tensor", [(i, i ^ (1 << bit)) for i in range(count)])


def add(one, other):
    return (one.astype(jnp.float32) + other.astype(jnp.float32)).astype(jnp.bfloat16)


def halves(keep, arrival):
    half = keep.shape[0] // 2
    return add(keep[:half], arrival[:half]), add(keep[half:], arrival[half:])


def on_device(
    hidden_in,
    attn_gain,
    w_query,
    w_keyval,
    cache_keys,
    cache_values,
    w_out,
    ffn_gain,
    lengths,
    positions,
):
    row_count = hidden_in.shape[0]
    count = lax.axis_size("tensor")
    cosine, sine = turns(positions)
    blocks, mine = project_in(hidden_in, attn_gain, w_query, w_keyval, cosine, sine, count)
    head_blocks = exchange(
        attend(exchange(blocks), lengths, cosine, sine, cache_keys, cache_values)
    )
    share_width = w_out.shape[1] // count
    gain = ffn_gain.astype(jnp.float32).reshape(count, share_width)
    orders = plans(count)
    sets = len(orders)
    set_rows = row_count // sets

    def core_sums(heads, side):
        sent, kept = project(heads, w_out, side)
        arrivals = [swap(block, 0, count) for block in sent]
        return [add(keep, arrival) for keep, arrival in zip(kept, arrivals)]

    far = core_sums(head_blocks, 1)
    first = timetable(count)[0]
    gate, far[first] = lax.optimization_barrier((head_blocks, far[first]))
    near = core_sums(gate, 0)
    held, leaving = [], []
    for k in range(sets):
        if orders[k][0][0] == 1:
            held.append(near[k])
            leaving.append(far[k])
        else:
            half = far[k].shape[0] // 2
            held.append(jnp.concatenate([near[k][:half], far[k][:half]], axis=0))
            leaving.append(jnp.concatenate([near[k][half:], far[k][half:]], axis=0))
    streams = [None] * sets
    offsets = [[0] for _ in range(sets)]
    steps = [0] * sets
    last = normed = None
    arrivals = [None] * sets
    for k in timetable(count):
        scatter, gather = orders[k]
        step = steps[k]
        steps[k] += 1
        if step == 0:
            if last is None:
                last = leaving[k]
            else:
                last, _ = lax.optimization_barrier((leaving[k], last))
            arrivals[k] = swap(last, scatter[0], count)
            continue
        held[k], arrivals[k], _ = lax.optimization_barrier((held[k], arrivals[k], last))
        if step < len(scatter):
            held[k], last = halves(held[k], arrivals[k])
            arrivals[k] = swap(last, scatter[step], count)
            continue
        if step == len(scatter):
            own_rows = mine[k * set_rows : (k + 1) * set_rows].astype(jnp.float32)
            total = held[k][0].astype(jnp.float32) + arrivals[k][0].astype(jnp.float32)
            streams[k] = (own_rows + total).astype(jnp.bfloat16)
            last = held[k] = streams[k][None]
        elif step <= len(scatter) + len(gather):
            last = held[k] = jnp.concatenate([held[k], arrivals[k]], axis=0)
        else:
            pair = [k - 1, k]
            parts = [block for m in pair for block in (held[m], arrivals[m])]
            lists = [offsets[m] for m in pair]
            last = normed = finish(parts, gain, lists, k // 2, sets // 2, normed)
            continue
        bit = (gather + [0])[step - len(scatter)]
        arrivals[k] = swap(held[k], bit, count)
        offsets[k] = offsets[k] + [offset ^ (1 << bit) for offset in offsets[k]]
    return (jnp.concatenate(streams, axis=0), normed)


def solution(mesh):
    placed = (
        P("groups", None),
        P(),
        P(None, "tensor"),
        P(None, "tensor"),
        P(("groups", "tensor"), None, None),
        P(("groups", "tensor"), None, None),
        P("tensor", None),
        P(),
        P(("groups", "tensor")),
        P("groups"),
    )
    return jax.shard_map(
        on_device,
        mesh=mesh,
        in_specs=placed,
        out_specs=(P("groups", "tensor"), P("groups", None)),
        check_vma=False,
    )
```

```python
import functools
import math

import jax
import jax.numpy as jnp
from jax import lax
from jax.experimental import pallas as pl
from jax.experimental.pallas import tpu as pltpu
from jax.sharding import PartitionSpec as P

HD = 128


TABLE = "032031032013021320123121302131"

epsilon = 1e-05
rope_theta = 500000.0


def turns(positions):
    half = HD // 2
    entry = jnp.arange(HD, dtype=jnp.int32)
    frequency = jnp.exp((entry % half).astype(jnp.float32) * (-math.log(rope_theta) / half))
    angles = positions.astype(jnp.float32)[:, None] * frequency[None, :]
    sign = jnp.where(entry < half, -1.0, 1.0)
    return jnp.cos(angles), jnp.sin(angles) * sign


def rotate(head, cosine, sine):
    return head * cosine + pltpu.roll(head, HD // 2, 1) * sine


def input_kernel(count, hidden_ref, gain_ref, w_ref, kv_ref, cosine_ref, sine_ref, *refs):
    out_ref, mine_ref, hidden, gain_buffer, w_buffer, kv_buffer, normed, products, kv_products, *sems = refs
    h_sem, w_sem, kv_sem, mine_sem, gain_sem = sems
    me = lax.axis_index("tensor")
    rows, columns = hidden.shape
    depth = normed.shape[2]
    chunks = columns // depth
    width = products.shape[1]
    kv_width = kv_products.shape[1]
    here = rows // count

    def span(k):
        return pl.ds(k * depth, depth)

    def hidden_copy(k):
        return pltpu.make_async_copy(
            hidden_ref.at[:, span(k)], hidden.at[:, span(k)], h_sem.at[k]
        )

    def w_copy(k):
        return pltpu.make_async_copy(w_ref.at[span(k), :], w_buffer.at[span(k), :], w_sem.at[k])

    for k in range(chunks):
        hidden_copy(k).start()
    gain_copy = pltpu.make_async_copy(gain_ref, gain_buffer, gain_sem)
    gain_copy.start()
    kv_copy = pltpu.make_async_copy(kv_ref, kv_buffer, kv_sem)
    own = pl.ds(pl.multiple_of(me * (columns // count), columns // count), columns // count)
    mine_copy = pltpu.make_async_copy(hidden_ref.at[:, own], mine_ref, mine_sem)
    products[...] = jnp.zeros_like(products)
    kv_products[...] = jnp.zeros_like(kv_products)
    total = jnp.zeros((rows, 128), jnp.float32)
    for k in range(chunks):
        hidden_copy(k).wait()
        w_copy(k).start()
        if k == 0:
            kv_copy.start()
        for lane in range(k * depth, (k + 1) * depth, 128):
            part = hidden[:, lane : lane + 128].astype(jnp.float32)
            total = total + part * part
    mine_copy.start()
    scale = lax.rsqrt(jnp.sum(total, axis=1, keepdims=True) / columns + epsilon)

    def norm(k):
        floats = hidden[:, span(k)].astype(jnp.float32)
        gain = gain_buffer[span(k)].astype(jnp.float32).reshape(1, depth)
        normed[k % 2] = (floats * scale * gain).astype(jnp.bfloat16)

    gain_copy.wait()
    norm(0)
    kv_copy.wait()
    for k in range(chunks):
        w_copy(k).wait()
        products[...] += jnp.dot(
            normed[k % 2], w_buffer[span(k), :], preferred_element_type=jnp.float32
        )
        kv_products[...] += lax.dot_general(
            normed[k % 2],
            kv_buffer[:, span(k)],
            (((1,), (1,)), ((), ())),
            preferred_element_type=jnp.float32,
        )
        if k + 1 < chunks:
            norm(k + 1)

    shift = lax.rem(me, HD // kv_width) * kv_width
    blank = jnp.zeros((rows, HD - kv_width), jnp.float32)
    moved = pltpu.roll(jnp.concatenate([kv_products[...], blank], axis=1), shift, 1)
    results = [
        rotate(products[:, start : start + HD], cosine_ref[...], sine_ref[...])
        for start in range(0, width, HD)
    ] + [moved]
    for part, result in enumerate(results):
        for k in range(count):
            out_ref[k, :, part * HD : (part + 1) * HD] = result[
                k * here : (k + 1) * here
            ].astype(jnp.bfloat16)
    mine_copy.wait()


def project_in(hidden_in, gain, w_query, w_keyval, cosine, sine, count):
    rows, columns = hidden_in.shape
    width, kv_width = w_query.shape[1], w_keyval.shape[1]
    depth = columns // 8
    chunks = columns // depth
    vmem = pl.BlockSpec(memory_space=pltpu.VMEM)
    whole = pl.BlockSpec(memory_space=pl.ANY)
    return pl.pallas_call(
        functools.partial(input_kernel, count),
        out_shape=(
            jax.ShapeDtypeStruct((count, rows // count, width + HD), jnp.bfloat16),
            jax.ShapeDtypeStruct((rows, columns // count), jnp.bfloat16),
        ),
        in_specs=[whole, whole, whole, whole, vmem, vmem],
        out_specs=(vmem, vmem),
        scratch_shapes=[
            pltpu.VMEM((rows, columns), jnp.bfloat16),
            pltpu.VMEM((columns,), jnp.bfloat16),
            pltpu.VMEM((columns, width), jnp.bfloat16),
            pltpu.VMEM((kv_width, columns), jnp.bfloat16),
            pltpu.VMEM((2, rows, depth), jnp.bfloat16),
            pltpu.VMEM((rows, width), jnp.float32),
            pltpu.VMEM((rows, kv_width), jnp.float32),
            pltpu.SemaphoreType.DMA((chunks,)),
            pltpu.SemaphoreType.DMA((chunks,)),
            pltpu.SemaphoreType.DMA,
            pltpu.SemaphoreType.DMA,
            pltpu.SemaphoreType.DMA,
        ],
        compiler_params=pltpu.CompilerParams(vmem_limit_bytes=52 * 1024 * 1024),
        cost_estimate=pl.CostEstimate(
            flops=2 * rows * columns * (width + kv_width),
            bytes_accessed=2 * columns * (rows + width + kv_width),
            transcendentals=0,
        ),
    )(hidden_in, gain, w_query, w_keyval.T, cosine, sine)


def attend_kernel(count, lengths_ref, cosine_ref, sine_ref, keys_ref, values_ref, *refs):
    in_ref, out_ref, queries, attended, scores, weights, keys, values, k_sem, v_sem = refs
    me = lax.axis_index("tensor")
    here, span, key_width = keys.shape
    kv_groups = key_width // HD
    parts = attended.shape[0]

    def key_copy(row):
        return pltpu.make_async_copy(keys_ref.at[row], keys.at[row], k_sem.at[row])

    def value_copy(row):
        return pltpu.make_async_copy(values_ref.at[row], values.at[row], v_sem.at[row])

    for row in range(here + 2):
        if row < here:
            key_copy(row).start()
        if row >= 2:
            value_copy(row - 2).start()

    for device in range(count):
        for part in range(parts + 1):
            queries[part, device * here : (device + 1) * here, :] = in_ref[
                device, :, part * HD : (part + 1) * HD
            ].astype(jnp.float32)
    mine = pl.ds(pl.multiple_of(me * here, here), here)
    cosine, sine = cosine_ref[mine, :], sine_ref[mine, :]
    shares = count // (2 * kv_groups)
    tiles = []
    for tile in range(2 * kv_groups):
        joined = jnp.zeros((here, HD), jnp.float32)
        for device in range(tile * shares, (tile + 1) * shares):
            joined = joined + queries[parts, device * here : (device + 1) * here, :]
        tiles.append(joined)
    new_keys = [rotate(tile, cosine, sine) for tile in tiles[:kv_groups]]
    new_keys = jnp.concatenate(new_keys, axis=1).astype(jnp.bfloat16).astype(jnp.float32)
    new_values = jnp.concatenate(tiles[kv_groups:], axis=1)

    shape = (parts * count, key_width)
    group_devices = count // kv_groups
    device = lax.rem(lax.broadcasted_iota(jnp.int32, shape, 0), count)
    column = lax.broadcasted_iota(jnp.int32, shape, 1)
    own_group = lax.div(device, group_devices) == lax.div(column, HD)
    token = lax.broadcasted_iota(jnp.int32, (1, span), 1)
    score_scale = HD ** (-0.5)
    own_scores, own_weights = {}, {}

    def score(row):
        heads = jnp.concatenate(
            [queries[part, pl.ds(row, count, stride=here), :] for part in range(parts)], axis=0
        )
        heads = jnp.where(own_group, jnp.concatenate([heads] * kv_groups, axis=1), 0.0)
        own_scores[row] = (
            jnp.sum(heads * new_keys[row : row + 1], axis=1, keepdims=True) * score_scale
        )
        scores[row % 2] = lax.dot_general(
            heads.astype(jnp.bfloat16),
            keys[row],
            (((1,), (1,)), ((), ())),
            preferred_element_type=jnp.float32,
        )

    def weigh(row):
        valid = token < lengths_ref[row]
        scaled = jnp.where(valid, scores[row % 2] * score_scale, -1e30)
        largest = jnp.maximum(jnp.max(scaled, axis=1, keepdims=True), own_scores[row])
        raised = jnp.exp(scaled - largest)
        own_raised = jnp.exp(own_scores[row] - largest)
        share = 1.0 / (jnp.sum(raised, axis=1, keepdims=True) + own_raised)
        weights[row % 2] = (raised * share).astype(jnp.bfloat16)
        own_weights[row] = (own_raised * share).astype(jnp.bfloat16).astype(jnp.float32)

    def mix(row):
        mixed = jnp.dot(weights[row % 2], values[row], preferred_element_type=jnp.float32)
        mixed = mixed + own_weights[row] * new_values[row : row + 1]
        mixed = jnp.where(own_group, mixed, 0.0)
        chosen = mixed[:, :HD]
        for group in range(1, kv_groups):
            chosen = chosen + mixed[:, group * HD : (group + 1) * HD]
        for part in range(parts):
            attended[part, pl.ds(row, count, stride=here), :] = chosen[
                part * count : (part + 1) * count
            ]

    for step in range(here + 2):
        if step < here:
            key_copy(step).wait()
        if step >= 2:
            value_copy(step - 2).wait()
        if step >= 2:
            mix(step - 2)
        if 1 <= step <= here:
            weigh(step - 1)
        if step < here:
            score(step)
    for k in range(count):
        for part in range(parts):
            out_ref[k, :, part * HD : (part + 1) * HD] = attended[
                part, k * here : (k + 1) * here, :
            ].astype(jnp.bfloat16)


def attend(blocks, lengths, cosine, sine, cache_keys, cache_values):
    count = blocks.shape[0]
    here, span, key_width = cache_keys.shape
    width = blocks.shape[2] - HD
    heads = count * width // HD
    vmem = pl.BlockSpec(memory_space=pltpu.VMEM)
    whole = pl.BlockSpec(memory_space=pl.ANY)
    return pl.pallas_call(
        functools.partial(attend_kernel, count),
        out_shape=jax.ShapeDtypeStruct((count, here, width), jnp.bfloat16),
        in_specs=[pl.BlockSpec(memory_space=pltpu.SMEM), vmem, vmem, whole, whole, vmem],
        out_specs=vmem,
        scratch_shapes=[
            pltpu.VMEM((width // HD + 1, here * count, HD), jnp.float32),
            pltpu.VMEM((width // HD, here * count, HD), jnp.float32),
            pltpu.VMEM((2, heads, span), jnp.float32),
            pltpu.VMEM((2, heads, span), jnp.bfloat16),
            pltpu.VMEM((here, span, key_width), jnp.bfloat16),
            pltpu.VMEM((here, span, key_width), jnp.bfloat16),
            pltpu.SemaphoreType.DMA((here,)),
            pltpu.SemaphoreType.DMA((here,)),
        ],
        compiler_params=pltpu.CompilerParams(vmem_limit_bytes=40 * 1024 * 1024),
        cost_estimate=pl.CostEstimate(
            flops=4 * here * count * width * span,
            bytes_accessed=4 * here * span * key_width,
            transcendentals=here * heads * span,
        ),
    )(lengths, cosine, sine, cache_keys, cache_values, blocks)


def exchange(blocks):
    return lax.all_to_all(blocks, "tensor", split_axis=0, concat_axis=0, tiled=True)


def plans(count):
    bits = list(range(1, count.bit_length() - 1))
    turned = bits[::-1]
    late = bits[1:2] + bits[:1] + bits[2:]
    crossed = late[::-1]
    return [(bits, turned), (bits, crossed), (late, turned), (bits, crossed)]


def timetable(count):
    if count == 16:
        return [int(c) for c in TABLE]
    steps = 2 * (count.bit_length() - 2) + 1
    return [s for _ in range(steps) for s in (1, 0, 2, 3)] + [1, 3]


def place(offset, order):
    spot = 0
    for bit in order:
        spot = spot * 2 + ((offset >> bit) & 1)
    return spot


def project_kernel(count, side, in_ref, w_ref, *refs):
    *set_refs, heads_buffer, w_buffer, arrived = refs
    me = lax.axis_index("tensor")
    width = w_buffer.shape[2]
    offsets = [k for k in range(count) if (k >> 1) % 2 == side]
    offsets = [k for k in offsets if k % 2] + [k for k in offsets if k % 2 == 0]
    copies = []
    for slot, offset in enumerate(offsets):
        column = pl.multiple_of(jnp.bitwise_xor(me, offset) * width, width)
        copies.append(
            pltpu.make_async_copy(
                w_ref.at[:, pl.ds(column, width)], w_buffer.at[slot], arrived.at[slot]
            )
        )
        copies[-1].start()
    here = in_ref.shape[1]
    for k in range(count):
        heads_buffer[k * here : (k + 1) * here, :] = in_ref[k].astype(jnp.float32)
    heads = heads_buffer[...].astype(jnp.bfloat16)
    for slot, offset in enumerate(offsets):
        copies[slot].wait()
        product = jnp.dot(heads, w_buffer[slot], preferred_element_type=jnp.float32).astype(
            jnp.bfloat16
        )
        start = 0
        for which, (order, _) in enumerate(plans(count)):
            ref = set_refs[2 * which + (1 - offset % 2)]
            spot = place(offset, [bit for bit in order if bit != 1])
            ref[spot] = product[start : start + ref.shape[1]]
            start += ref.shape[1]


def project(blocks, w_out, side):
    count, here, depth = blocks.shape
    rows = count * here
    width = w_out.shape[1] // count
    sets = len(plans(count))
    share = jax.ShapeDtypeStruct((count // 4, rows // sets, width), jnp.bfloat16)
    outs = pl.pallas_call(
        functools.partial(project_kernel, count, side),
        out_shape=(share,) * (2 * sets),
        in_specs=[pl.BlockSpec(memory_space=pltpu.VMEM), pl.BlockSpec(memory_space=pl.ANY)],
        out_specs=(pl.BlockSpec(memory_space=pltpu.VMEM),) * (2 * sets),
        scratch_shapes=[
            pltpu.VMEM((rows, depth), jnp.float32),
            pltpu.VMEM((count // 2, depth, width), jnp.bfloat16),
            pltpu.SemaphoreType.DMA((count // 2,)),
        ],
        compiler_params=pltpu.CompilerParams(vmem_limit_bytes=48 * 1024 * 1024),
        cost_estimate=pl.CostEstimate(
            flops=rows * depth * width * count,
            bytes_accessed=(depth + rows) * width * count,
            transcendentals=0,
        ),
    )(blocks, w_out)
    return outs[0::2], outs[1::2]


def finish_kernel(offsets, gain_ref, *refs):
    out_ref = refs[-1]
    me = lax.axis_index("tensor")
    half, rows, width = refs[0].shape

    def norm(k, order):
        parts = refs[2 * k : 2 * k + 2]
        total = jnp.zeros((rows, width), jnp.float32)
        for ref in parts:
            for spot in range(half):
                block = ref[spot].astype(jnp.float32)
                total = total + block * block
        mean_square = jnp.sum(total, axis=1, keepdims=True) / (2 * half * width)
        scale = lax.rsqrt(mean_square + epsilon)
        for spot, offset in enumerate(order):
            block = parts[spot // half][spot % half].astype(jnp.float32)
            index = jnp.bitwise_xor(me, offset)
            column = pl.multiple_of(index * width, width)
            gain = gain_ref[pl.ds(index, 1), :]
            out_ref[:, pl.ds(column, width)] = (block * scale * gain).astype(jnp.bfloat16)

    for k, order in enumerate(offsets):
        pl.when(pl.program_id(0) == k)(functools.partial(norm, k, order))


def finish(parts, gain, offsets, which, groups, earlier):
    half, rows, width = parts[0].shape
    columns, count = 2 * half * width, len(offsets)
    operands = [gain, *parts] + ([] if earlier is None else [earlier])
    specs = [pl.BlockSpec(memory_space=pltpu.VMEM)] * (1 + len(parts))
    if earlier is not None:
        specs.append(pl.BlockSpec(memory_space=pl.ANY))
    return pl.pallas_call(
        functools.partial(finish_kernel, offsets),
        grid=(count,),
        out_shape=jax.ShapeDtypeStruct((rows * count * groups, columns), jnp.bfloat16),
        in_specs=specs,
        out_specs=pl.BlockSpec((rows, columns), lambda i: (which * count + i, 0)),
        input_output_aliases={} if earlier is None else {len(operands) - 1: 0},
        compiler_params=pltpu.CompilerParams(vmem_limit_bytes=24 * 1024 * 1024),
        cost_estimate=pl.CostEstimate(
            flops=6 * count * rows * columns,
            bytes_accessed=4 * count * rows * columns,
            transcendentals=0,
        ),
    )(*operands)


def swap(values, bit, count):
    return lax.ppermute(values, "tensor", [(i, i ^ (1 << bit)) for i in range(count)])


def add(one, other):
    return (one.astype(jnp.float32) + other.astype(jnp.float32)).astype(jnp.bfloat16)


def halves(keep, arrival):
    half = keep.shape[0] // 2
    return add(keep[:half], arrival[:half]), add(keep[half:], arrival[half:])


def on_device(
    hidden_in,
    attn_gain,
    w_query,
    w_keyval,
    cache_keys,
    cache_values,
    w_out,
    ffn_gain,
    lengths,
    positions,
):
    row_count = hidden_in.shape[0]
    count = lax.axis_size("tensor")
    cosine, sine = turns(positions)
    blocks, mine = project_in(hidden_in, attn_gain, w_query, w_keyval, cosine, sine, count)
    head_blocks = exchange(
        attend(exchange(blocks), lengths, cosine, sine, cache_keys, cache_values)
    )
    share_width = w_out.shape[1] // count
    gain = ffn_gain.astype(jnp.float32).reshape(count, share_width)
    orders = plans(count)
    sets = len(orders)
    set_rows = row_count // sets

    def core_sums(heads, side):
        sent, kept = project(heads, w_out, side)
        arrivals = [swap(block, 0, count) for block in sent]
        return [add(keep, arrival) for keep, arrival in zip(kept, arrivals)]

    far = core_sums(head_blocks, 1)
    first = timetable(count)[0]
    gate, far[first] = lax.optimization_barrier((head_blocks, far[first]))
    near = core_sums(gate, 0)
    held, leaving = [], []
    for k in range(sets):
        if orders[k][0][0] == 1:
            held.append(near[k])
            leaving.append(far[k])
        else:
            half = far[k].shape[0] // 2
            held.append(jnp.concatenate([near[k][:half], far[k][:half]], axis=0))
            leaving.append(jnp.concatenate([near[k][half:], far[k][half:]], axis=0))
    streams = [None] * sets
    offsets = [[0] for _ in range(sets)]
    steps = [0] * sets
    last = normed = None
    arrivals = [None] * sets
    for k in timetable(count):
        scatter, gather = orders[k]
        step = steps[k]
        steps[k] += 1
        if step == 0:
            if last is None:
                last = leaving[k]
            else:
                last, _ = lax.optimization_barrier((leaving[k], last))
            arrivals[k] = swap(last, scatter[0], count)
            continue
        held[k], arrivals[k], _ = lax.optimization_barrier((held[k], arrivals[k], last))
        if step < len(scatter):
            held[k], last = halves(held[k], arrivals[k])
            arrivals[k] = swap(last, scatter[step], count)
            continue
        if step == len(scatter):
            own_rows = mine[k * set_rows : (k + 1) * set_rows].astype(jnp.float32)
            total = held[k][0].astype(jnp.float32) + arrivals[k][0].astype(jnp.float32)
            streams[k] = (own_rows + total).astype(jnp.bfloat16)
            last = held[k] = streams[k][None]
        elif step <= len(scatter) + len(gather):
            last = held[k] = jnp.concatenate([held[k], arrivals[k]], axis=0)
        else:
            pair = [k - 1, k]
            parts = [block for m in pair for block in (held[m], arrivals[m])]
            lists = [offsets[m] for m in pair]
            last = normed = finish(parts, gain, lists, k // 2, sets // 2, normed)
            continue
        bit = (gather + [0])[step - len(scatter)]
        arrivals[k] = swap(held[k], bit, count)
        offsets[k] = offsets[k] + [offset ^ (1 << bit) for offset in offsets[k]]
    return (jnp.concatenate(streams, axis=0), normed)


def solution(mesh):
    placed = (
        P("groups", None),
        P(),
        P(None, "tensor"),
        P(None, "tensor"),
        P(("groups", "tensor"), None, None),
        P(("groups", "tensor"), None, None),
        P("tensor", None),
        P(),
        P(("groups", "tensor")),
        P("groups"),
    )
    return jax.shard_map(
        on_device,
        mesh=mesh,
        in_specs=placed,
        out_specs=(P("groups", "tensor"), P("groups", None)),
        check_vma=False,
    )
```

```python
import functools
import math

import jax
import jax.numpy as jnp
from jax import lax
from jax.experimental import pallas as pl
from jax.experimental.pallas import tpu as pltpu
from jax.sharding import PartitionSpec as P

HD = 128


TABLE = "03203103201302312012312130320121"

epsilon = 1e-05
rope_theta = 500000.0


def turns(positions):
    half = HD // 2
    entry = jnp.arange(HD, dtype=jnp.int32)
    frequency = jnp.exp((entry % half).astype(jnp.float32) * (-math.log(rope_theta) / half))
    angles = positions.astype(jnp.float32)[:, None] * frequency[None, :]
    sign = jnp.where(entry < half, -1.0, 1.0)
    return jnp.cos(angles), jnp.sin(angles) * sign


def rotate(head, cosine, sine):
    return head * cosine + pltpu.roll(head, HD // 2, 1) * sine


def input_kernel(count, hidden_ref, gain_ref, w_ref, kv_ref, cosine_ref, sine_ref, *refs):
    out_ref, mine_ref, hidden, gain_buffer, w_buffer, kv_buffer, normed, products, kv_products, *sems = refs
    h_sem, w_sem, kv_sem, mine_sem, gain_sem = sems
    me = lax.axis_index("tensor")
    rows, columns = hidden.shape
    depth = normed.shape[2]
    chunks = columns // depth
    width = products.shape[1]
    kv_width = kv_products.shape[1]
    here = rows // count

    def span(k):
        return pl.ds(k * depth, depth)

    def hidden_copy(k):
        return pltpu.make_async_copy(
            hidden_ref.at[:, span(k)], hidden.at[:, span(k)], h_sem.at[k]
        )

    def w_copy(k):
        return pltpu.make_async_copy(w_ref.at[span(k), :], w_buffer.at[span(k), :], w_sem.at[k])

    for k in range(chunks):
        hidden_copy(k).start()
    gain_copy = pltpu.make_async_copy(gain_ref, gain_buffer, gain_sem)
    gain_copy.start()
    kv_copy = pltpu.make_async_copy(kv_ref, kv_buffer, kv_sem)
    own = pl.ds(pl.multiple_of(me * (columns // count), columns // count), columns // count)
    mine_copy = pltpu.make_async_copy(hidden_ref.at[:, own], mine_ref, mine_sem)
    products[...] = jnp.zeros_like(products)
    kv_products[...] = jnp.zeros_like(kv_products)
    total = jnp.zeros((rows, 128), jnp.float32)
    for k in range(chunks):
        hidden_copy(k).wait()
        w_copy(k).start()
        if k == 0:
            kv_copy.start()
        for lane in range(k * depth, (k + 1) * depth, 128):
            part = hidden[:, lane : lane + 128].astype(jnp.float32)
            total = total + part * part
    mine_copy.start()
    scale = lax.rsqrt(jnp.sum(total, axis=1, keepdims=True) / columns + epsilon)

    def norm(k):
        floats = hidden[:, span(k)].astype(jnp.float32)
        gain = gain_buffer[span(k)].astype(jnp.float32).reshape(1, depth)
        normed[k % 2] = (floats * scale * gain).astype(jnp.bfloat16)

    gain_copy.wait()
    norm(0)
    kv_copy.wait()
    for k in range(chunks):
        w_copy(k).wait()
        products[...] += jnp.dot(
            normed[k % 2], w_buffer[span(k), :], preferred_element_type=jnp.float32
        )
        kv_products[...] += lax.dot_general(
            normed[k % 2],
            kv_buffer[:, span(k)],
            (((1,), (1,)), ((), ())),
            preferred_element_type=jnp.float32,
        )
        if k + 1 < chunks:
            norm(k + 1)

    shift = lax.rem(me, HD // kv_width) * kv_width
    blank = jnp.zeros((rows, HD - kv_width), jnp.float32)
    moved = pltpu.roll(jnp.concatenate([kv_products[...], blank], axis=1), shift, 1)
    results = [
        rotate(products[:, start : start + HD], cosine_ref[...], sine_ref[...])
        for start in range(0, width, HD)
    ] + [moved]
    for part, result in enumerate(results):
        for k in range(count):
            out_ref[k, :, part * HD : (part + 1) * HD] = result[
                k * here : (k + 1) * here
            ].astype(jnp.bfloat16)
    mine_copy.wait()


def project_in(hidden_in, gain, w_query, w_keyval, cosine, sine, count):
    rows, columns = hidden_in.shape
    width, kv_width = w_query.shape[1], w_keyval.shape[1]
    depth = columns // 8
    chunks = columns // depth
    vmem = pl.BlockSpec(memory_space=pltpu.VMEM)
    whole = pl.BlockSpec(memory_space=pl.ANY)
    return pl.pallas_call(
        functools.partial(input_kernel, count),
        out_shape=(
            jax.ShapeDtypeStruct((count, rows // count, width + HD), jnp.bfloat16),
            jax.ShapeDtypeStruct((rows, columns // count), jnp.bfloat16),
        ),
        in_specs=[whole, whole, whole, whole, vmem, vmem],
        out_specs=(vmem, vmem),
        scratch_shapes=[
            pltpu.VMEM((rows, columns), jnp.bfloat16),
            pltpu.VMEM((columns,), jnp.bfloat16),
            pltpu.VMEM((columns, width), jnp.bfloat16),
            pltpu.VMEM((kv_width, columns), jnp.bfloat16),
            pltpu.VMEM((2, rows, depth), jnp.bfloat16),
            pltpu.VMEM((rows, width), jnp.float32),
            pltpu.VMEM((rows, kv_width), jnp.float32),
            pltpu.SemaphoreType.DMA((chunks,)),
            pltpu.SemaphoreType.DMA((chunks,)),
            pltpu.SemaphoreType.DMA,
            pltpu.SemaphoreType.DMA,
            pltpu.SemaphoreType.DMA,
        ],
        compiler_params=pltpu.CompilerParams(vmem_limit_bytes=52 * 1024 * 1024),
        cost_estimate=pl.CostEstimate(
            flops=2 * rows * columns * (width + kv_width),
            bytes_accessed=2 * columns * (rows + width + kv_width),
            transcendentals=0,
        ),
    )(hidden_in, gain, w_query, w_keyval.T, cosine, sine)


def attend_kernel(count, lengths_ref, cosine_ref, sine_ref, keys_ref, values_ref, *refs):
    in_ref, out_ref, queries, attended, scores, weights, keys, values, k_sem, v_sem = refs
    me = lax.axis_index("tensor")
    here, span, key_width = keys.shape
    kv_groups = key_width // HD
    parts = attended.shape[0]

    def key_copy(row):
        return pltpu.make_async_copy(keys_ref.at[row], keys.at[row], k_sem.at[row])

    def value_copy(row):
        return pltpu.make_async_copy(values_ref.at[row], values.at[row], v_sem.at[row])

    for row in range(here + 2):
        if row < here:
            key_copy(row).start()
        if row >= 2:
            value_copy(row - 2).start()

    for device in range(count):
        for part in range(parts + 1):
            queries[part, device * here : (device + 1) * here, :] = in_ref[
                device, :, part * HD : (part + 1) * HD
            ].astype(jnp.float32)
    mine = pl.ds(pl.multiple_of(me * here, here), here)
    cosine, sine = cosine_ref[mine, :], sine_ref[mine, :]
    shares = count // (2 * kv_groups)
    tiles = []
    for tile in range(2 * kv_groups):
        joined = jnp.zeros((here, HD), jnp.float32)
        for device in range(tile * shares, (tile + 1) * shares):
            joined = joined + queries[parts, device * here : (device + 1) * here, :]
        tiles.append(joined)
    new_keys = [rotate(tile, cosine, sine) for tile in tiles[:kv_groups]]
    new_keys = jnp.concatenate(new_keys, axis=1).astype(jnp.bfloat16).astype(jnp.float32)
    new_values = jnp.concatenate(tiles[kv_groups:], axis=1)

    shape = (parts * count, key_width)
    group_devices = count // kv_groups
    device = lax.rem(lax.broadcasted_iota(jnp.int32, shape, 0), count)
    column = lax.broadcasted_iota(jnp.int32, shape, 1)
    own_group = lax.div(device, group_devices) == lax.div(column, HD)
    token = lax.broadcasted_iota(jnp.int32, (1, span), 1)
    score_scale = HD ** (-0.5)
    own_scores, own_weights = {}, {}

    def score(row):
        heads = jnp.concatenate(
            [queries[part, pl.ds(row, count, stride=here), :] for part in range(parts)], axis=0
        )
        heads = jnp.where(own_group, jnp.concatenate([heads] * kv_groups, axis=1), 0.0)
        own_scores[row] = (
            jnp.sum(heads * new_keys[row : row + 1], axis=1, keepdims=True) * score_scale
        )
        scores[row % 2] = lax.dot_general(
            heads.astype(jnp.bfloat16),
            keys[row],
            (((1,), (1,)), ((), ())),
            preferred_element_type=jnp.float32,
        )

    def weigh(row):
        valid = token < lengths_ref[row]
        scaled = jnp.where(valid, scores[row % 2] * score_scale, -1e30)
        largest = jnp.maximum(jnp.max(scaled, axis=1, keepdims=True), own_scores[row])
        raised = jnp.exp(scaled - largest)
        own_raised = jnp.exp(own_scores[row] - largest)
        share = 1.0 / (jnp.sum(raised, axis=1, keepdims=True) + own_raised)
        weights[row % 2] = (raised * share).astype(jnp.bfloat16)
        own_weights[row] = (own_raised * share).astype(jnp.bfloat16).astype(jnp.float32)

    def mix(row):
        mixed = jnp.dot(weights[row % 2], values[row], preferred_element_type=jnp.float32)
        mixed = mixed + own_weights[row] * new_values[row : row + 1]
        mixed = jnp.where(own_group, mixed, 0.0)
        chosen = mixed[:, :HD]
        for group in range(1, kv_groups):
            chosen = chosen + mixed[:, group * HD : (group + 1) * HD]
        for part in range(parts):
            attended[part, pl.ds(row, count, stride=here), :] = chosen[
                part * count : (part + 1) * count
            ]

    for step in range(here + 2):
        if step < here:
            key_copy(step).wait()
        if step >= 2:
            value_copy(step - 2).wait()
        if step >= 2:
            mix(step - 2)
        if 1 <= step <= here:
            weigh(step - 1)
        if step < here:
            score(step)
    for k in range(count):
        for part in range(parts):
            out_ref[k, :, part * HD : (part + 1) * HD] = attended[
                part, k * here : (k + 1) * here, :
            ].astype(jnp.bfloat16)


def attend(blocks, lengths, cosine, sine, cache_keys, cache_values):
    count = blocks.shape[0]
    here, span, key_width = cache_keys.shape
    width = blocks.shape[2] - HD
    heads = count * width // HD
    vmem = pl.BlockSpec(memory_space=pltpu.VMEM)
    whole = pl.BlockSpec(memory_space=pl.ANY)
    return pl.pallas_call(
        functools.partial(attend_kernel, count),
        out_shape=jax.ShapeDtypeStruct((count, here, width), jnp.bfloat16),
        in_specs=[pl.BlockSpec(memory_space=pltpu.SMEM), vmem, vmem, whole, whole, vmem],
        out_specs=vmem,
        scratch_shapes=[
            pltpu.VMEM((width // HD + 1, here * count, HD), jnp.float32),
            pltpu.VMEM((width // HD, here * count, HD), jnp.float32),
            pltpu.VMEM((2, heads, span), jnp.float32),
            pltpu.VMEM((2, heads, span), jnp.bfloat16),
            pltpu.VMEM((here, span, key_width), jnp.bfloat16),
            pltpu.VMEM((here, span, key_width), jnp.bfloat16),
            pltpu.SemaphoreType.DMA((here,)),
            pltpu.SemaphoreType.DMA((here,)),
        ],
        compiler_params=pltpu.CompilerParams(vmem_limit_bytes=40 * 1024 * 1024),
        cost_estimate=pl.CostEstimate(
            flops=4 * here * count * width * span,
            bytes_accessed=4 * here * span * key_width,
            transcendentals=here * heads * span,
        ),
    )(lengths, cosine, sine, cache_keys, cache_values, blocks)


def exchange(blocks):
    return lax.all_to_all(blocks, "tensor", split_axis=0, concat_axis=0, tiled=True)


def plans(count):
    bits = list(range(1, count.bit_length() - 1))
    turned = bits[::-1]
    late = bits[1:2] + bits[:1] + bits[2:]
    crossed = late[::-1]
    return [(bits, turned), (bits, crossed), (late, turned), (bits, crossed)]


def timetable(count):
    if count == 16:
        return [int(c) for c in TABLE]
    return [s for _ in range(2 * (count.bit_length() - 2) + 2) for s in (1, 0, 2, 3)]


def place(offset, order):
    spot = 0
    for bit in order:
        spot = spot * 2 + ((offset >> bit) & 1)
    return spot


def project_kernel(count, side, in_ref, w_ref, *refs):
    *set_refs, heads_buffer, w_buffer, arrived = refs
    me = lax.axis_index("tensor")
    width = w_buffer.shape[2]
    offsets = [k for k in range(count) if (k >> 1) % 2 == side]
    offsets = [k for k in offsets if k % 2] + [k for k in offsets if k % 2 == 0]
    copies = []
    for slot, offset in enumerate(offsets):
        column = pl.multiple_of(jnp.bitwise_xor(me, offset) * width, width)
        copies.append(
            pltpu.make_async_copy(
                w_ref.at[:, pl.ds(column, width)], w_buffer.at[slot], arrived.at[slot]
            )
        )
        copies[-1].start()
    here = in_ref.shape[1]
    for k in range(count):
        heads_buffer[k * here : (k + 1) * here, :] = in_ref[k].astype(jnp.float32)
    heads = heads_buffer[...].astype(jnp.bfloat16)
    for slot, offset in enumerate(offsets):
        copies[slot].wait()
        product = jnp.dot(heads, w_buffer[slot], preferred_element_type=jnp.float32).astype(
            jnp.bfloat16
        )
        start = 0
        for which, (order, _) in enumerate(plans(count)):
            ref = set_refs[2 * which + (1 - offset % 2)]
            spot = place(offset, [bit for bit in order if bit != 1])
            ref[spot] = product[start : start + ref.shape[1]]
            start += ref.shape[1]


def project(blocks, w_out, side):
    count, here, depth = blocks.shape
    rows = count * here
    width = w_out.shape[1] // count
    sets = len(plans(count))
    share = jax.ShapeDtypeStruct((count // 4, rows // sets, width), jnp.bfloat16)
    outs = pl.pallas_call(
        functools.partial(project_kernel, count, side),
        out_shape=(share,) * (2 * sets),
        in_specs=[pl.BlockSpec(memory_space=pltpu.VMEM), pl.BlockSpec(memory_space=pl.ANY)],
        out_specs=(pl.BlockSpec(memory_space=pltpu.VMEM),) * (2 * sets),
        scratch_shapes=[
            pltpu.VMEM((rows, depth), jnp.float32),
            pltpu.VMEM((count // 2, depth, width), jnp.bfloat16),
            pltpu.SemaphoreType.DMA((count // 2,)),
        ],
        compiler_params=pltpu.CompilerParams(vmem_limit_bytes=48 * 1024 * 1024),
        cost_estimate=pl.CostEstimate(
            flops=rows * depth * width * count,
            bytes_accessed=(depth + rows) * width * count,
            transcendentals=0,
        ),
    )(blocks, w_out)
    return outs[0::2], outs[1::2]


def finish_kernel(offsets, own_ref, other_ref, gain_ref, *refs):
    out_ref = refs[-1]
    me = lax.axis_index("tensor")
    half, _, width = own_ref.shape
    rows = out_ref.shape[0]
    here = pl.ds(pl.multiple_of(pl.program_id(0) * rows, rows), rows)
    total = jnp.zeros((rows, width), jnp.float32)
    for ref in (own_ref, other_ref):
        for k in range(half):
            block = ref[k, here, :].astype(jnp.float32)
            total = total + block * block
    mean_square = jnp.sum(total, axis=1, keepdims=True) / (2 * half * width)
    scale = lax.rsqrt(mean_square + epsilon)
    for k, offset in enumerate(offsets):
        block = (own_ref if k < half else other_ref)[k % half, here, :].astype(jnp.float32)
        index = jnp.bitwise_xor(me, offset)
        column = pl.multiple_of(index * width, width)
        gain = gain_ref[pl.ds(index, 1), :]
        out_ref[:, pl.ds(column, width)] = (block * scale * gain).astype(jnp.bfloat16)


def finish(own, other, gain, offsets, which, sets, earlier):
    half, rows, width = own.shape
    columns, tiles = 2 * half * width, 2
    operands = [own, other, gain] + ([] if earlier is None else [earlier])
    whole = pl.BlockSpec(memory_space=pltpu.VMEM)
    return pl.pallas_call(
        functools.partial(finish_kernel, offsets),
        grid=(tiles,),
        out_shape=jax.ShapeDtypeStruct((rows * sets, columns), jnp.bfloat16),
        in_specs=[whole] * 3 + [pl.BlockSpec(memory_space=pl.ANY)] * (len(operands) - 3),
        out_specs=pl.BlockSpec((rows // tiles, columns), lambda i: (which * tiles + i, 0)),
        input_output_aliases={} if earlier is None else {3: 0},
        compiler_params=pltpu.CompilerParams(vmem_limit_bytes=24 * 1024 * 1024),
        cost_estimate=pl.CostEstimate(
            flops=6 * rows * columns, bytes_accessed=4 * rows * columns, transcendentals=0
        ),
    )(*operands)


def swap(values, bit, count):
    return lax.ppermute(values, "tensor", [(i, i ^ (1 << bit)) for i in range(count)])


def add(one, other):
    return (one.astype(jnp.float32) + other.astype(jnp.float32)).astype(jnp.bfloat16)


def halves(keep, arrival):
    half = keep.shape[0] // 2
    return add(keep[:half], arrival[:half]), add(keep[half:], arrival[half:])


def on_device(
    hidden_in,
    attn_gain,
    w_query,
    w_keyval,
    cache_keys,
    cache_values,
    w_out,
    ffn_gain,
    lengths,
    positions,
):
    row_count = hidden_in.shape[0]
    count = lax.axis_size("tensor")
    cosine, sine = turns(positions)
    blocks, mine = project_in(hidden_in, attn_gain, w_query, w_keyval, cosine, sine, count)
    head_blocks = exchange(
        attend(exchange(blocks), lengths, cosine, sine, cache_keys, cache_values)
    )
    share_width = w_out.shape[1] // count
    gain = ffn_gain.astype(jnp.float32).reshape(count, share_width)
    orders = plans(count)
    sets = len(orders)
    set_rows = row_count // sets

    def core_sums(heads, side):
        sent, kept = project(heads, w_out, side)
        arrivals = [swap(block, 0, count) for block in sent]
        return [add(keep, arrival) for keep, arrival in zip(kept, arrivals)]

    far = core_sums(head_blocks, 1)
    first = timetable(count)[0]
    gate, far[first] = lax.optimization_barrier((head_blocks, far[first]))
    near = core_sums(gate, 0)
    held, leaving = [], []
    for k in range(sets):
        if orders[k][0][0] == 1:
            held.append(near[k])
            leaving.append(far[k])
        else:
            half = far[k].shape[0] // 2
            held.append(jnp.concatenate([near[k][:half], far[k][:half]], axis=0))
            leaving.append(jnp.concatenate([near[k][half:], far[k][half:]], axis=0))
    streams = [None] * sets
    offsets = [[0] for _ in range(sets)]
    steps = [0] * sets
    last = normed = None
    arrivals = [None] * sets
    for k in timetable(count):
        scatter, gather = orders[k]
        step = steps[k]
        steps[k] += 1
        if step == 0:
            if last is None:
                last = leaving[k]
            else:
                last, _ = lax.optimization_barrier((leaving[k], last))
            arrivals[k] = swap(last, scatter[0], count)
            continue
        held[k], arrivals[k], _ = lax.optimization_barrier((held[k], arrivals[k], last))
        if step < len(scatter):
            held[k], last = halves(held[k], arrivals[k])
            arrivals[k] = swap(last, scatter[step], count)
            continue
        if step == len(scatter):
            own_rows = mine[k * set_rows : (k + 1) * set_rows].astype(jnp.float32)
            total = held[k][0].astype(jnp.float32) + arrivals[k][0].astype(jnp.float32)
            streams[k] = (own_rows + total).astype(jnp.bfloat16)
            last = held[k] = streams[k][None]
        elif step <= len(scatter) + len(gather):
            last = held[k] = jnp.concatenate([held[k], arrivals[k]], axis=0)
        else:
            last = normed = finish(held[k], arrivals[k], gain, offsets[k], k, sets, normed)
            continue
        bit = (gather + [0])[step - len(scatter)]
        arrivals[k] = swap(held[k], bit, count)
        offsets[k] = offsets[k] + [offset ^ (1 << bit) for offset in offsets[k]]
    return (jnp.concatenate(streams, axis=0), normed)


def solution(mesh):
    placed = (
        P("groups", None),
        P(),
        P(None, "tensor"),
        P(None, "tensor"),
        P(("groups", "tensor"), None, None),
        P(("groups", "tensor"), None, None),
        P("tensor", None),
        P(),
        P(("groups", "tensor")),
        P("groups"),
    )
    return jax.shard_map(
        on_device,
        mesh=mesh,
        in_specs=placed,
        out_specs=(P("groups", "tensor"), P("groups", None)),
        check_vma=False,
    )
```

```python
import functools
import math

import jax
import jax.numpy as jnp
from jax import lax
from jax.experimental import pallas as pl
from jax.experimental.pallas import tpu as pltpu
from jax.sharding import PartitionSpec as P

HD = 128


TABLE = "032031032013021320123121302131"

epsilon = 1e-05
rope_theta = 500000.0


def turns(positions):
    half = HD // 2
    entry = jnp.arange(HD, dtype=jnp.int32)
    frequency = jnp.exp((entry % half).astype(jnp.float32) * (-math.log(rope_theta) / half))
    angles = positions.astype(jnp.float32)[:, None] * frequency[None, :]
    sign = jnp.where(entry < half, -1.0, 1.0)
    return jnp.cos(angles), jnp.sin(angles) * sign


def rotate(head, cosine, sine):
    return head * cosine + pltpu.roll(head, HD // 2, 1) * sine


def input_kernel(count, hidden_ref, gain_ref, w_ref, kv_ref, cosine_ref, sine_ref, *refs):
    out_ref, mine_ref, hidden, gain_buffer, w_buffer, kv_buffer, normed, products, kv_products, *sems = refs
    h_sem, w_sem, kv_sem, mine_sem, gain_sem = sems
    me = lax.axis_index("tensor")
    rows, columns = hidden.shape
    depth = normed.shape[2]
    chunks = columns // depth
    width = products.shape[1]
    kv_width = kv_products.shape[1]
    here = rows // count

    def span(k):
        return pl.ds(k * depth, depth)

    def hidden_copy(k):
        return pltpu.make_async_copy(
            hidden_ref.at[:, span(k)], hidden.at[:, span(k)], h_sem.at[k]
        )

    def w_copy(k):
        return pltpu.make_async_copy(w_ref.at[span(k), :], w_buffer.at[span(k), :], w_sem.at[k])

    for k in range(chunks):
        hidden_copy(k).start()
    gain_copy = pltpu.make_async_copy(gain_ref, gain_buffer, gain_sem)
    gain_copy.start()
    kv_copy = pltpu.make_async_copy(kv_ref, kv_buffer, kv_sem)
    own = pl.ds(pl.multiple_of(me * (columns // count), columns // count), columns // count)
    mine_copy = pltpu.make_async_copy(hidden_ref.at[:, own], mine_ref, mine_sem)
    products[...] = jnp.zeros_like(products)
    kv_products[...] = jnp.zeros_like(kv_products)
    total = jnp.zeros((rows, 128), jnp.float32)
    for k in range(chunks):
        hidden_copy(k).wait()
        w_copy(k).start()
        if k == 0:
            kv_copy.start()
        for lane in range(k * depth, (k + 1) * depth, 128):
            part = hidden[:, lane : lane + 128].astype(jnp.float32)
            total = total + part * part
    mine_copy.start()
    scale = lax.rsqrt(jnp.sum(total, axis=1, keepdims=True) / columns + epsilon)

    def norm(k):
        floats = hidden[:, span(k)].astype(jnp.float32)
        gain = gain_buffer[span(k)].astype(jnp.float32).reshape(1, depth)
        normed[k % 2] = (floats * scale * gain).astype(jnp.bfloat16)

    gain_copy.wait()
    norm(0)
    kv_copy.wait()
    for k in range(chunks):
        w_copy(k).wait()
        products[...] += jnp.dot(
            normed[k % 2], w_buffer[span(k), :], preferred_element_type=jnp.float32
        )
        kv_products[...] += lax.dot_general(
            normed[k % 2],
            kv_buffer[:, span(k)],
            (((1,), (1,)), ((), ())),
            preferred_element_type=jnp.float32,
        )
        if k + 1 < chunks:
            norm(k + 1)

    shift = lax.rem(me, HD // kv_width) * kv_width
    blank = jnp.zeros((rows, HD - kv_width), jnp.float32)
    moved = pltpu.roll(jnp.concatenate([kv_products[...], blank], axis=1), shift, 1)
    results = [
        rotate(products[:, start : start + HD], cosine_ref[...], sine_ref[...])
        for start in range(0, width, HD)
    ] + [moved]
    for part, result in enumerate(results):
        for k in range(count):
            out_ref[k, :, part * HD : (part + 1) * HD] = result[
                k * here : (k + 1) * here
            ].astype(jnp.bfloat16)
    mine_copy.wait()


def project_in(hidden_in, gain, w_query, w_keyval, cosine, sine, count):
    rows, columns = hidden_in.shape
    width, kv_width = w_query.shape[1], w_keyval.shape[1]
    depth = columns // 8
    chunks = columns // depth
    vmem = pl.BlockSpec(memory_space=pltpu.VMEM)
    whole = pl.BlockSpec(memory_space=pl.ANY)
    return pl.pallas_call(
        functools.partial(input_kernel, count),
        out_shape=(
            jax.ShapeDtypeStruct((count, rows // count, width + HD), jnp.bfloat16),
            jax.ShapeDtypeStruct((rows, columns // count), jnp.bfloat16),
        ),
        in_specs=[whole, whole, whole, whole, vmem, vmem],
        out_specs=(vmem, vmem),
        scratch_shapes=[
            pltpu.VMEM((rows, columns), jnp.bfloat16),
            pltpu.VMEM((columns,), jnp.bfloat16),
            pltpu.VMEM((columns, width), jnp.bfloat16),
            pltpu.VMEM((kv_width, columns), jnp.bfloat16),
            pltpu.VMEM((2, rows, depth), jnp.bfloat16),
            pltpu.VMEM((rows, width), jnp.float32),
            pltpu.VMEM((rows, kv_width), jnp.float32),
            pltpu.SemaphoreType.DMA((chunks,)),
            pltpu.SemaphoreType.DMA((chunks,)),
            pltpu.SemaphoreType.DMA,
            pltpu.SemaphoreType.DMA,
            pltpu.SemaphoreType.DMA,
        ],
        compiler_params=pltpu.CompilerParams(vmem_limit_bytes=52 * 1024 * 1024),
        cost_estimate=pl.CostEstimate(
            flops=2 * rows * columns * (width + kv_width),
            bytes_accessed=2 * columns * (rows + width + kv_width),
            transcendentals=0,
        ),
    )(hidden_in, gain, w_query, w_keyval.T, cosine, sine)


def attend_kernel(count, lengths_ref, cosine_ref, sine_ref, keys_ref, values_ref, *refs):
    in_ref, out_ref, queries, attended, scores, weights, keys, values, k_sem, v_sem = refs
    me = lax.axis_index("tensor")
    here, span, key_width = keys.shape
    kv_groups = key_width // HD
    parts = attended.shape[0]

    def key_copy(row):
        return pltpu.make_async_copy(keys_ref.at[row], keys.at[row], k_sem.at[row])

    def value_copy(row):
        return pltpu.make_async_copy(values_ref.at[row], values.at[row], v_sem.at[row])

    for row in range(here + 2):
        if row < here:
            key_copy(row).start()
        if row >= 2:
            value_copy(row - 2).start()

    for device in range(count):
        for part in range(parts + 1):
            queries[part, device * here : (device + 1) * here, :] = in_ref[
                device, :, part * HD : (part + 1) * HD
            ].astype(jnp.float32)
    mine = pl.ds(pl.multiple_of(me * here, here), here)
    cosine, sine = cosine_ref[mine, :], sine_ref[mine, :]
    shares = count // (2 * kv_groups)
    tiles = []
    for tile in range(2 * kv_groups):
        joined = jnp.zeros((here, HD), jnp.float32)
        for device in range(tile * shares, (tile + 1) * shares):
            joined = joined + queries[parts, device * here : (device + 1) * here, :]
        tiles.append(joined)
    new_keys = [rotate(tile, cosine, sine) for tile in tiles[:kv_groups]]
    new_keys = jnp.concatenate(new_keys, axis=1).astype(jnp.bfloat16).astype(jnp.float32)
    new_values = jnp.concatenate(tiles[kv_groups:], axis=1)

    shape = (parts * count, key_width)
    group_devices = count // kv_groups
    device = lax.rem(lax.broadcasted_iota(jnp.int32, shape, 0), count)
    column = lax.broadcasted_iota(jnp.int32, shape, 1)
    own_group = lax.div(device, group_devices) == lax.div(column, HD)
    token = lax.broadcasted_iota(jnp.int32, (1, span), 1)
    score_scale = HD ** (-0.5)
    own_scores, own_weights = {}, {}

    def score(row):
        heads = jnp.concatenate(
            [queries[part, pl.ds(row, count, stride=here), :] for part in range(parts)], axis=0
        )
        heads = jnp.where(own_group, jnp.concatenate([heads] * kv_groups, axis=1), 0.0)
        own_scores[row] = (
            jnp.sum(heads * new_keys[row : row + 1], axis=1, keepdims=True) * score_scale
        )
        scores[row % 2] = lax.dot_general(
            heads.astype(jnp.bfloat16),
            keys[row],
            (((1,), (1,)), ((), ())),
            preferred_element_type=jnp.float32,
        )

    def weigh(row):
        valid = token < lengths_ref[row]
        scaled = jnp.where(valid, scores[row % 2] * score_scale, -1e30)
        largest = jnp.maximum(jnp.max(scaled, axis=1, keepdims=True), own_scores[row])
        raised = jnp.exp(scaled - largest)
        own_raised = jnp.exp(own_scores[row] - largest)
        share = 1.0 / (jnp.sum(raised, axis=1, keepdims=True) + own_raised)
        weights[row % 2] = (raised * share).astype(jnp.bfloat16)
        own_weights[row] = (own_raised * share).astype(jnp.bfloat16).astype(jnp.float32)

    def mix(row):
        mixed = jnp.dot(weights[row % 2], values[row], preferred_element_type=jnp.float32)
        mixed = mixed + own_weights[row] * new_values[row : row + 1]
        mixed = jnp.where(own_group, mixed, 0.0)
        chosen = mixed[:, :HD]
        for group in range(1, kv_groups):
            chosen = chosen + mixed[:, group * HD : (group + 1) * HD]
        for part in range(parts):
            attended[part, pl.ds(row, count, stride=here), :] = chosen[
                part * count : (part + 1) * count
            ]

    for step in range(here + 2):
        if step < here:
            key_copy(step).wait()
        if step >= 2:
            value_copy(step - 2).wait()
        if step >= 2:
            mix(step - 2)
        if 1 <= step <= here:
            weigh(step - 1)
        if step < here:
            score(step)
    for k in range(count):
        for part in range(parts):
            out_ref[k, :, part * HD : (part + 1) * HD] = attended[
                part, k * here : (k + 1) * here, :
            ].astype(jnp.bfloat16)


def attend(blocks, lengths, cosine, sine, cache_keys, cache_values):
    count = blocks.shape[0]
    here, span, key_width = cache_keys.shape
    width = blocks.shape[2] - HD
    heads = count * width // HD
    vmem = pl.BlockSpec(memory_space=pltpu.VMEM)
    whole = pl.BlockSpec(memory_space=pl.ANY)
    return pl.pallas_call(
        functools.partial(attend_kernel, count),
        out_shape=jax.ShapeDtypeStruct((count, here, width), jnp.bfloat16),
        in_specs=[pl.BlockSpec(memory_space=pltpu.SMEM), vmem, vmem, whole, whole, vmem],
        out_specs=vmem,
        scratch_shapes=[
            pltpu.VMEM((width // HD + 1, here * count, HD), jnp.float32),
            pltpu.VMEM((width // HD, here * count, HD), jnp.float32),
            pltpu.VMEM((2, heads, span), jnp.float32),
            pltpu.VMEM((2, heads, span), jnp.bfloat16),
            pltpu.VMEM((here, span, key_width), jnp.bfloat16),
            pltpu.VMEM((here, span, key_width), jnp.bfloat16),
            pltpu.SemaphoreType.DMA((here,)),
            pltpu.SemaphoreType.DMA((here,)),
        ],
        compiler_params=pltpu.CompilerParams(vmem_limit_bytes=40 * 1024 * 1024),
        cost_estimate=pl.CostEstimate(
            flops=4 * here * count * width * span,
            bytes_accessed=4 * here * span * key_width,
            transcendentals=here * heads * span,
        ),
    )(lengths, cosine, sine, cache_keys, cache_values, blocks)


def exchange(blocks):
    return lax.all_to_all(blocks, "tensor", split_axis=0, concat_axis=0, tiled=True)


def plans(count):
    bits = list(range(1, count.bit_length() - 1))
    turned = bits[::-1]
    late = bits[1:2] + bits[:1] + bits[2:]
    crossed = late[::-1]
    return [(bits, turned), (bits, crossed), (late, turned), (bits, crossed)]


def timetable(count):
    if count == 16:
        return [int(c) for c in TABLE]
    steps = 2 * (count.bit_length() - 2) + 1
    return [s for _ in range(steps) for s in (1, 0, 2, 3)] + [1, 3]


def place(offset, order):
    spot = 0
    for bit in order:
        spot = spot * 2 + ((offset >> bit) & 1)
    return spot


def project_kernel(count, side, in_ref, w_ref, *refs):
    *set_refs, heads_buffer, w_buffer, arrived = refs
    me = lax.axis_index("tensor")
    width = w_buffer.shape[2]
    offsets = [k for k in range(count) if (k >> 1) % 2 == side]
    offsets = [k for k in offsets if k % 2] + [k for k in offsets if k % 2 == 0]
    copies = []
    for slot, offset in enumerate(offsets):
        column = pl.multiple_of(jnp.bitwise_xor(me, offset) * width, width)
        copies.append(
            pltpu.make_async_copy(
                w_ref.at[:, pl.ds(column, width)], w_buffer.at[slot], arrived.at[slot]
            )
        )
        copies[-1].start()
    here = in_ref.shape[1]
    for k in range(count):
        heads_buffer[k * here : (k + 1) * here, :] = in_ref[k].astype(jnp.float32)
    heads = heads_buffer[...].astype(jnp.bfloat16)
    for slot, offset in enumerate(offsets):
        copies[slot].wait()
        product = jnp.dot(heads, w_buffer[slot], preferred_element_type=jnp.float32).astype(
            jnp.bfloat16
        )
        start = 0
        for which, (order, _) in enumerate(plans(count)):
            ref = set_refs[2 * which + (1 - offset % 2)]
            spot = place(offset, [bit for bit in order if bit != 1])
            ref[spot] = product[start : start + ref.shape[1]]
            start += ref.shape[1]


def project(blocks, w_out, side):
    count, here, depth = blocks.shape
    rows = count * here
    width = w_out.shape[1] // count
    sets = len(plans(count))
    share = jax.ShapeDtypeStruct((count // 4, rows // sets, width), jnp.bfloat16)
    outs = pl.pallas_call(
        functools.partial(project_kernel, count, side),
        out_shape=(share,) * (2 * sets),
        in_specs=[pl.BlockSpec(memory_space=pltpu.VMEM), pl.BlockSpec(memory_space=pl.ANY)],
        out_specs=(pl.BlockSpec(memory_space=pltpu.VMEM),) * (2 * sets),
        scratch_shapes=[
            pltpu.VMEM((rows, depth), jnp.float32),
            pltpu.VMEM((count // 2, depth, width), jnp.bfloat16),
            pltpu.SemaphoreType.DMA((count // 2,)),
        ],
        compiler_params=pltpu.CompilerParams(vmem_limit_bytes=48 * 1024 * 1024),
        cost_estimate=pl.CostEstimate(
            flops=rows * depth * width * count,
            bytes_accessed=(depth + rows) * width * count,
            transcendentals=0,
        ),
    )(blocks, w_out)
    return outs[0::2], outs[1::2]


def finish_kernel(offsets, gain_ref, *refs):
    out_ref, own_ref = refs[-2:]
    me = lax.axis_index("tensor")
    half, rows, width = refs[0].shape

    def norm(k, order):
        parts = refs[2 * k : 2 * k + 2]
        own_ref[...] = parts[0][0]
        total = jnp.zeros((rows, width), jnp.float32)
        for ref in parts:
            for spot in range(half):
                block = ref[spot].astype(jnp.float32)
                total = total + block * block
        mean_square = jnp.sum(total, axis=1, keepdims=True) / (2 * half * width)
        scale = lax.rsqrt(mean_square + epsilon)
        for spot, offset in enumerate(order):
            block = parts[spot // half][spot % half].astype(jnp.float32)
            index = jnp.bitwise_xor(me, offset)
            column = pl.multiple_of(index * width, width)
            gain = gain_ref[pl.ds(index, 1), :]
            out_ref[:, pl.ds(column, width)] = (block * scale * gain).astype(jnp.bfloat16)

    for k, order in enumerate(offsets):
        pl.when(pl.program_id(0) == k)(functools.partial(norm, k, order))


def finish(parts, gain, offsets, which, groups, earlier):
    half, rows, width = parts[0].shape
    columns, count = 2 * half * width, len(offsets)
    operands = [gain, *parts, *earlier]
    specs = [pl.BlockSpec(memory_space=pltpu.VMEM)] * (1 + len(parts))
    specs += [pl.BlockSpec(memory_space=pl.ANY)] * len(earlier)
    return pl.pallas_call(
        functools.partial(finish_kernel, offsets),
        grid=(count,),
        out_shape=tuple(
            jax.ShapeDtypeStruct((rows * count * groups, size), jnp.bfloat16)
            for size in (columns, width)
        ),
        in_specs=specs,
        out_specs=tuple(
            pl.BlockSpec((rows, size), lambda i: (which * count + i, 0))
            for size in (columns, width)
        ),
        input_output_aliases={1 + len(parts) + k: k for k in range(len(earlier))},
        compiler_params=pltpu.CompilerParams(vmem_limit_bytes=12 * 1024 * 1024),
        cost_estimate=pl.CostEstimate(
            flops=6 * count * rows * columns,
            bytes_accessed=4 * count * rows * columns,
            transcendentals=0,
        ),
    )(*operands)


def swap(values, bit, count):
    return lax.ppermute(values, "tensor", [(i, i ^ (1 << bit)) for i in range(count)])


def add(one, other):
    return (one.astype(jnp.float32) + other.astype(jnp.float32)).astype(jnp.bfloat16)


def halves(keep, arrival):
    half = keep.shape[0] // 2
    return add(keep[:half], arrival[:half]), add(keep[half:], arrival[half:])


def on_device(
    hidden_in,
    attn_gain,
    w_query,
    w_keyval,
    cache_keys,
    cache_values,
    w_out,
    ffn_gain,
    lengths,
    positions,
):
    row_count = hidden_in.shape[0]
    count = lax.axis_size("tensor")
    cosine, sine = turns(positions)
    blocks, mine = project_in(hidden_in, attn_gain, w_query, w_keyval, cosine, sine, count)
    head_blocks = exchange(
        attend(exchange(blocks), lengths, cosine, sine, cache_keys, cache_values)
    )
    share_width = w_out.shape[1] // count
    gain = ffn_gain.astype(jnp.float32).reshape(count, share_width)
    orders = plans(count)
    sets = len(orders)
    set_rows = row_count // sets

    def core_sums(heads, side):
        sent, kept = project(heads, w_out, side)
        arrivals = [swap(block, 0, count) for block in sent]
        return [add(keep, arrival) for keep, arrival in zip(kept, arrivals)]

    far = core_sums(head_blocks, 1)
    first = timetable(count)[0]
    gate, far[first] = lax.optimization_barrier((head_blocks, far[first]))
    near = core_sums(gate, 0)
    held, leaving = [], []
    for k in range(sets):
        if orders[k][0][0] == 1:
            held.append(near[k])
            leaving.append(far[k])
        else:
            half = far[k].shape[0] // 2
            held.append(jnp.concatenate([near[k][:half], far[k][:half]], axis=0))
            leaving.append(jnp.concatenate([near[k][half:], far[k][half:]], axis=0))
    offsets = [[0] for _ in range(sets)]
    steps = [0] * sets
    last, results = None, ()
    arrivals = [None] * sets
    for k in timetable(count):
        scatter, gather = orders[k]
        step = steps[k]
        steps[k] += 1
        if step == 0:
            if last is None:
                last = leaving[k]
            else:
                last, _ = lax.optimization_barrier((leaving[k], last))
            arrivals[k] = swap(last, scatter[0], count)
            continue
        held[k], arrivals[k], _ = lax.optimization_barrier((held[k], arrivals[k], last))
        if step < len(scatter):
            held[k], last = halves(held[k], arrivals[k])
            arrivals[k] = swap(last, scatter[step], count)
            continue
        if step == len(scatter):
            own_rows = mine[k * set_rows : (k + 1) * set_rows].astype(jnp.float32)
            total = held[k][0].astype(jnp.float32) + arrivals[k][0].astype(jnp.float32)
            last = held[k] = (own_rows + total).astype(jnp.bfloat16)[None]
        elif step <= len(scatter) + len(gather):
            last = held[k] = jnp.concatenate([held[k], arrivals[k]], axis=0)
        else:
            pair = [k - 1, k]
            parts = [block for m in pair for block in (held[m], arrivals[m])]
            lists = [offsets[m] for m in pair]
            results = finish(parts, gain, lists, k // 2, sets // 2, results)
            last = results[0]
            continue
        bit = (gather + [0])[step - len(scatter)]
        arrivals[k] = swap(held[k], bit, count)
        offsets[k] = offsets[k] + [offset ^ (1 << bit) for offset in offsets[k]]
    normed, stream = results
    return (stream, normed)


def solution(mesh):
    placed = (
        P("groups", None),
        P(),
        P(None, "tensor"),
        P(None, "tensor"),
        P(("groups", "tensor"), None, None),
        P(("groups", "tensor"), None, None),
        P("tensor", None),
        P(),
        P(("groups", "tensor")),
        P("groups"),
    )
    return jax.shard_map(
        on_device,
        mesh=mesh,
        in_specs=placed,
        out_specs=(P("groups", "tensor"), P("groups", None)),
        check_vma=False,
    )
```

```python
import functools
import math

import jax
import jax.numpy as jnp
from jax import lax
from jax.experimental import pallas as pl
from jax.experimental.pallas import tpu as pltpu
from jax.sharding import PartitionSpec as P

HD = 128


TABLE = "032031032013021320123121302131"

epsilon = 1e-05
rope_theta = 500000.0


def turns(positions):
    half = HD // 2
    entry = jnp.arange(HD, dtype=jnp.int32)
    frequency = jnp.exp((entry % half).astype(jnp.float32) * (-math.log(rope_theta) / half))
    angles = positions.astype(jnp.float32)[:, None] * frequency[None, :]
    sign = jnp.where(entry < half, -1.0, 1.0)
    return jnp.cos(angles), jnp.sin(angles) * sign


def rotate(head, cosine, sine):
    return head * cosine + pltpu.roll(head, HD // 2, 1) * sine


def input_kernel(count, hidden_ref, gain_ref, w_ref, kv_ref, cosine_ref, sine_ref, *refs):
    out_ref, mine_ref, hidden, gain_buffer, w_buffer, kv_buffer, normed, products, kv_products, *sems = refs
    h_sem, w_sem, kv_sem, mine_sem, gain_sem = sems
    me = lax.axis_index("tensor")
    rows, columns = hidden.shape
    depth = normed.shape[2]
    chunks = columns // depth
    width = products.shape[1]
    kv_width = kv_products.shape[1]
    here = rows // count

    def span(k):
        return pl.ds(k * depth, depth)

    def hidden_copy(k):
        return pltpu.make_async_copy(
            hidden_ref.at[:, span(k)], hidden.at[:, span(k)], h_sem.at[k]
        )

    def w_copy(k):
        return pltpu.make_async_copy(w_ref.at[span(k), :], w_buffer.at[span(k), :], w_sem.at[k])

    for k in range(chunks):
        hidden_copy(k).start()
    gain_copy = pltpu.make_async_copy(gain_ref, gain_buffer, gain_sem)
    gain_copy.start()
    kv_copy = pltpu.make_async_copy(kv_ref, kv_buffer, kv_sem)
    own = pl.ds(pl.multiple_of(me * (columns // count), columns // count), columns // count)
    mine_copy = pltpu.make_async_copy(hidden_ref.at[:, own], mine_ref, mine_sem)
    products[...] = jnp.zeros_like(products)
    kv_products[...] = jnp.zeros_like(kv_products)
    total = jnp.zeros((rows, 128), jnp.float32)
    for k in range(chunks):
        hidden_copy(k).wait()
        w_copy(k).start()
        if k == 0:
            kv_copy.start()
        for lane in range(k * depth, (k + 1) * depth, 128):
            part = hidden[:, lane : lane + 128].astype(jnp.float32)
            total = total + part * part
    mine_copy.start()
    scale = lax.rsqrt(jnp.sum(total, axis=1, keepdims=True) / columns + epsilon)

    def norm(k):
        floats = hidden[:, span(k)].astype(jnp.float32)
        gain = gain_buffer[span(k)].astype(jnp.float32).reshape(1, depth)
        normed[k % 2] = (floats * scale * gain).astype(jnp.bfloat16)

    gain_copy.wait()
    norm(0)
    kv_copy.wait()
    for k in range(chunks):
        w_copy(k).wait()
        products[...] += jnp.dot(
            normed[k % 2], w_buffer[span(k), :], preferred_element_type=jnp.float32
        )
        kv_products[...] += lax.dot_general(
            normed[k % 2],
            kv_buffer[:, span(k)],
            (((1,), (1,)), ((), ())),
            preferred_element_type=jnp.float32,
        )
        if k + 1 < chunks:
            norm(k + 1)

    shift = lax.rem(me, HD // kv_width) * kv_width
    blank = jnp.zeros((rows, HD - kv_width), jnp.float32)
    moved = pltpu.roll(jnp.concatenate([kv_products[...], blank], axis=1), shift, 1)
    results = [
        rotate(products[:, start : start + HD], cosine_ref[...], sine_ref[...])
        for start in range(0, width, HD)
    ] + [moved]
    for part, result in enumerate(results):
        for k in range(count):
            out_ref[k, :, part * HD : (part + 1) * HD] = result[
                k * here : (k + 1) * here
            ].astype(jnp.bfloat16)
    mine_copy.wait()


def project_in(hidden_in, gain, w_query, w_keyval, cosine, sine, count):
    rows, columns = hidden_in.shape
    width, kv_width = w_query.shape[1], w_keyval.shape[1]
    depth = columns // 8
    chunks = columns // depth
    vmem = pl.BlockSpec(memory_space=pltpu.VMEM)
    whole = pl.BlockSpec(memory_space=pl.ANY)
    return pl.pallas_call(
        functools.partial(input_kernel, count),
        out_shape=(
            jax.ShapeDtypeStruct((count, rows // count, width + HD), jnp.bfloat16),
            jax.ShapeDtypeStruct((rows, columns // count), jnp.bfloat16),
        ),
        in_specs=[whole, whole, whole, whole, vmem, vmem],
        out_specs=(vmem, vmem),
        scratch_shapes=[
            pltpu.VMEM((rows, columns), jnp.bfloat16),
            pltpu.VMEM((columns,), jnp.bfloat16),
            pltpu.VMEM((columns, width), jnp.bfloat16),
            pltpu.VMEM((kv_width, columns), jnp.bfloat16),
            pltpu.VMEM((2, rows, depth), jnp.bfloat16),
            pltpu.VMEM((rows, width), jnp.float32),
            pltpu.VMEM((rows, kv_width), jnp.float32),
            pltpu.SemaphoreType.DMA((chunks,)),
            pltpu.SemaphoreType.DMA((chunks,)),
            pltpu.SemaphoreType.DMA,
            pltpu.SemaphoreType.DMA,
            pltpu.SemaphoreType.DMA,
        ],
        compiler_params=pltpu.CompilerParams(vmem_limit_bytes=52 * 1024 * 1024),
        cost_estimate=pl.CostEstimate(
            flops=2 * rows * columns * (width + kv_width),
            bytes_accessed=2 * columns * (rows + width + kv_width),
            transcendentals=0,
        ),
    )(hidden_in, gain, w_query, w_keyval.T, cosine, sine)


def attend_kernel(count, lengths_ref, cosine_ref, sine_ref, keys_ref, values_ref, *refs):
    in_ref, out_ref, queries, attended, scores, weights, keys, values, k_sem, v_sem = refs
    me = lax.axis_index("tensor")
    here, span, key_width = keys.shape
    kv_groups = key_width // HD
    parts = attended.shape[0]

    def key_copy(row):
        return pltpu.make_async_copy(keys_ref.at[row], keys.at[row], k_sem.at[row])

    def value_copy(row):
        return pltpu.make_async_copy(values_ref.at[row], values.at[row], v_sem.at[row])

    for row in range(here + 2):
        if row < here:
            key_copy(row).start()
        if row >= 2:
            value_copy(row - 2).start()

    for device in range(count):
        for part in range(parts + 1):
            queries[part, device * here : (device + 1) * here, :] = in_ref[
                device, :, part * HD : (part + 1) * HD
            ].astype(jnp.float32)
    mine = pl.ds(pl.multiple_of(me * here, here), here)
    cosine, sine = cosine_ref[mine, :], sine_ref[mine, :]
    shares = count // (2 * kv_groups)
    tiles = []
    for tile in range(2 * kv_groups):
        joined = jnp.zeros((here, HD), jnp.float32)
        for device in range(tile * shares, (tile + 1) * shares):
            joined = joined + queries[parts, device * here : (device + 1) * here, :]
        tiles.append(joined)
    new_keys = [rotate(tile, cosine, sine) for tile in tiles[:kv_groups]]
    new_keys = jnp.concatenate(new_keys, axis=1).astype(jnp.bfloat16).astype(jnp.float32)
    new_values = jnp.concatenate(tiles[kv_groups:], axis=1)

    shape = (parts * count, key_width)
    group_devices = count // kv_groups
    device = lax.rem(lax.broadcasted_iota(jnp.int32, shape, 0), count)
    column = lax.broadcasted_iota(jnp.int32, shape, 1)
    own_group = lax.div(device, group_devices) == lax.div(column, HD)
    token = lax.broadcasted_iota(jnp.int32, (1, span), 1)
    score_scale = HD ** (-0.5)
    own_scores, own_weights = {}, {}

    def score(row):
        heads = jnp.concatenate(
            [queries[part, pl.ds(row, count, stride=here), :] for part in range(parts)], axis=0
        )
        heads = jnp.where(own_group, jnp.concatenate([heads] * kv_groups, axis=1), 0.0)
        own_scores[row] = (
            jnp.sum(heads * new_keys[row : row + 1], axis=1, keepdims=True) * score_scale
        )
        scores[row % 2] = lax.dot_general(
            heads.astype(jnp.bfloat16),
            keys[row],
            (((1,), (1,)), ((), ())),
            preferred_element_type=jnp.float32,
        )

    def weigh(row):
        valid = token < lengths_ref[row]
        scaled = jnp.where(valid, scores[row % 2] * score_scale, -1e30)
        largest = jnp.maximum(jnp.max(scaled, axis=1, keepdims=True), own_scores[row])
        raised = jnp.exp(scaled - largest)
        own_raised = jnp.exp(own_scores[row] - largest)
        share = 1.0 / (jnp.sum(raised, axis=1, keepdims=True) + own_raised)
        weights[row % 2] = (raised * share).astype(jnp.bfloat16)
        own_weights[row] = (own_raised * share).astype(jnp.bfloat16).astype(jnp.float32)

    def mix(row):
        mixed = jnp.dot(weights[row % 2], values[row], preferred_element_type=jnp.float32)
        mixed = mixed + own_weights[row] * new_values[row : row + 1]
        mixed = jnp.where(own_group, mixed, 0.0)
        chosen = mixed[:, :HD]
        for group in range(1, kv_groups):
            chosen = chosen + mixed[:, group * HD : (group + 1) * HD]
        for part in range(parts):
            attended[part, pl.ds(row, count, stride=here), :] = chosen[
                part * count : (part + 1) * count
            ]

    for step in range(here + 2):
        if step < here:
            key_copy(step).wait()
        if step >= 2:
            value_copy(step - 2).wait()
        if step >= 2:
            mix(step - 2)
        if 1 <= step <= here:
            weigh(step - 1)
        if step < here:
            score(step)
    for k in range(count):
        for part in range(parts):
            out_ref[k, :, part * HD : (part + 1) * HD] = attended[
                part, k * here : (k + 1) * here, :
            ].astype(jnp.bfloat16)


def attend(blocks, lengths, cosine, sine, cache_keys, cache_values):
    count = blocks.shape[0]
    here, span, key_width = cache_keys.shape
    width = blocks.shape[2] - HD
    heads = count * width // HD
    vmem = pl.BlockSpec(memory_space=pltpu.VMEM)
    whole = pl.BlockSpec(memory_space=pl.ANY)
    return pl.pallas_call(
        functools.partial(attend_kernel, count),
        out_shape=jax.ShapeDtypeStruct((count, here, width), jnp.bfloat16),
        in_specs=[pl.BlockSpec(memory_space=pltpu.SMEM), vmem, vmem, whole, whole, vmem],
        out_specs=vmem,
        scratch_shapes=[
            pltpu.VMEM((width // HD + 1, here * count, HD), jnp.float32),
            pltpu.VMEM((width // HD, here * count, HD), jnp.float32),
            pltpu.VMEM((2, heads, span), jnp.float32),
            pltpu.VMEM((2, heads, span), jnp.bfloat16),
            pltpu.VMEM((here, span, key_width), jnp.bfloat16),
            pltpu.VMEM((here, span, key_width), jnp.bfloat16),
            pltpu.SemaphoreType.DMA((here,)),
            pltpu.SemaphoreType.DMA((here,)),
        ],
        compiler_params=pltpu.CompilerParams(vmem_limit_bytes=40 * 1024 * 1024),
        cost_estimate=pl.CostEstimate(
            flops=4 * here * count * width * span,
            bytes_accessed=4 * here * span * key_width,
            transcendentals=here * heads * span,
        ),
    )(lengths, cosine, sine, cache_keys, cache_values, blocks)


def exchange(blocks):
    return lax.all_to_all(blocks, "tensor", split_axis=0, concat_axis=0, tiled=True)


def plans(count):
    bits = list(range(1, count.bit_length() - 1))
    turned = bits[::-1]
    late = bits[1:2] + bits[:1] + bits[2:]
    crossed = late[::-1]
    return [(bits, turned), (bits, crossed), (late, turned), (bits, crossed)]


def timetable(count):
    if count == 16:
        return [int(c) for c in TABLE]
    steps = 2 * (count.bit_length() - 2) + 1
    return [s for _ in range(steps) for s in (1, 0, 2, 3)] + [1, 3]


def place(offset, order):
    spot = 0
    for bit in order:
        spot = spot * 2 + ((offset >> bit) & 1)
    return spot


def project_kernel(count, side, in_ref, w_ref, *refs):
    *set_refs, heads_buffer, w_buffer, arrived = refs
    me = lax.axis_index("tensor")
    width = w_buffer.shape[2]
    offsets = [k for k in range(count) if (k >> 1) % 2 == side]
    offsets = [k for k in offsets if k % 2] + [k for k in offsets if k % 2 == 0]
    copies = []
    for slot, offset in enumerate(offsets):
        column = pl.multiple_of(jnp.bitwise_xor(me, offset) * width, width)
        copies.append(
            pltpu.make_async_copy(
                w_ref.at[:, pl.ds(column, width)], w_buffer.at[slot], arrived.at[slot]
            )
        )
        copies[-1].start()
    here = in_ref.shape[1]
    for k in range(count):
        heads_buffer[k * here : (k + 1) * here, :] = in_ref[k].astype(jnp.float32)
    heads = heads_buffer[...].astype(jnp.bfloat16)
    for slot, offset in enumerate(offsets):
        copies[slot].wait()
        product = jnp.dot(heads, w_buffer[slot], preferred_element_type=jnp.float32).astype(
            jnp.bfloat16
        )
        start = 0
        for which, (order, _) in enumerate(plans(count)):
            ref = set_refs[2 * which + (1 - offset % 2)]
            spot = place(offset, [bit for bit in order if bit != 1])
            ref[spot] = product[start : start + ref.shape[1]]
            start += ref.shape[1]


def project(blocks, w_out, side):
    count, here, depth = blocks.shape
    rows = count * here
    width = w_out.shape[1] // count
    sets = len(plans(count))
    share = jax.ShapeDtypeStruct((count // 4, rows // sets, width), jnp.bfloat16)
    outs = pl.pallas_call(
        functools.partial(project_kernel, count, side),
        out_shape=(share,) * (2 * sets),
        in_specs=[pl.BlockSpec(memory_space=pltpu.VMEM), pl.BlockSpec(memory_space=pl.ANY)],
        out_specs=(pl.BlockSpec(memory_space=pltpu.VMEM),) * (2 * sets),
        scratch_shapes=[
            pltpu.VMEM((rows, depth), jnp.float32),
            pltpu.VMEM((count // 2, depth, width), jnp.bfloat16),
            pltpu.SemaphoreType.DMA((count // 2,)),
        ],
        compiler_params=pltpu.CompilerParams(vmem_limit_bytes=48 * 1024 * 1024),
        cost_estimate=pl.CostEstimate(
            flops=rows * depth * width * count,
            bytes_accessed=(depth + rows) * width * count,
            transcendentals=0,
        ),
    )(blocks, w_out)
    return outs[0::2], outs[1::2]


def finish_kernel(offsets, gain_ref, *refs):
    out_ref, own_ref = refs[-2:]
    me = lax.axis_index("tensor")
    half, rows, width = refs[0].shape

    def norm(k, order):
        parts = refs[2 * k : 2 * k + 2]
        own_ref[...] = parts[0][0]
        total = jnp.zeros((rows, width), jnp.float32)
        for ref in parts:
            for spot in range(half):
                block = ref[spot].astype(jnp.float32)
                total = total + block * block
        mean_square = jnp.sum(total, axis=1, keepdims=True) / (2 * half * width)
        scale = lax.rsqrt(mean_square + epsilon)
        for spot, offset in enumerate(order):
            block = parts[spot // half][spot % half].astype(jnp.float32)
            index = jnp.bitwise_xor(me, offset)
            column = pl.multiple_of(index * width, width)
            gain = gain_ref[pl.ds(index, 1), :]
            out_ref[:, pl.ds(column, width)] = (block * scale * gain).astype(jnp.bfloat16)

    for k, order in enumerate(offsets):
        pl.when(pl.program_id(0) == k)(functools.partial(norm, k, order))


def finish(parts, gain, offsets, which, groups, earlier):
    half, rows, width = parts[0].shape
    columns, count = 2 * half * width, len(offsets)
    parts = [pltpu.with_memory_space_constraint(part, pltpu.VMEM) for part in parts]
    operands = [gain, *parts, *earlier]
    specs = [pl.BlockSpec(memory_space=pltpu.VMEM)] * (1 + len(parts))
    specs += [pl.BlockSpec(memory_space=pl.ANY)] * len(earlier)
    return pl.pallas_call(
        functools.partial(finish_kernel, offsets),
        grid=(count,),
        out_shape=tuple(
            jax.ShapeDtypeStruct((rows * count * groups, size), jnp.bfloat16)
            for size in (columns, width)
        ),
        in_specs=specs,
        out_specs=tuple(
            pl.BlockSpec((rows, size), lambda i: (which * count + i, 0))
            for size in (columns, width)
        ),
        input_output_aliases={1 + len(parts) + k: k for k in range(len(earlier))},
        compiler_params=pltpu.CompilerParams(vmem_limit_bytes=12 * 1024 * 1024),
        cost_estimate=pl.CostEstimate(
            flops=6 * count * rows * columns,
            bytes_accessed=4 * count * rows * columns,
            transcendentals=0,
        ),
    )(*operands)


def swap(values, bit, count):
    return lax.ppermute(values, "tensor", [(i, i ^ (1 << bit)) for i in range(count)])


def add(one, other):
    return (one.astype(jnp.float32) + other.astype(jnp.float32)).astype(jnp.bfloat16)


def halves(keep, arrival):
    half = keep.shape[0] // 2
    return add(keep[:half], arrival[:half]), add(keep[half:], arrival[half:])


def on_device(
    hidden_in,
    attn_gain,
    w_query,
    w_keyval,
    cache_keys,
    cache_values,
    w_out,
    ffn_gain,
    lengths,
    positions,
):
    row_count = hidden_in.shape[0]
    count = lax.axis_size("tensor")
    cosine, sine = turns(positions)
    blocks, mine = project_in(hidden_in, attn_gain, w_query, w_keyval, cosine, sine, count)
    head_blocks = exchange(
        attend(exchange(blocks), lengths, cosine, sine, cache_keys, cache_values)
    )
    share_width = w_out.shape[1] // count
    gain = ffn_gain.astype(jnp.float32).reshape(count, share_width)
    orders = plans(count)
    sets = len(orders)
    set_rows = row_count // sets

    def core_sums(heads, side):
        sent, kept = project(heads, w_out, side)
        arrivals = [swap(block, 0, count) for block in sent]
        return [add(keep, arrival) for keep, arrival in zip(kept, arrivals)]

    far = core_sums(head_blocks, 1)
    first = timetable(count)[0]
    gate, far[first] = lax.optimization_barrier((head_blocks, far[first]))
    near = core_sums(gate, 0)
    held, leaving = [], []
    for k in range(sets):
        if orders[k][0][0] == 1:
            held.append(near[k])
            leaving.append(far[k])
        else:
            half = far[k].shape[0] // 2
            held.append(jnp.concatenate([near[k][:half], far[k][:half]], axis=0))
            leaving.append(jnp.concatenate([near[k][half:], far[k][half:]], axis=0))
    offsets = [[0] for _ in range(sets)]
    steps = [0] * sets
    last, results = None, ()
    arrivals = [None] * sets
    for k in timetable(count):
        scatter, gather = orders[k]
        step = steps[k]
        steps[k] += 1
        if step == 0:
            if last is None:
                last = leaving[k]
            else:
                last, _ = lax.optimization_barrier((leaving[k], last))
            arrivals[k] = swap(last, scatter[0], count)
            continue
        held[k], arrivals[k], _ = lax.optimization_barrier((held[k], arrivals[k], last))
        if step < len(scatter):
            held[k], last = halves(held[k], arrivals[k])
            arrivals[k] = swap(last, scatter[step], count)
            continue
        if step == len(scatter):
            own_rows = mine[k * set_rows : (k + 1) * set_rows].astype(jnp.float32)
            total = held[k][0].astype(jnp.float32) + arrivals[k][0].astype(jnp.float32)
            last = held[k] = (own_rows + total).astype(jnp.bfloat16)[None]
        elif step <= len(scatter) + len(gather):
            last = held[k] = jnp.concatenate([held[k], arrivals[k]], axis=0)
        else:
            pair = [k - 1, k]
            parts = [block for m in pair for block in (held[m], arrivals[m])]
            lists = [offsets[m] for m in pair]
            results = finish(parts, gain, lists, k // 2, sets // 2, results)
            last = results[0]
            continue
        bit = (gather + [0])[step - len(scatter)]
        arrivals[k] = swap(held[k], bit, count)
        offsets[k] = offsets[k] + [offset ^ (1 << bit) for offset in offsets[k]]
    normed, stream = results
    return (stream, normed)


def solution(mesh):
    placed = (
        P("groups", None),
        P(),
        P(None, "tensor"),
        P(None, "tensor"),
        P(("groups", "tensor"), None, None),
        P(("groups", "tensor"), None, None),
        P("tensor", None),
        P(),
        P(("groups", "tensor")),
        P("groups"),
    )
    return jax.shard_map(
        on_device,
        mesh=mesh,
        in_specs=placed,
        out_specs=(P("groups", "tensor"), P("groups", None)),
        check_vma=False,
    )
```

```python
import functools
import math

import jax
import jax.numpy as jnp
from jax import lax
from jax.experimental import pallas as pl
from jax.experimental.pallas import tpu as pltpu
from jax.sharding import PartitionSpec as P

HD = 128


TABLE = "032031032013023120123121302131"

epsilon = 1e-05
rope_theta = 500000.0


def turns(positions):
    half = HD // 2
    entry = jnp.arange(HD, dtype=jnp.int32)
    frequency = jnp.exp((entry % half).astype(jnp.float32) * (-math.log(rope_theta) / half))
    angles = positions.astype(jnp.float32)[:, None] * frequency[None, :]
    sign = jnp.where(entry < half, -1.0, 1.0)
    return jnp.cos(angles), jnp.sin(angles) * sign


def rotate(head, cosine, sine):
    return head * cosine + pltpu.roll(head, HD // 2, 1) * sine


def input_kernel(count, hidden_ref, gain_ref, w_ref, kv_ref, cosine_ref, sine_ref, *refs):
    out_ref, mine_ref, hidden, gain_buffer, w_buffer, kv_buffer, normed, products, kv_products, *sems = refs
    h_sem, w_sem, kv_sem, mine_sem, gain_sem = sems
    me = lax.axis_index("tensor")
    rows, columns = hidden.shape
    depth = normed.shape[2]
    chunks = columns // depth
    width = products.shape[1]
    kv_width = kv_products.shape[1]
    here = rows // count

    def span(k):
        return pl.ds(k * depth, depth)

    def hidden_copy(k):
        return pltpu.make_async_copy(
            hidden_ref.at[:, span(k)], hidden.at[:, span(k)], h_sem.at[k]
        )

    def w_copy(k):
        return pltpu.make_async_copy(w_ref.at[span(k), :], w_buffer.at[span(k), :], w_sem.at[k])

    for k in range(chunks):
        hidden_copy(k).start()
    gain_copy = pltpu.make_async_copy(gain_ref, gain_buffer, gain_sem)
    gain_copy.start()
    kv_copy = pltpu.make_async_copy(kv_ref, kv_buffer, kv_sem)
    own = pl.ds(pl.multiple_of(me * (columns // count), columns // count), columns // count)
    mine_copy = pltpu.make_async_copy(hidden_ref.at[:, own], mine_ref, mine_sem)
    products[...] = jnp.zeros_like(products)
    kv_products[...] = jnp.zeros_like(kv_products)
    total = jnp.zeros((rows, 128), jnp.float32)
    for k in range(chunks):
        hidden_copy(k).wait()
        w_copy(k).start()
        if k == 0:
            kv_copy.start()
        for lane in range(k * depth, (k + 1) * depth, 128):
            part = hidden[:, lane : lane + 128].astype(jnp.float32)
            total = total + part * part
    mine_copy.start()
    scale = lax.rsqrt(jnp.sum(total, axis=1, keepdims=True) / columns + epsilon)

    def norm(k):
        floats = hidden[:, span(k)].astype(jnp.float32)
        gain = gain_buffer[span(k)].astype(jnp.float32).reshape(1, depth)
        normed[k % 2] = (floats * scale * gain).astype(jnp.bfloat16)

    gain_copy.wait()
    norm(0)
    kv_copy.wait()
    for k in range(chunks):
        w_copy(k).wait()
        products[...] += jnp.dot(
            normed[k % 2], w_buffer[span(k), :], preferred_element_type=jnp.float32
        )
        kv_products[...] += lax.dot_general(
            normed[k % 2],
            kv_buffer[:, span(k)],
            (((1,), (1,)), ((), ())),
            preferred_element_type=jnp.float32,
        )
        if k + 1 < chunks:
            norm(k + 1)

    shift = lax.rem(me, HD // kv_width) * kv_width
    blank = jnp.zeros((rows, HD - kv_width), jnp.float32)
    moved = pltpu.roll(jnp.concatenate([kv_products[...], blank], axis=1), shift, 1)
    results = [
        rotate(products[:, start : start + HD], cosine_ref[...], sine_ref[...])
        for start in range(0, width, HD)
    ] + [moved]
    for part, result in enumerate(results):
        for k in range(count):
            out_ref[k, :, part * HD : (part + 1) * HD] = result[
                k * here : (k + 1) * here
            ].astype(jnp.bfloat16)
    mine_copy.wait()


def project_in(hidden_in, gain, w_query, w_keyval, cosine, sine, count):
    rows, columns = hidden_in.shape
    width, kv_width = w_query.shape[1], w_keyval.shape[1]
    depth = columns // 8
    chunks = columns // depth
    vmem = pl.BlockSpec(memory_space=pltpu.VMEM)
    whole = pl.BlockSpec(memory_space=pl.ANY)
    return pl.pallas_call(
        functools.partial(input_kernel, count),
        out_shape=(
            jax.ShapeDtypeStruct((count, rows // count, width + HD), jnp.bfloat16),
            jax.ShapeDtypeStruct((rows, columns // count), jnp.bfloat16),
        ),
        in_specs=[whole, whole, whole, whole, vmem, vmem],
        out_specs=(vmem, vmem),
        scratch_shapes=[
            pltpu.VMEM((rows, columns), jnp.bfloat16),
            pltpu.VMEM((columns,), jnp.bfloat16),
            pltpu.VMEM((columns, width), jnp.bfloat16),
            pltpu.VMEM((kv_width, columns), jnp.bfloat16),
            pltpu.VMEM((2, rows, depth), jnp.bfloat16),
            pltpu.VMEM((rows, width), jnp.float32),
            pltpu.VMEM((rows, kv_width), jnp.float32),
            pltpu.SemaphoreType.DMA((chunks,)),
            pltpu.SemaphoreType.DMA((chunks,)),
            pltpu.SemaphoreType.DMA,
            pltpu.SemaphoreType.DMA,
            pltpu.SemaphoreType.DMA,
        ],
        compiler_params=pltpu.CompilerParams(vmem_limit_bytes=52 * 1024 * 1024),
        cost_estimate=pl.CostEstimate(
            flops=2 * rows * columns * (width + kv_width),
            bytes_accessed=2 * columns * (rows + width + kv_width),
            transcendentals=0,
        ),
    )(hidden_in, gain, w_query, w_keyval.T, cosine, sine)


def attend_kernel(count, lengths_ref, cosine_ref, sine_ref, keys_ref, values_ref, *refs):
    in_ref, out_ref, queries, attended, scores, weights, keys, values, k_sem, v_sem = refs
    me = lax.axis_index("tensor")
    here, span, key_width = keys.shape
    kv_groups = key_width // HD
    parts = attended.shape[0]

    def key_copy(row):
        return pltpu.make_async_copy(keys_ref.at[row], keys.at[row], k_sem.at[row])

    def value_copy(row):
        return pltpu.make_async_copy(values_ref.at[row], values.at[row], v_sem.at[row])

    for row in range(here + 2):
        if row < here:
            key_copy(row).start()
        if row >= 2:
            value_copy(row - 2).start()

    for device in range(count):
        for part in range(parts + 1):
            queries[part, device * here : (device + 1) * here, :] = in_ref[
                device, :, part * HD : (part + 1) * HD
            ].astype(jnp.float32)
    mine = pl.ds(pl.multiple_of(me * here, here), here)
    cosine, sine = cosine_ref[mine, :], sine_ref[mine, :]
    shares = count // (2 * kv_groups)
    tiles = []
    for tile in range(2 * kv_groups):
        joined = jnp.zeros((here, HD), jnp.float32)
        for device in range(tile * shares, (tile + 1) * shares):
            joined = joined + queries[parts, device * here : (device + 1) * here, :]
        tiles.append(joined)
    new_keys = [rotate(tile, cosine, sine) for tile in tiles[:kv_groups]]
    new_keys = jnp.concatenate(new_keys, axis=1).astype(jnp.bfloat16).astype(jnp.float32)
    new_values = jnp.concatenate(tiles[kv_groups:], axis=1)

    shape = (parts * count, key_width)
    group_devices = count // kv_groups
    device = lax.rem(lax.broadcasted_iota(jnp.int32, shape, 0), count)
    column = lax.broadcasted_iota(jnp.int32, shape, 1)
    own_group = lax.div(device, group_devices) == lax.div(column, HD)
    token = lax.broadcasted_iota(jnp.int32, (1, span), 1)
    score_scale = HD ** (-0.5)
    own_scores, own_weights = {}, {}

    def score(row):
        heads = jnp.concatenate(
            [queries[part, pl.ds(row, count, stride=here), :] for part in range(parts)], axis=0
        )
        heads = jnp.where(own_group, jnp.concatenate([heads] * kv_groups, axis=1), 0.0)
        own_scores[row] = (
            jnp.sum(heads * new_keys[row : row + 1], axis=1, keepdims=True) * score_scale
        )
        scores[row % 2] = lax.dot_general(
            heads.astype(jnp.bfloat16),
            keys[row],
            (((1,), (1,)), ((), ())),
            preferred_element_type=jnp.float32,
        )

    def weigh(row):
        valid = token < lengths_ref[row]
        scaled = jnp.where(valid, scores[row % 2] * score_scale, -1e30)
        largest = jnp.maximum(jnp.max(scaled, axis=1, keepdims=True), own_scores[row])
        raised = jnp.exp(scaled - largest)
        own_raised = jnp.exp(own_scores[row] - largest)
        share = 1.0 / (jnp.sum(raised, axis=1, keepdims=True) + own_raised)
        weights[row % 2] = (raised * share).astype(jnp.bfloat16)
        own_weights[row] = (own_raised * share).astype(jnp.bfloat16).astype(jnp.float32)

    def mix(row):
        mixed = jnp.dot(weights[row % 2], values[row], preferred_element_type=jnp.float32)
        mixed = mixed + own_weights[row] * new_values[row : row + 1]
        mixed = jnp.where(own_group, mixed, 0.0)
        chosen = mixed[:, :HD]
        for group in range(1, kv_groups):
            chosen = chosen + mixed[:, group * HD : (group + 1) * HD]
        for part in range(parts):
            attended[part, pl.ds(row, count, stride=here), :] = chosen[
                part * count : (part + 1) * count
            ]

    for step in range(here + 2):
        if step < here:
            key_copy(step).wait()
        if step >= 2:
            value_copy(step - 2).wait()
        if step >= 2:
            mix(step - 2)
        if 1 <= step <= here:
            weigh(step - 1)
        if step < here:
            score(step)
    for k in range(count):
        for part in range(parts):
            out_ref[k, :, part * HD : (part + 1) * HD] = attended[
                part, k * here : (k + 1) * here, :
            ].astype(jnp.bfloat16)


def attend(blocks, lengths, cosine, sine, cache_keys, cache_values):
    count = blocks.shape[0]
    here, span, key_width = cache_keys.shape
    width = blocks.shape[2] - HD
    heads = count * width // HD
    vmem = pl.BlockSpec(memory_space=pltpu.VMEM)
    whole = pl.BlockSpec(memory_space=pl.ANY)
    return pl.pallas_call(
        functools.partial(attend_kernel, count),
        out_shape=jax.ShapeDtypeStruct((count, here, width), jnp.bfloat16),
        in_specs=[pl.BlockSpec(memory_space=pltpu.SMEM), vmem, vmem, whole, whole, vmem],
        out_specs=vmem,
        scratch_shapes=[
            pltpu.VMEM((width // HD + 1, here * count, HD), jnp.float32),
            pltpu.VMEM((width // HD, here * count, HD), jnp.float32),
            pltpu.VMEM((2, heads, span), jnp.float32),
            pltpu.VMEM((2, heads, span), jnp.bfloat16),
            pltpu.VMEM((here, span, key_width), jnp.bfloat16),
            pltpu.VMEM((here, span, key_width), jnp.bfloat16),
            pltpu.SemaphoreType.DMA((here,)),
            pltpu.SemaphoreType.DMA((here,)),
        ],
        compiler_params=pltpu.CompilerParams(vmem_limit_bytes=40 * 1024 * 1024),
        cost_estimate=pl.CostEstimate(
            flops=4 * here * count * width * span,
            bytes_accessed=4 * here * span * key_width,
            transcendentals=here * heads * span,
        ),
    )(lengths, cosine, sine, cache_keys, cache_values, blocks)


def exchange(blocks):
    return lax.all_to_all(blocks, "tensor", split_axis=0, concat_axis=0, tiled=True)


def plans(count):
    bits = list(range(1, count.bit_length() - 1))
    turned = bits[::-1]
    late = bits[1:2] + bits[:1] + bits[2:]
    crossed = late[::-1]
    return [(bits, turned), (bits, crossed), (late, turned), (bits, crossed)]


def timetable(count):
    if count == 16:
        return [int(c) for c in TABLE]
    steps = 2 * (count.bit_length() - 2) + 1
    return [s for _ in range(steps) for s in (1, 0, 2, 3)] + [1, 3]


def place(offset, order):
    spot = 0
    for bit in order:
        spot = spot * 2 + ((offset >> bit) & 1)
    return spot


def project_kernel(count, side, in_ref, w_ref, *refs):
    *set_refs, heads_buffer, w_buffer, arrived = refs
    me = lax.axis_index("tensor")
    width = w_buffer.shape[2]
    offsets = [k for k in range(count) if (k >> 1) % 2 == side]
    offsets = [k for k in offsets if k % 2] + [k for k in offsets if k % 2 == 0]
    copies = []
    for slot, offset in enumerate(offsets):
        column = pl.multiple_of(jnp.bitwise_xor(me, offset) * width, width)
        copies.append(
            pltpu.make_async_copy(
                w_ref.at[:, pl.ds(column, width)], w_buffer.at[slot], arrived.at[slot]
            )
        )
        copies[-1].start()
    here = in_ref.shape[1]
    for k in range(count):
        heads_buffer[k * here : (k + 1) * here, :] = in_ref[k].astype(jnp.float32)
    heads = heads_buffer[...].astype(jnp.bfloat16)
    for slot, offset in enumerate(offsets):
        copies[slot].wait()
        product = jnp.dot(heads, w_buffer[slot], preferred_element_type=jnp.float32).astype(
            jnp.bfloat16
        )
        start = 0
        for which, (order, _) in enumerate(plans(count)):
            ref = set_refs[2 * which + (1 - offset % 2)]
            spot = place(offset, [bit for bit in order if bit != 1])
            ref[spot] = product[start : start + ref.shape[1]]
            start += ref.shape[1]


def project(blocks, w_out, side):
    count, here, depth = blocks.shape
    rows = count * here
    width = w_out.shape[1] // count
    sets = len(plans(count))
    share = jax.ShapeDtypeStruct((count // 4, rows // sets, width), jnp.bfloat16)
    outs = pl.pallas_call(
        functools.partial(project_kernel, count, side),
        out_shape=(share,) * (2 * sets),
        in_specs=[pl.BlockSpec(memory_space=pltpu.VMEM), pl.BlockSpec(memory_space=pl.ANY)],
        out_specs=(pl.BlockSpec(memory_space=pltpu.VMEM),) * (2 * sets),
        scratch_shapes=[
            pltpu.VMEM((rows, depth), jnp.float32),
            pltpu.VMEM((count // 2, depth, width), jnp.bfloat16),
            pltpu.SemaphoreType.DMA((count // 2,)),
        ],
        compiler_params=pltpu.CompilerParams(vmem_limit_bytes=48 * 1024 * 1024),
        cost_estimate=pl.CostEstimate(
            flops=rows * depth * width * count,
            bytes_accessed=(depth + rows) * width * count,
            transcendentals=0,
        ),
    )(blocks, w_out)
    return outs[0::2], outs[1::2]


def finish_kernel(offsets, gain_ref, *refs):
    out_ref, own_ref = refs[-2:]
    me = lax.axis_index("tensor")
    half, rows, width = refs[0].shape

    def norm(k, order):
        parts = refs[2 * k : 2 * k + 2]
        own_ref[...] = parts[0][0]
        total = jnp.zeros((rows, width), jnp.float32)
        for ref in parts:
            for spot in range(half):
                block = ref[spot].astype(jnp.float32)
                total = total + block * block
        mean_square = jnp.sum(total, axis=1, keepdims=True) / (2 * half * width)
        scale = lax.rsqrt(mean_square + epsilon)
        for spot, offset in enumerate(order):
            block = parts[spot // half][spot % half].astype(jnp.float32)
            index = jnp.bitwise_xor(me, offset)
            column = pl.multiple_of(index * width, width)
            gain = gain_ref[pl.ds(index, 1), :]
            out_ref[:, pl.ds(column, width)] = (block * scale * gain).astype(jnp.bfloat16)

    for k, order in enumerate(offsets):
        pl.when(pl.program_id(0) == k)(functools.partial(norm, k, order))


def finish(parts, gain, offsets, which, groups, earlier):
    half, rows, width = parts[0].shape
    columns, count = 2 * half * width, len(offsets)
    parts = [pltpu.with_memory_space_constraint(part, pltpu.VMEM) for part in parts]
    operands = [gain, *parts, *earlier]
    specs = [pl.BlockSpec(memory_space=pltpu.VMEM)] * (1 + len(parts))
    specs += [pl.BlockSpec(memory_space=pl.ANY)] * len(earlier)
    return pl.pallas_call(
        functools.partial(finish_kernel, offsets),
        grid=(count,),
        out_shape=tuple(
            jax.ShapeDtypeStruct((rows * count * groups, size), jnp.bfloat16)
            for size in (columns, width)
        ),
        in_specs=specs,
        out_specs=tuple(
            pl.BlockSpec((rows, size), lambda i: (which * count + i, 0))
            for size in (columns, width)
        ),
        input_output_aliases={1 + len(parts) + k: k for k in range(len(earlier))},
        compiler_params=pltpu.CompilerParams(vmem_limit_bytes=12 * 1024 * 1024),
        cost_estimate=pl.CostEstimate(
            flops=6 * count * rows * columns,
            bytes_accessed=4 * count * rows * columns,
            transcendentals=0,
        ),
    )(*operands)


def swap(values, bit, count):
    return lax.ppermute(values, "tensor", [(i, i ^ (1 << bit)) for i in range(count)])


def add(one, other):
    return (one.astype(jnp.float32) + other.astype(jnp.float32)).astype(jnp.bfloat16)


def halves(keep, arrival):
    half = keep.shape[0] // 2
    return add(keep[:half], arrival[:half]), add(keep[half:], arrival[half:])


def on_device(
    hidden_in,
    attn_gain,
    w_query,
    w_keyval,
    cache_keys,
    cache_values,
    w_out,
    ffn_gain,
    lengths,
    positions,
):
    row_count = hidden_in.shape[0]
    count = lax.axis_size("tensor")
    cosine, sine = turns(positions)
    blocks, mine = project_in(hidden_in, attn_gain, w_query, w_keyval, cosine, sine, count)
    head_blocks = exchange(
        attend(exchange(blocks), lengths, cosine, sine, cache_keys, cache_values)
    )
    share_width = w_out.shape[1] // count
    gain = ffn_gain.astype(jnp.float32).reshape(count, share_width)
    orders = plans(count)
    sets = len(orders)
    set_rows = row_count // sets

    def core_sums(heads, side):
        sent, kept = project(heads, w_out, side)
        arrivals = [swap(block, 0, count) for block in sent]
        return [add(keep, arrival) for keep, arrival in zip(kept, arrivals)]

    far = core_sums(head_blocks, 1)
    first = timetable(count)[0]
    gate, far[first] = lax.optimization_barrier((head_blocks, far[first]))
    near = core_sums(gate, 0)
    held, leaving = [], []
    for k in range(sets):
        if orders[k][0][0] == 1:
            held.append(near[k])
            leaving.append(far[k])
        else:
            half = far[k].shape[0] // 2
            held.append(jnp.concatenate([near[k][:half], far[k][:half]], axis=0))
            leaving.append(jnp.concatenate([near[k][half:], far[k][half:]], axis=0))
    offsets = [[0] for _ in range(sets)]
    steps = [0] * sets
    last, results = None, ()
    arrivals = [None] * sets
    for k in timetable(count):
        scatter, gather = orders[k]
        step = steps[k]
        steps[k] += 1
        if step == 0:
            if last is None:
                last = leaving[k]
            else:
                last, _ = lax.optimization_barrier((leaving[k], last))
            arrivals[k] = swap(last, scatter[0], count)
            continue
        held[k], arrivals[k], _ = lax.optimization_barrier((held[k], arrivals[k], last))
        if step < len(scatter):
            held[k], last = halves(held[k], arrivals[k])
            arrivals[k] = swap(last, scatter[step], count)
            continue
        if step == len(scatter):
            own_rows = mine[k * set_rows : (k + 1) * set_rows].astype(jnp.float32)
            total = held[k][0].astype(jnp.float32) + arrivals[k][0].astype(jnp.float32)
            last = held[k] = (own_rows + total).astype(jnp.bfloat16)[None]
        elif step <= len(scatter) + len(gather):
            last = held[k] = jnp.concatenate([held[k], arrivals[k]], axis=0)
        else:
            pair = [k - 1, k]
            parts = [block for m in pair for block in (held[m], arrivals[m])]
            lists = [offsets[m] for m in pair]
            results = finish(parts, gain, lists, k // 2, sets // 2, results)
            last = results[0]
            continue
        bit = (gather + [0])[step - len(scatter)]
        arrivals[k] = swap(held[k], bit, count)
        offsets[k] = offsets[k] + [offset ^ (1 << bit) for offset in offsets[k]]
    normed, stream = results
    return (stream, normed)


def solution(mesh):
    placed = (
        P("groups", None),
        P(),
        P(None, "tensor"),
        P(None, "tensor"),
        P(("groups", "tensor"), None, None),
        P(("groups", "tensor"), None, None),
        P("tensor", None),
        P(),
        P(("groups", "tensor")),
        P("groups"),
    )
    return jax.shard_map(
        on_device,
        mesh=mesh,
        in_specs=placed,
        out_specs=(P("groups", "tensor"), P("groups", None)),
        check_vma=False,
    )
```
